512 devices in a mesh: lon: 32 (over x, z_lo), lat: 16 (over z_hi, y, core).
Axes of the slice: x: 4, y: 4, z: 16 (z_hi: 2, z_lo: 8; z = z_hi * 8 + z_lo), core: 2. Of those that a mesh axis runs over, the one named last changes fastest.
Arguments:
- ensemble_state: bfloat16 [512, 2048, 256], P('lat', 'lon'), may hold values from -6 to 6
- courant: float32 [2, 512, 2048], P(None, 'lat', 'lon'), may hold values from -0.45 to 0.45
- obs_where: int32 [2, 3, 128], replicated, may hold values from 0 to 2047, as said below
- obs_value: float32 [2, 128], replicated, may hold values from -6 to 6
- obs_variance: float32 [2, 128], replicated, may hold values from 0.25 to 2
- obs_noise: float32 [2, 128, 256], replicated, may hold values from -5 to 5
Outputs:
- analysis: bfloat16 [512, 2048, 256], P('lat', 'lon')
The draws below stay inside these ranges and needn't reach their ends.
Inputs may be any that keep to these rules, and one draw needn't show every extreme that they name: `obs_where`: row 0 holds latitude rows, row 1 longitude columns, row 2 radii of 24 to 96 cells; observations cluster around a few centres per batch, the rest spread over the grid.
All inputs are finite; a program needn't handle non-finite values.
Results may differ from the reference program's by a relative error of at most 0.001.
Values sent between devices are 32-bit elements; how exact they have to be, the bound alone decides.
A program may use at most 64 MiB of HBM per device.

```python
import math
import jax
import jax.numpy as jnp
from jax import lax

M = 256
NOBS = 128
BATCHES = 2
ADV_STEPS = 2
NLAT = 512
NLON = 2048
RADIUS_MAX = 96
RADIUS_MIN = 24


def draw_obs_where(key, part):
    key = jax.random.fold_in(key, 7)
    keys = jax.random.split(key, 9)
    center_lat = jax.random.randint(keys[0], (BATCHES, 4), 0, NLAT)
    center_lon = jax.random.randint(keys[1], (BATCHES, 4), 0, NLON)
    chosen = jax.random.randint(keys[2], (BATCHES, NOBS), 0, 4)
    near_lat = jnp.take_along_axis(center_lat, chosen, axis=1) + jax.random.randint(keys[3], (BATCHES, NOBS), -RADIUS_MAX, RADIUS_MAX + 1)
    near_lon = jnp.take_along_axis(center_lon, chosen, axis=1) + jax.random.randint(keys[4], (BATCHES, NOBS), -RADIUS_MAX, RADIUS_MAX + 1)
    near_lat = jnp.clip(near_lat, 0, NLAT - 1)
    near_lon = jnp.mod(near_lon, NLON)
    spread = jax.random.randint(keys[5], (BATCHES, NOBS), 0, 2)
    far_lat = jax.random.randint(keys[6], (BATCHES, NOBS), 0, NLAT)
    far_lon = jax.random.randint(keys[7], (BATCHES, NOBS), 0, NLON)
    row_lat = jnp.where(spread == 1, far_lat, near_lat)
    row_lon = jnp.where(spread == 1, far_lon, near_lon)
    row_lat = row_lat.at[:, 1].set(NLAT - 1).at[:, 2].set(0)
    row_lon = row_lon.at[:, 1].set(NLON - 1).at[:, 2].set(0)
    radius = jax.random.randint(keys[8], (BATCHES, NOBS), RADIUS_MIN, RADIUS_MAX + 1)
    radius = radius.at[:, 0].set(RADIUS_MAX)
    return jnp.stack([row_lat, row_lon, radius], axis=1).astype(jnp.int32)


def block_levels(key, shape, cuts, least, largest):
    loudness = 1.0
    for dim, parts in cuts:
        heights = jax.random.uniform(jax.random.fold_in(jax.random.fold_in(key, 6), dim), (parts,), jnp.float32, least / len(cuts), largest / len(cuts))
        loudness = loudness * jnp.repeat(jnp.exp(heights), shape[dim] // parts).reshape((-1,) + (1,) * (len(shape) - 1 - dim))
    return loudness


def bell_draw(key, shape, scale, bound, cuts=(), held_as=jnp.bfloat16):
    gain = block_levels(key, shape, cuts, -0.22, 0.18) if cuts else 1.0
    result = jax.random.normal(key, shape, jnp.float32) * scale * gain
    return jnp.minimum(jnp.maximum(result, -bound), bound).astype(held_as)


def setup_inputs(seed: int = 0) -> dict:
    key_list = jax.random.split(jax.random.key(seed), 7)
    return {
        "ensemble_state": bell_draw(key_list[0], (NLAT, NLON, M), 1.0, 6.0, ((0, 16), (1, 32))),
        "courant": jnp.clip(jax.random.uniform(key_list[1], (2, NLAT, NLON), jnp.float32, -0.45, 0.45) * block_levels(key_list[1], (2, NLAT, NLON), ((1, 16), (2, 32)), -0.4, 0.0), -0.45, 0.45),
        "obs_where": draw_obs_where(jax.random.fold_in(key_list[6], 71), 0),
        "obs_value": bell_draw(key_list[3], (BATCHES, NOBS), 1.5, 6.0, (), jnp.float32),
        "obs_variance": jnp.clip(jnp.exp(jax.random.uniform(key_list[4], (BATCHES, NOBS), jnp.float32, math.log(0.25), math.log(2.0))), 0.25, 2.0),
        "obs_noise": bell_draw(key_list[5], (BATCHES, NOBS, M), 1.0, 5.0, (), jnp.float32),
    }


def matmul_exact(left, right):
    return jnp.dot(left.astype(jnp.float32), right.astype(jnp.float32), precision=lax.Precision.HIGHEST, preferred_element_type=jnp.float32)

def combine_upwind(grid_field, below_rows, above_rows, west_side, east_side, speed_lat, speed_lon):
    lat_plus = jnp.maximum(speed_lat, 0.0)[..., None]
    lat_minus = jnp.minimum(speed_lat, 0.0)[..., None]
    lon_plus = jnp.maximum(speed_lon, 0.0)[..., None]
    lon_minus = jnp.minimum(speed_lon, 0.0)[..., None]
    return grid_field - lat_plus * (grid_field - below_rows) - lat_minus * (above_rows - grid_field) - lon_plus * (grid_field - west_side) - lon_minus * (east_side - grid_field)

def upwind_step(grid_field, courant):
    zero_row = jnp.zeros_like(grid_field[:1])
    below_rows = jnp.concatenate([zero_row, grid_field[:-1]], axis=0)
    above_rows = jnp.concatenate([grid_field[1:], zero_row], axis=0)
    west_side = jnp.roll(grid_field, 1, axis=1)
    east_side = jnp.roll(grid_field, -1, axis=1)
    return combine_upwind(grid_field, below_rows, above_rows, west_side, east_side, courant[0], courant[1])

def taper_weights(cell_lat, cell_lon, obs_lat, obs_lon, radius, width):
    lat_gap = cell_lat - obs_lat
    lon_gap = jnp.abs(cell_lon - obs_lon)
    lon_gap = jnp.minimum(lon_gap, width - lon_gap)
    distance_sq = (lat_gap * lat_gap + lon_gap * lon_gap).astype(jnp.float32)
    radius_sq = (radius * radius).astype(jnp.float32)
    return jnp.square(jnp.maximum(1.0 - distance_sq / radius_sq, 0.0))

def batch_weights(priors, values, variance, noise):
    members = priors.shape[1]
    anomaly = priors - lax.optimization_barrier(jnp.mean(priors, axis=1, keepdims=True))
    system = matmul_exact(anomaly, anomaly.T) / (members - 1) + jnp.diag(variance)
    misfit = values[:, None] + jnp.sqrt(variance)[:, None] * noise - priors
    factor = jnp.linalg.cholesky(system)
    halfway = lax.linalg.triangular_solve(factor, misfit, left_side=True, lower=True)
    weights = lax.linalg.triangular_solve(factor, halfway, left_side=True, lower=True, transpose_a=True)
    return (anomaly, weights)

def reference(ensemble_state, courant, obs_where, obs_value, obs_variance, obs_noise):
    grid_field = ensemble_state.astype(jnp.float32)
    for step_index in range(ADV_STEPS):
        grid_field = upwind_step(grid_field, courant)
    rows_all, cols_all, members = grid_field.shape
    for batch_index in range(BATCHES):
        obs_lat = obs_where[batch_index, 0]
        obs_lon = obs_where[batch_index, 1]
        radius = obs_where[batch_index, 2]
        priors = grid_field[obs_lat, obs_lon]
        anomaly_obs, weights = batch_weights(priors, obs_value[batch_index], obs_variance[batch_index], obs_noise[batch_index])
        blocks = grid_field.reshape(rows_all // 8, 8, cols_all, members)
        starts = jnp.arange(rows_all // 8, dtype=jnp.int32) * 8

        def update_block(block_pair):
            row_block, row_first = block_pair
            ensemble = row_block.reshape(8 * cols_all, members)
            cell_index = jnp.arange(8 * cols_all, dtype=jnp.int32)
            cell_lat = (row_first + cell_index // cols_all)[:, None]
            cell_lon = (cell_index % cols_all)[:, None]
            weight_map = taper_weights(cell_lat, cell_lon, obs_lat[None, :], obs_lon[None, :], radius[None, :], cols_all)
            anomaly = ensemble - lax.optimization_barrier(jnp.mean(ensemble, axis=1, keepdims=True))
            covariance = matmul_exact(anomaly, anomaly_obs.T) / (members - 1)
            ensemble = ensemble + matmul_exact(weight_map * covariance, weights)
            return ensemble.reshape(8, cols_all, members)
        grid_field = lax.map(update_block, (blocks, starts)).reshape(rows_all, cols_all, members)
    return grid_field.astype(jnp.bfloat16)
```

```python
import functools
import jax
import jax.numpy as jnp
from jax import lax
from jax.experimental import pallas as pl
from jax.experimental.pallas import tpu as pltpu
from jax.sharding import PartitionSpec as P

BATCHES = 2
MESH = pl.DeviceIdType.MESH
PAD = 8
LANES = 128
HIGHEST = lax.Precision.HIGHEST
ONE_STEP = ((0, 0), (-1, 0), (1, 0), (0, -1), (0, 1))
TWO_STEPS = tuple(sorted({(a + c, b + d) for a, b in ONE_STEP for c, d in ONE_STEP}))


def split_mesh(lon_count, lat_count):
    plane_lat = 8 if lat_count == 16 else lat_count // 2
    line_lon = 8 if lon_count == 32 else lon_count // 2
    return lon_count // line_lon, line_lon, lat_count // plane_lat, plane_lat


def shifted(field, rows, lanes):
    if rows:
        field = pltpu.roll(field, rows % field.shape[0], 0)
    if lanes:
        field = pltpu.roll(field, lanes % field.shape[1], 1)
    return field


def link_weights(speed_lat, speed_lon, row, total_rows):
    inside = (row >= 0) & (row < total_rows)
    lat_plus = jnp.maximum(speed_lat, 0.0)
    lat_minus = jnp.minimum(speed_lat, 0.0)
    lon_plus = jnp.maximum(speed_lon, 0.0)
    lon_minus = jnp.minimum(speed_lon, 0.0)
    zero = jnp.zeros_like(speed_lat)
    return {
        (0, 0): jnp.where(inside, 1.0 - lat_plus + lat_minus - lon_plus + lon_minus, zero),
        (-1, 0): jnp.where(inside & (row > 0), lat_plus, zero),
        (1, 0): jnp.where(inside & (row < total_rows - 1), -lat_minus, zero),
        (0, -1): jnp.where(inside, lon_plus, zero),
        (0, 1): jnp.where(inside, -lon_minus, zero),
    }


def gather_kernel(
    sizes, state_ref, courant_ref, where_ref,
    priors_ref, field_ref,
    near_ns, near_ew, near_corner, reach, wide, stencil, links, weights, part, pieces, piece, line, got,
    grid, edge_send, edge_got,
    near_sem, reach_sem, part_sem, line_sem, all_sem, send_sem, out_sem,
):
    lon_count, lat_count = sizes
    plane_lon, line_lon, line_lat, plane_lat = split_mesh(lon_count, lat_count)
    plane, lines = plane_lon * plane_lat, line_lat * line_lon
    rows, cols, members = state_ref.shape
    total_rows, total_cols = rows * lat_count, cols * lon_count
    nobs = where_ref.shape[2]
    lon, lat = lax.axis_index("lon"), lax.axis_index("lat")
    plane_me = (lon // line_lon) * plane_lat + lat % plane_lat
    line_me = (lat // plane_lat) * line_lon + lon % line_lon

    def plane_device(index):
        return {
            "lon": (index // plane_lat) * line_lon + lon % line_lon,
            "lat": (lat // plane_lat) * plane_lat + index % plane_lat,
        }

    def line_device(index):
        return {
            "lon": (lon // line_lon) * line_lon + index % line_lon,
            "lat": (index // line_lon) * plane_lat + lat % plane_lat,
        }

    def neighbour(lat_step, lon_step):
        return {
            "lon": lax.rem(lon + lon_step + lon_count, lon_count),
            "lat": lax.rem(lat + lat_step + lat_count, lat_count),
        }

    around = [(a, b) for a in (-1, 0, 1) for b in (-1, 0, 1) if a or b]

    barrier = pltpu.get_barrier_semaphore()
    for step in around:
        pl.semaphore_signal(barrier, inc=1, device_id=neighbour(*step), device_id_type=MESH)

    def greet_line(d, carry):
        target = line_device(lax.rem(line_me + d, lines))
        pl.semaphore_signal(barrier, inc=1, device_id=target, device_id_type=MESH)
        return carry

    def greet_plane(d, carry):
        target = plane_device(lax.rem(plane_me + d, plane))
        pl.semaphore_signal(barrier, inc=1, device_id=target, device_id_type=MESH)
        return carry

    lax.fori_loop(1, lines, greet_line, 0)
    lax.fori_loop(1, plane, greet_plane, 0)

    for r in range(rows):
        grid[r + 2, PAD : PAD + cols, :] = state_ref[r].astype(jnp.float32)
    for side, first in ((0, 0), (1, cols - 2)):
        for j in range(2):
            edge_send[side, j] = state_ref[:, first + j, :].astype(jnp.float32)
    pl.semaphore_wait(barrier, len(around) + plane - 1 + lines - 1)

    copies = []

    def send(src, dst, sem, step):
        copy = pltpu.make_async_remote_copy(
            src_ref=src, dst_ref=dst, send_sem=sem.at[0], recv_sem=sem.at[1],
            device_id=neighbour(*step), device_id_type=MESH,
        )
        copy.start()
        copies.append(copy)
        return copy

    low, high = pl.ds(0, 8), pl.ds(rows - 8, 8)
    near = []
    for index, (a, b) in enumerate(around):
        source = courant_ref.at[:, {-1: low, 1: high}[a], :] if a else courant_ref
        if a and b:
            target = near_corner.at[(0 if a > 0 else 2) + (0 if b > 0 else 1)]
        elif a:
            target = near_ns.at[0 if a > 0 else 1]
        else:
            target = near_ew.at[0 if b > 0 else 1]
        near.append(send(source, target, near_sem.at[index], (a, b)))

    far = []
    inner = pl.ds(PAD, cols)
    blocks = {
        (1, 0): (grid.at[pl.ds(rows, 2), inner], grid.at[pl.ds(0, 2), inner]),
        (-1, 0): (grid.at[pl.ds(2, 2), inner], grid.at[pl.ds(rows + 2, 2), inner]),
        (0, 1): (edge_send.at[1], edge_got.at[0]),
        (0, -1): (edge_send.at[0], edge_got.at[1]),
        (1, 1): (grid.at[rows + 1, pl.ds(cols, 8)], grid.at[1, pl.ds(0, 8)]),
        (1, -1): (grid.at[rows + 1, pl.ds(PAD, 8)], grid.at[1, pl.ds(PAD + cols, 8)]),
        (-1, 1): (grid.at[2, pl.ds(cols, 8)], grid.at[rows + 2, pl.ds(0, 8)]),
        (-1, -1): (grid.at[2, pl.ds(PAD, 8)], grid.at[rows + 2, pl.ds(PAD + cols, 8)]),
    }
    for index, step in enumerate(around):
        far.append(send(*blocks[step], reach_sem.at[index], step))
    for copy in near:
        copy.wait_recv()

    lane = lax.broadcasted_iota(jnp.int32, (8, LANES), 1)

    def assemble(own, west, east):
        blank = jnp.zeros((8, LANES - cols), jnp.float32)
        own = jnp.concatenate([own, blank], axis=1)
        west = jnp.concatenate([blank, west], axis=1)
        east = jnp.concatenate([blank, east], axis=1) if cols * 2 == LANES else None
        return jnp.where(lane < cols, own, jnp.where(lane < cols + 2, east, west))

    for c in range(2):
        reach[c, 0:8] = assemble(near_ns[0, c], near_corner[0, c], near_corner[1, c])
        for r in range(0, rows, 8):
            band = pl.ds(r, 8)
            reach[c, r + 8 : r + 16] = assemble(courant_ref[c, band], near_ew[0, c, band], near_ew[1, c, band])
        reach[c, rows + 8 : rows + 16] = assemble(near_ns[1, c], near_corner[2, c], near_corner[3, c])

    row = lax.broadcasted_iota(jnp.int32, (rows + 16, LANES), 0) - 8 + lat * rows
    weight = link_weights(reach[0], reach[1], row, total_rows)

    arrived = {step: shifted(weight[step], *step) for step in ONE_STEP}
    sums = {}
    for first in ONE_STEP:
        for second in ONE_STEP:
            total = (first[0] + second[0], first[1] + second[1])
            term = shifted(arrived[first] * weight[second], *second)
            sums[total] = sums[total] + term if total in sums else term
    half = lax.broadcasted_iota(jnp.int32, (rows // 2, LANES), 1) < cols
    for index, total in enumerate(TWO_STEPS):
        wide[index] = sums[total][8 : 8 + rows]
        even = wide[index, pl.ds(0, rows // 2, 2), :]
        odd = wide[index, pl.ds(1, rows // 2, 2), :]
        stencil[index] = jnp.where(half, even, pltpu.roll(odd, cols, 1))

    cells = rows * cols
    flat_lane = lax.broadcasted_iota(jnp.int32, (nobs, LANES), 1)
    second_row = jnp.where(flat_lane >= cols, 1, 0)
    column = flat_lane - second_row * cols
    flat_state = state_ref[...].reshape(cells, members)
    for batch in range(BATCHES):
        where = jnp.concatenate([where_ref[batch], jnp.zeros((8 - 3, nobs), jnp.int32)], axis=0)
        where = jnp.transpose(where.astype(jnp.float32)).astype(jnp.int32)
        obs_row = where[:, 0:1] - lat * rows
        obs_col = where[:, 1:2] - lon * cols + 2
        obs_col = jnp.where(obs_col < 0, obs_col + total_cols, obs_col) - 2
        obs_col = jnp.where(obs_col >= total_cols - 2, obs_col - total_cols, obs_col)
        lon_step = column - obs_col
        lat_base = second_row - obs_row

        def one_pair(pair, carry):
            lat_step = lat_base + 2 * pair
            total = jnp.zeros((nobs, LANES), jnp.float32)
            for a in range(-2, 3):
                for b in range(-2, 3):
                    if (a, b) in TWO_STEPS:
                        value = stencil[TWO_STEPS.index((a, b)), pl.ds(pair, 1), :]
                        total = jnp.where((lat_step == a) & (lon_step == b), value, total)
            upper = total.astype(jnp.bfloat16)
            columns = pl.ds(pl.multiple_of(pair * LANES, LANES), LANES)
            weights[0:nobs, columns] = upper
            weights[nobs : 2 * nobs, columns] = (total - upper.astype(jnp.float32)).astype(jnp.bfloat16)
            return carry

        lax.fori_loop(0, rows // 2, one_pair, 0)
        share = jnp.dot(weights[...], flat_state, preferred_element_type=jnp.float32)
        part[batch] = share[:nobs] + share[nobs:]

        def send_part(d, carry):
            index = lax.rem(plane_me + d, plane)
            copy = pltpu.make_async_remote_copy(
                src_ref=part.at[batch, *tile_of(index)], dst_ref=pieces.at[batch, d],
                send_sem=send_sem.at[batch, 0], recv_sem=part_sem.at[batch],
                device_id=plane_device(index), device_id_type=MESH,
            )
            copy.start()
            return carry

        def tile_of(index):
            halves = members // LANES
            band = nobs * halves // plane
            return (
                pl.ds(pl.multiple_of((index // halves) * band, band), band),
                pl.ds(pl.multiple_of((index % halves) * LANES, LANES), LANES),
            )

        lax.fori_loop(1, plane, send_part, 0)

    for batch in range(BATCHES):
        pltpu.make_async_copy(pieces.at[batch, 1:plane], pieces.at[batch, 1:plane], part_sem.at[batch]).wait()
        piece[batch] = part[batch, *tile_of(plane_me)] + jnp.sum(pieces[batch, 1:plane], axis=0)

        def send_line(d, carry):
            copy = pltpu.make_async_remote_copy(
                src_ref=piece.at[batch], dst_ref=line.at[batch, d],
                send_sem=send_sem.at[batch, 1], recv_sem=line_sem.at[batch],
                device_id=line_device(lax.rem(line_me + d, lines)), device_id_type=MESH,
            )
            copy.start()
            return carry

        lax.fori_loop(1, lines, send_line, 0)

    for copy in far:
        copy.wait_recv()
    for side, first in ((0, PAD - 2), (1, PAD + cols)):
        for j in range(2):
            grid[2 : 2 + rows, first + j, :] = edge_got[side, j]
    width = cols + 2 * PAD
    for index, step in enumerate(ONE_STEP):
        upright = jnp.concatenate([weight[step], jnp.zeros((LANES - rows - 16, LANES), jnp.float32)], axis=0)
        links[index] = jnp.transpose(pltpu.roll(upright, PAD, 1))[:width]

    def one_row(r, source, target):
        rolled = [
            jnp.broadcast_to(pltpu.roll(links[i], lax.rem(LANES - r - 6, LANES), 1)[:, 0:1], (width, LANES))
            for i in range(len(ONE_STEP))
        ]
        for first in range(0, members, LANES):
            lanes = pl.ds(first, LANES)
            here = source[r, :, lanes]
            target(
                r, lanes,
                rolled[0] * here
                + rolled[1] * source[r - 1, :, lanes]
                + rolled[2] * source[r + 1, :, lanes]
                + rolled[3] * pltpu.roll(here, 1, 0)
                + rolled[4] * pltpu.roll(here, width - 1, 0),
            )

    def first_row(r, carry):
        def store(r, lanes, value):
            halfway[r, :, lanes] = value

        one_row(r, grid, store)
        return carry

    halfway = got[1]
    lax.fori_loop(1, rows + 3, first_row, 0)

    def second_row_of(r, carry):
        def store(r, lanes, value):
            grid[r, :, lanes] = value

        one_row(r, halfway, store)
        return carry

    for copy in far:
        copy.wait_send()
    lax.fori_loop(2, rows + 2, second_row_of, 0)
    out = pltpu.make_async_copy(grid.at[pl.ds(2, rows), pl.ds(PAD, cols)], field_ref, out_sem)
    out.start()

    priors = got[0]
    for batch in range(BATCHES):
        pltpu.make_async_copy(line.at[batch, 1:lines], line.at[batch, 1:lines], line_sem.at[batch]).wait()
        mine = tile_of(plane_me)
        priors[batch, *mine] = piece[batch] + jnp.sum(line[batch, 1:lines], axis=0)

        def send_all(d, carry):
            copy = pltpu.make_async_remote_copy(
                src_ref=priors.at[batch, *mine], dst_ref=priors.at[batch, *mine],
                send_sem=send_sem.at[batch, 2], recv_sem=all_sem.at[batch],
                device_id=plane_device(lax.rem(plane_me + d, plane)), device_id_type=MESH,
            )
            copy.start()
            return carry

        lax.fori_loop(1, plane, send_all, 0)
    for batch in range(BATCHES):
        block = pieces.at[batch, 1:plane]
        pltpu.make_async_copy(block, block, all_sem.at[batch]).wait()
        priors_ref[batch] = priors[batch]

    for copy in near:
        copy.wait_send()
    for batch in range(BATCHES):
        block = pieces.at[batch, 1:plane]
        pltpu.make_async_copy(block, block, send_sem.at[batch, 0]).wait()
        block = line.at[batch, 1:lines]
        pltpu.make_async_copy(block, block, send_sem.at[batch, 1]).wait()
        block = pieces.at[batch, 1:plane]
        pltpu.make_async_copy(block, block, send_sem.at[batch, 2]).wait()
    out.wait()


def gather(state, courant, where, lon_count, lat_count):
    rows, cols, members = state.shape
    nobs = where.shape[2]
    plane_lon, line_lon, line_lat, plane_lat = split_mesh(lon_count, lat_count)
    plane, lines = plane_lon * plane_lat, line_lat * line_lon
    band = nobs * (members // LANES) // plane
    width = cols + 2 * PAD
    f32 = jnp.float32
    vmem = pl.BlockSpec(memory_space=pltpu.VMEM)
    dma = pltpu.SemaphoreType.DMA
    return pl.pallas_call(
        functools.partial(gather_kernel, (lon_count, lat_count)),
        out_shape=(
            jax.ShapeDtypeStruct((BATCHES, nobs, members), f32),
            jax.ShapeDtypeStruct((rows, cols, members), f32),
        ),
        in_specs=[vmem] * 3,
        out_specs=(vmem, pl.BlockSpec(memory_space=pl.ANY)),
        scratch_shapes=[
            pltpu.VMEM((2, 2, 8, cols), f32),
            pltpu.VMEM((2, 2, rows, cols), f32),
            pltpu.VMEM((4, 2, 8, cols), f32),
            pltpu.VMEM((2, rows + 16, LANES), f32),
            pltpu.VMEM((len(TWO_STEPS), rows, LANES), f32),
            pltpu.VMEM((len(TWO_STEPS), rows // 2, LANES), f32),
            pltpu.VMEM((len(ONE_STEP), width, LANES), f32),
            pltpu.VMEM((2 * nobs, rows * cols), jnp.bfloat16),
            pltpu.VMEM((BATCHES, nobs, members), f32),
            pltpu.VMEM((BATCHES, plane, band, LANES), f32),
            pltpu.VMEM((BATCHES, band, LANES), f32),
            pltpu.VMEM((BATCHES, lines, band, LANES), f32),
            [pltpu.VMEM((BATCHES, nobs, members), f32), pltpu.VMEM((rows + 4, width, members), f32)],
            pltpu.VMEM((rows + 4, width, members), f32),
            pltpu.VMEM((2, 2, rows, members), f32),
            pltpu.VMEM((2, 2, rows, members), f32),
            dma((8, 2)),
            dma((8, 2)),
            dma((BATCHES,)),
            dma((BATCHES,)),
            dma((BATCHES,)),
            dma((BATCHES, 3)),
            dma,
        ],
        compiler_params=pltpu.CompilerParams(
            collective_id=0, has_side_effects=True, vmem_limit_bytes=48 * 1024 * 1024
        ),
        name="advance_and_gather",
    )(state, courant, where)


def matmul_exact(left, right):
    return jnp.dot(left, right, precision=HIGHEST, preferred_element_type=jnp.float32)


def taper_weights(cell_lat, cell_lon, obs_lat, obs_lon, radius, width):
    lat_gap = cell_lat - obs_lat
    lon_gap = jnp.abs(cell_lon - obs_lon)
    lon_gap = jnp.minimum(lon_gap, width - lon_gap)
    distance_sq = (lat_gap * lat_gap + lon_gap * lon_gap).astype(jnp.float32)
    radius_sq = (radius * radius).astype(jnp.float32)
    return jnp.square(jnp.maximum(1.0 - distance_sq / radius_sq, 0.0))


def batch_weights(priors, values, variance, noise):
    members = priors.shape[1]
    anomaly = priors - jnp.mean(priors, axis=1, keepdims=True)
    system = matmul_exact(anomaly, anomaly.T) / (members - 1) + jnp.diag(variance)
    misfit = values[:, None] + jnp.sqrt(variance)[:, None] * noise - priors
    factor = jnp.linalg.cholesky(system)
    halfway = lax.linalg.triangular_solve(factor, misfit, left_side=True, lower=True)
    weights = lax.linalg.triangular_solve(
        factor, halfway, left_side=True, lower=True, transpose_a=True
    )
    return (anomaly, weights)


def body(ensemble_state, courant, obs_where, obs_value, obs_variance, obs_noise):
    rows_tile, cols_tile, members = ensemble_state.shape
    lat_count, lon_count = lax.axis_size("lat"), lax.axis_size("lon")
    total_cols = cols_tile * lon_count
    row_start = lax.axis_index("lat") * rows_tile
    col_start = lax.axis_index("lon") * cols_tile
    priors, field = gather(ensemble_state, courant, obs_where, lon_count, lat_count)
    ensemble = field.reshape(rows_tile * cols_tile, members)
    cell_index = jnp.arange(rows_tile * cols_tile, dtype=jnp.int32)
    cell_lat = (row_start + cell_index // cols_tile)[:, None]
    cell_lon = (col_start + cell_index % cols_tile)[:, None]

    def update(cells, lat, lon, batch, anomaly_obs, weights):
        taper = taper_weights(
            lat, lon,
            obs_where[batch, 0][None, :], obs_where[batch, 1][None, :], obs_where[batch, 2][None, :],
            total_cols,
        )
        anomaly = cells - jnp.mean(cells, axis=1, keepdims=True)
        covariance = matmul_exact(anomaly, anomaly_obs.T) / (members - 1)
        return cells + matmul_exact(taper * covariance, weights)

    for batch in range(BATCHES):
        anomaly_obs, weights = batch_weights(
            priors[batch], obs_value[batch], obs_variance[batch], obs_noise[batch]
        )
        ensemble = update(ensemble, cell_lat, cell_lon, batch, anomaly_obs, weights)
        if batch + 1 < BATCHES:
            later = update(
                priors[batch + 1],
                obs_where[batch + 1, 0][:, None], obs_where[batch + 1, 1][:, None],
                batch, anomaly_obs, weights,
            )
            priors = priors.at[batch + 1].set(later)
    return ensemble.reshape(rows_tile, cols_tile, members).astype(jnp.bfloat16)


def solution(mesh):
    placed = (P("lat", "lon", None), P(None, "lat", "lon"), P(), P(), P(), P())
    return jax.shard_map(
        body, mesh=mesh, in_specs=placed, out_specs=P("lat", "lon", None), check_vma=False
    )
```

```python
import functools
import jax
import jax.numpy as jnp
from jax import lax
from jax.experimental import pallas as pl
from jax.experimental.pallas import tpu as pltpu
from jax.sharding import PartitionSpec as P

BATCHES = 2
MESH = pl.DeviceIdType.MESH
PAD = 8
LANES = 128
HIGHEST = lax.Precision.HIGHEST
ONE_STEP = ((0, 0), (-1, 0), (1, 0), (0, -1), (0, 1))
TWO_STEPS = tuple(sorted({(a + c, b + d) for a, b in ONE_STEP for c, d in ONE_STEP}))


def split_mesh(lon_count, lat_count):
    plane_lat = 8 if lat_count == 16 else lat_count // 2
    line_lon = 8 if lon_count == 32 else lon_count // 2
    return lon_count // line_lon, line_lon, lat_count // plane_lat, plane_lat


def shifted(field, rows, lanes):
    if rows:
        field = pltpu.roll(field, rows % field.shape[0], 0)
    if lanes:
        field = pltpu.roll(field, lanes % field.shape[1], 1)
    return field


def link_weights(speed_lat, speed_lon, row, total_rows):
    inside = (row >= 0) & (row < total_rows)
    lat_plus = jnp.maximum(speed_lat, 0.0)
    lat_minus = jnp.minimum(speed_lat, 0.0)
    lon_plus = jnp.maximum(speed_lon, 0.0)
    lon_minus = jnp.minimum(speed_lon, 0.0)
    zero = jnp.zeros_like(speed_lat)
    return {
        (0, 0): jnp.where(inside, 1.0 - lat_plus + lat_minus - lon_plus + lon_minus, zero),
        (-1, 0): jnp.where(inside & (row > 0), lat_plus, zero),
        (1, 0): jnp.where(inside & (row < total_rows - 1), -lat_minus, zero),
        (0, -1): jnp.where(inside, lon_plus, zero),
        (0, 1): jnp.where(inside, -lon_minus, zero),
    }


def gather_kernel(
    sizes, state_ref, courant_ref, where_ref,
    priors_ref, field_ref,
    near_ns, near_ew, near_corner, reach, wide, stencil, links, weights, part, pieces, piece, line, got,
    grid, edge_send, edge_got,
    near_sem, reach_sem, part_sem, line_sem, all_sem, send_sem, out_sem,
):
    lon_count, lat_count = sizes
    plane_lon, line_lon, line_lat, plane_lat = split_mesh(lon_count, lat_count)
    plane, lines = plane_lon * plane_lat, line_lat * line_lon
    rows, cols, members = state_ref.shape
    total_rows, total_cols = rows * lat_count, cols * lon_count
    nobs = where_ref.shape[2]
    lon, lat = lax.axis_index("lon"), lax.axis_index("lat")
    plane_me = (lon // line_lon) * plane_lat + lat % plane_lat
    line_me = (lat // plane_lat) * line_lon + lon % line_lon

    def plane_device(index):
        return {
            "lon": (index // plane_lat) * line_lon + lon % line_lon,
            "lat": (lat // plane_lat) * plane_lat + index % plane_lat,
        }

    def line_device(index):
        return {
            "lon": (lon // line_lon) * line_lon + index % line_lon,
            "lat": (index // line_lon) * plane_lat + lat % plane_lat,
        }

    def neighbour(lat_step, lon_step):
        return {
            "lon": lax.rem(lon + lon_step + lon_count, lon_count),
            "lat": lax.rem(lat + lat_step + lat_count, lat_count),
        }

    around = [(a, b) for a in (-1, 0, 1) for b in (-1, 0, 1) if a or b]

    barrier = pltpu.get_barrier_semaphore()
    for step in around:
        pl.semaphore_signal(barrier, inc=1, device_id=neighbour(*step), device_id_type=MESH)

    def greet_line(d, carry):
        target = line_device(lax.rem(line_me + d, lines))
        pl.semaphore_signal(barrier, inc=1, device_id=target, device_id_type=MESH)
        return carry

    def greet_plane(d, carry):
        target = plane_device(lax.rem(plane_me + d, plane))
        pl.semaphore_signal(barrier, inc=1, device_id=target, device_id_type=MESH)
        return carry

    lax.fori_loop(1, lines, greet_line, 0)
    lax.fori_loop(1, plane, greet_plane, 0)

    for r in range(rows):
        grid[r + 2, PAD : PAD + cols, :] = state_ref[r].astype(jnp.float32)
    for side, first in ((0, 0), (1, cols - 2)):
        for j in range(2):
            edge_send[side, j] = state_ref[:, first + j, :].astype(jnp.float32)
    pl.semaphore_wait(barrier, len(around) + plane - 1 + lines - 1)

    copies = []

    def send(src, dst, sem, step):
        copy = pltpu.make_async_remote_copy(
            src_ref=src, dst_ref=dst, send_sem=sem.at[0], recv_sem=sem.at[1],
            device_id=neighbour(*step), device_id_type=MESH,
        )
        copy.start()
        copies.append(copy)
        return copy

    low, high = pl.ds(0, 8), pl.ds(rows - 8, 8)
    near = []
    for index, (a, b) in enumerate(around):
        source = courant_ref.at[:, {-1: low, 1: high}[a], :] if a else courant_ref
        if a and b:
            target = near_corner.at[(0 if a > 0 else 2) + (0 if b > 0 else 1)]
        elif a:
            target = near_ns.at[0 if a > 0 else 1]
        else:
            target = near_ew.at[0 if b > 0 else 1]
        near.append(send(source, target, near_sem.at[index], (a, b)))

    far = []
    inner = pl.ds(PAD, cols)
    blocks = {
        (1, 0): (grid.at[pl.ds(rows, 2), inner], grid.at[pl.ds(0, 2), inner]),
        (-1, 0): (grid.at[pl.ds(2, 2), inner], grid.at[pl.ds(rows + 2, 2), inner]),
        (0, 1): (edge_send.at[1], edge_got.at[0]),
        (0, -1): (edge_send.at[0], edge_got.at[1]),
        (1, 1): (grid.at[rows + 1, pl.ds(cols, 8)], grid.at[1, pl.ds(0, 8)]),
        (1, -1): (grid.at[rows + 1, pl.ds(PAD, 8)], grid.at[1, pl.ds(PAD + cols, 8)]),
        (-1, 1): (grid.at[2, pl.ds(cols, 8)], grid.at[rows + 2, pl.ds(0, 8)]),
        (-1, -1): (grid.at[2, pl.ds(PAD, 8)], grid.at[rows + 2, pl.ds(PAD + cols, 8)]),
    }
    for index, step in enumerate(around):
        far.append(send(*blocks[step], reach_sem.at[index], step))
    for copy in near:
        copy.wait_recv()

    lane = lax.broadcasted_iota(jnp.int32, (8, LANES), 1)

    def assemble(own, west, east):
        blank = jnp.zeros((8, LANES - cols), jnp.float32)
        own = jnp.concatenate([own, blank], axis=1)
        west = jnp.concatenate([blank, west], axis=1)
        east = jnp.concatenate([blank, east], axis=1) if cols * 2 == LANES else None
        return jnp.where(lane < cols, own, jnp.where(lane < cols + 2, east, west))

    for c in range(2):
        reach[c, 0:8] = assemble(near_ns[0, c], near_corner[0, c], near_corner[1, c])
        for r in range(0, rows, 8):
            band = pl.ds(r, 8)
            reach[c, r + 8 : r + 16] = assemble(courant_ref[c, band], near_ew[0, c, band], near_ew[1, c, band])
        reach[c, rows + 8 : rows + 16] = assemble(near_ns[1, c], near_corner[2, c], near_corner[3, c])

    row = lax.broadcasted_iota(jnp.int32, (rows + 16, LANES), 0) - 8 + lat * rows
    weight = link_weights(reach[0], reach[1], row, total_rows)

    arrived = {step: shifted(weight[step], *step) for step in ONE_STEP}
    sums = {}
    for first in ONE_STEP:
        for second in ONE_STEP:
            total = (first[0] + second[0], first[1] + second[1])
            term = shifted(arrived[first] * weight[second], *second)
            sums[total] = sums[total] + term if total in sums else term
    half = lax.broadcasted_iota(jnp.int32, (rows // 2, LANES), 1) < cols
    for index, total in enumerate(TWO_STEPS):
        wide[index] = sums[total][8 : 8 + rows]
        even = wide[index, pl.ds(0, rows // 2, 2), :]
        odd = wide[index, pl.ds(1, rows // 2, 2), :]
        stencil[index] = jnp.where(half, even, pltpu.roll(odd, cols, 1))

    cells = rows * cols
    flat_lane = lax.broadcasted_iota(jnp.int32, (nobs, LANES), 1)
    second_row = jnp.where(flat_lane >= cols, 1, 0)
    column = flat_lane - second_row * cols
    flat_state = state_ref[...].reshape(cells, members)
    for batch in range(BATCHES):
        where = jnp.concatenate([where_ref[batch], jnp.zeros((8 - 3, nobs), jnp.int32)], axis=0)
        where = jnp.transpose(where.astype(jnp.float32)).astype(jnp.int32)
        obs_row = where[:, 0:1] - lat * rows
        obs_col = where[:, 1:2] - lon * cols + 2
        obs_col = jnp.where(obs_col < 0, obs_col + total_cols, obs_col) - 2
        obs_col = jnp.where(obs_col >= total_cols - 2, obs_col - total_cols, obs_col)
        lon_step = column - obs_col
        lat_base = second_row - obs_row

        def one_pair(pair, carry):
            lat_step = lat_base + 2 * pair
            total = jnp.zeros((nobs, LANES), jnp.float32)
            for a in range(-2, 3):
                for b in range(-2, 3):
                    if (a, b) in TWO_STEPS:
                        value = stencil[TWO_STEPS.index((a, b)), pl.ds(pair, 1), :]
                        total = jnp.where((lat_step == a) & (lon_step == b), value, total)
            upper = total.astype(jnp.bfloat16)
            columns = pl.ds(pl.multiple_of(pair * LANES, LANES), LANES)
            weights[0:nobs, columns] = upper
            weights[nobs : 2 * nobs, columns] = (total - upper.astype(jnp.float32)).astype(jnp.bfloat16)
            return carry

        lax.fori_loop(0, rows // 2, one_pair, 0)
        share = jnp.dot(weights[...], flat_state, preferred_element_type=jnp.float32)
        part[batch] = share[:nobs] + share[nobs:]

        def send_part(d, carry):
            index = lax.rem(plane_me + d, plane)
            copy = pltpu.make_async_remote_copy(
                src_ref=part.at[batch, *tile_of(index)], dst_ref=pieces.at[batch, d],
                send_sem=send_sem.at[batch, 0], recv_sem=part_sem.at[batch],
                device_id=plane_device(index), device_id_type=MESH,
            )
            copy.start()
            return carry

        def tile_of(index):
            halves = members // LANES
            band = nobs * halves // plane
            return (
                pl.ds(pl.multiple_of((index // halves) * band, band), band),
                pl.ds(pl.multiple_of((index % halves) * LANES, LANES), LANES),
            )

        lax.fori_loop(1, plane, send_part, 0)

    for batch in range(BATCHES):
        pltpu.make_async_copy(pieces.at[batch, 1:plane], pieces.at[batch, 1:plane], part_sem.at[batch]).wait()
        piece[batch] = part[batch, *tile_of(plane_me)] + jnp.sum(pieces[batch, 1:plane], axis=0)

        def send_line(d, carry):
            copy = pltpu.make_async_remote_copy(
                src_ref=piece.at[batch], dst_ref=line.at[batch, d],
                send_sem=send_sem.at[batch, 1], recv_sem=line_sem.at[batch],
                device_id=line_device(lax.rem(line_me + d, lines)), device_id_type=MESH,
            )
            copy.start()
            return carry

        lax.fori_loop(1, lines, send_line, 0)

    for copy in far:
        copy.wait_recv()
    for side, first in ((0, PAD - 2), (1, PAD + cols)):
        for j in range(2):
            grid[2 : 2 + rows, first + j, :] = edge_got[side, j]
    width = cols + 2 * PAD
    for index, step in enumerate(ONE_STEP):
        upright = jnp.concatenate([weight[step], jnp.zeros((LANES - rows - 16, LANES), jnp.float32)], axis=0)
        links[index] = jnp.transpose(pltpu.roll(upright, PAD, 1))[:width]

    def one_row(r, source, target):
        rolled = [
            jnp.broadcast_to(pltpu.roll(links[i], lax.rem(LANES - r - 6, LANES), 1)[:, 0:1], (width, LANES))
            for i in range(len(ONE_STEP))
        ]
        for first in range(0, members, LANES):
            lanes = pl.ds(first, LANES)
            here = source[r, :, lanes]
            target(
                r, lanes,
                rolled[0] * here
                + rolled[1] * source[r - 1, :, lanes]
                + rolled[2] * source[r + 1, :, lanes]
                + rolled[3] * pltpu.roll(here, 1, 0)
                + rolled[4] * pltpu.roll(here, width - 1, 0),
            )

    def first_row(r, carry):
        def store(r, lanes, value):
            halfway[r, :, lanes] = value

        one_row(r, grid, store)
        return carry

    halfway = got[1]
    lax.fori_loop(1, rows + 3, first_row, 0)

    def second_row_of(r, carry):
        def store(r, lanes, value):
            grid[r, :, lanes] = value

        one_row(r, halfway, store)
        return carry

    for copy in far:
        copy.wait_send()
    lax.fori_loop(2, rows + 2, second_row_of, 0)
    out = pltpu.make_async_copy(grid.at[pl.ds(2, rows), pl.ds(PAD, cols)], field_ref, out_sem)
    out.start()

    priors = got[0]
    for batch in range(BATCHES):
        pltpu.make_async_copy(line.at[batch, 1:lines], line.at[batch, 1:lines], line_sem.at[batch]).wait()
        mine = tile_of(plane_me)
        priors[batch, *mine] = piece[batch] + jnp.sum(line[batch, 1:lines], axis=0)

        def send_all(d, carry):
            copy = pltpu.make_async_remote_copy(
                src_ref=priors.at[batch, *mine], dst_ref=priors.at[batch, *mine],
                send_sem=send_sem.at[batch, 2], recv_sem=all_sem.at[batch],
                device_id=plane_device(lax.rem(plane_me + d, plane)), device_id_type=MESH,
            )
            copy.start()
            return carry

        lax.fori_loop(1, plane, send_all, 0)
    for batch in range(BATCHES):
        block = pieces.at[batch, 1:plane]
        pltpu.make_async_copy(block, block, all_sem.at[batch]).wait()
        priors_ref[batch] = priors[batch]

    for copy in near:
        copy.wait_send()
    for batch in range(BATCHES):
        block = pieces.at[batch, 1:plane]
        pltpu.make_async_copy(block, block, send_sem.at[batch, 0]).wait()
        block = line.at[batch, 1:lines]
        pltpu.make_async_copy(block, block, send_sem.at[batch, 1]).wait()
        block = pieces.at[batch, 1:plane]
        pltpu.make_async_copy(block, block, send_sem.at[batch, 2]).wait()
    out.wait()


def gather(state, courant, where, lon_count, lat_count):
    rows, cols, members = state.shape
    nobs = where.shape[2]
    plane_lon, line_lon, line_lat, plane_lat = split_mesh(lon_count, lat_count)
    plane, lines = plane_lon * plane_lat, line_lat * line_lon
    band = nobs * (members // LANES) // plane
    width = cols + 2 * PAD
    f32 = jnp.float32
    vmem = pl.BlockSpec(memory_space=pltpu.VMEM)
    dma = pltpu.SemaphoreType.DMA
    return pl.pallas_call(
        functools.partial(gather_kernel, (lon_count, lat_count)),
        out_shape=(
            jax.ShapeDtypeStruct((BATCHES, nobs, members), f32),
            jax.ShapeDtypeStruct((rows, cols, members), f32),
        ),
        in_specs=[vmem] * 3,
        out_specs=(vmem, pl.BlockSpec(memory_space=pl.ANY)),
        scratch_shapes=[
            pltpu.VMEM((2, 2, 8, cols), f32),
            pltpu.VMEM((2, 2, rows, cols), f32),
            pltpu.VMEM((4, 2, 8, cols), f32),
            pltpu.VMEM((2, rows + 16, LANES), f32),
            pltpu.VMEM((len(TWO_STEPS), rows, LANES), f32),
            pltpu.VMEM((len(TWO_STEPS), rows // 2, LANES), f32),
            pltpu.VMEM((len(ONE_STEP), width, LANES), f32),
            pltpu.VMEM((2 * nobs, rows * cols), jnp.bfloat16),
            pltpu.VMEM((BATCHES, nobs, members), f32),
            pltpu.VMEM((BATCHES, plane, band, LANES), f32),
            pltpu.VMEM((BATCHES, band, LANES), f32),
            pltpu.VMEM((BATCHES, lines, band, LANES), f32),
            [pltpu.VMEM((BATCHES, nobs, members), f32), pltpu.VMEM((rows + 4, width, members), f32)],
            pltpu.VMEM((rows + 4, width, members), f32),
            pltpu.VMEM((2, 2, rows, members), f32),
            pltpu.VMEM((2, 2, rows, members), f32),
            dma((8, 2)),
            dma((8, 2)),
            dma((BATCHES,)),
            dma((BATCHES,)),
            dma((BATCHES,)),
            dma((BATCHES, 3)),
            dma,
        ],
        compiler_params=pltpu.CompilerParams(
            collective_id=0, has_side_effects=True, vmem_limit_bytes=48 * 1024 * 1024
        ),
        name="advance_and_gather",
    )(state, courant, where)


def matmul_exact(left, right, contract=(1, 0)):
    return lax.dot_general(
        left, right, (((contract[0],), (contract[1],)), ((), ())),
        precision=HIGHEST, preferred_element_type=jnp.float32,
    )


def halves_of(value):
    upper = value.astype(jnp.bfloat16)
    return upper, (value - upper.astype(jnp.float32)).astype(jnp.bfloat16)


def matmul_halves(left, right):
    total = jnp.dot(left[0], right[1], preferred_element_type=jnp.float32)
    total += jnp.dot(left[1], right[0], preferred_element_type=jnp.float32)
    return total + jnp.dot(left[0], right[0], preferred_element_type=jnp.float32)


def solve_pivot(pivot, rows):
    count = len(rows)
    pivot, rows, factor, inverse = dict(pivot), list(rows), {}, {}
    for j in range(0, count, 2):
        a, b, c = pivot[j, j], pivot[j + 1, j], pivot[j + 1, j + 1]
        scale = 1.0 / (a * c - b * b)
        inverse[j] = first, cross, last = c * scale, -b * scale, a * scale
        for i in range(j + 2, count):
            factor[i, j] = pivot[i, j] * first + pivot[i, j + 1] * cross
            factor[i, j + 1] = pivot[i, j] * cross + pivot[i, j + 1] * last
        for i in range(j + 2, count):
            for k in range(j + 2, i + 1):
                pivot[i, k] -= factor[i, j] * pivot[k, j] + factor[i, j + 1] * pivot[k, j + 1]
    for j in range(0, count, 2):
        for i in range(j + 2, count):
            rows[i] -= factor[i, j] * rows[j] + factor[i, j + 1] * rows[j + 1]
    for j in range(0, count, 2):
        first, cross, last = inverse[j]
        rows[j], rows[j + 1] = first * rows[j] + cross * rows[j + 1], cross * rows[j] + last * rows[j + 1]
    for i in reversed(range(0, count, 2)):
        for j in range(i):
            rows[j] -= factor[i, j] * rows[i] + factor[i + 1, j] * rows[i + 1]
    return rows


def tree_sum(terms):
    while len(terms) > 1:
        terms = [a + b for a, b in zip(terms[::2], terms[1::2])] + terms[len(terms) // 2 * 2 :]
    return terms[0]


def inverse_of(system, panel=32):
    size = system.shape[0]
    spread = (8, size)
    lane = lax.broadcasted_iota(jnp.int32, spread, 1)
    sub = lax.broadcasted_iota(jnp.int32, spread, 0)
    panel_lane = lax.broadcasted_iota(jnp.int32, (panel, size), 1)
    panel_sub = lax.broadcasted_iota(jnp.int32, (panel, size), 0)
    whole_lane = lax.broadcasted_iota(jnp.int32, (size, size), 1)
    for start in range(0, size, panel):
        old = system[start : start + panel]
        bands = [old[i : i + 8] for i in range(0, panel, 8)]
        for here in range(panel // 8):
            first = start + 8 * here
            inside = (lane >= first) & (lane < first + 8)
            columns = [
                [jnp.broadcast_to(band[:, first + j : first + j + 1], spread) for j in range(8)] for band in bands
            ]
            pivot = {
                (i, j): jnp.broadcast_to(columns[here][j][i : i + 1], spread) for i in range(8) for j in range(i + 1)
            }
            rows = [
                jnp.where(inside, jnp.where(lane == first + j, -1.0, 0.0), jnp.broadcast_to(bands[here][j : j + 1], spread))
                for j in range(8)
            ]
            rows = solve_pivot(pivot, rows)
            for i, band in enumerate(bands):
                if i != here:
                    terms = [columns[i][j] * rows[j] for j in range(8)]
                    bands[i] = jnp.where(inside, 0.0, band) - tree_sum(terms)
            swept = rows[7]
            for j in range(7):
                swept = jnp.where(sub == j, rows[j], swept)
            bands[here] = swept
        swept = jnp.concatenate(bands, axis=0)
        inside = (panel_lane >= start) & (panel_lane < start + panel)
        old = jnp.where(inside, jnp.where(panel_lane == panel_sub + start, -1.0, 0.0), old)
        inside = (whole_lane >= start) & (whole_lane < start + panel)
        system = jnp.where(inside, 0.0, system) - matmul_exact(old, swept, (0, 0))
        parts = [system[:start], swept, system[start + panel :]]
        system = jnp.concatenate([part for part in parts if part.shape[0]], axis=0)
    return -system


def square(value):
    return value * value


def analysis_kernel(
    sizes, priors_ref, field_ref, where_ref, value_ref, variance_ref, noise_ref, out_ref,
    field, spread, analysis, field_sem, out_sem,
):
    lon_count, lat_count = sizes
    rows, cols, members = field_ref.shape
    nobs = where_ref.shape[2]
    total_cols = cols * lon_count
    first_row, first_col = lax.axis_index("lat") * rows, lax.axis_index("lon") * cols
    fetch = pltpu.make_async_copy(field_ref, field, field_sem)
    fetch.start()

    blank = jnp.zeros((8 - 2 * BATCHES, nobs), jnp.float32)
    upright = jnp.transpose(jnp.concatenate([value_ref[...], variance_ref[...], blank], axis=0))
    eye = lax.broadcasted_iota(jnp.int32, (nobs, nobs), 0) == lax.broadcasted_iota(jnp.int32, (nobs, nobs), 1)

    def lon_distance(cell, obs):
        gap = jnp.abs(cell - obs)
        return jnp.minimum(gap, total_cols - gap)

    def scaled_square(gap, radius):
        return square(gap).astype(jnp.float32) / square(radius).astype(jnp.float32)

    def weights_of(batch, priors, anomaly):
        variance = upright[:, BATCHES + batch : BATCHES + batch + 1]
        system = matmul_exact(anomaly, anomaly, (1, 1)) / (members - 1)
        system += jnp.where(eye, variance, 0.0)
        misfit = upright[:, batch : batch + 1] + jnp.sqrt(variance) * noise_ref[batch] - priors
        return matmul_exact(inverse_of(system), misfit)

    def centred(priors):
        return priors - jnp.mean(priors, axis=1, keepdims=True)

    obs = [[where_ref[batch, i : i + 1, :] for i in range(3)] for batch in range(BATCHES)]
    priors = [priors_ref[batch] for batch in range(BATCHES)]
    anomaly, weights = [centred(priors[0])], []
    weights.append(weights_of(0, priors[0], anomaly[0]))

    where = jnp.concatenate([where_ref[1].astype(jnp.float32), jnp.zeros((8 - 3, nobs), jnp.float32)], axis=0)
    where = jnp.transpose(where).astype(jnp.int32)
    lat_gap = where[:, 0:1] - obs[0][0]
    lon_gap = lon_distance(where[:, 1:2], obs[0][1])
    distance = (square(lat_gap) + square(lon_gap)).astype(jnp.float32)
    taper = square(jnp.maximum(1.0 - distance / square(obs[0][2]).astype(jnp.float32), 0.0))
    covariance = matmul_exact(centred(priors[1]), anomaly[0], (1, 1)) / (members - 1)
    priors[1] += matmul_exact(taper * covariance, weights[0])
    anomaly.append(centred(priors[1]))
    carried = halves_of(matmul_exact(centred(weights[0]), anomaly[1], (1, 1)) / (members - 1))

    both = [jnp.transpose(part) for part in halves_of(jnp.concatenate(anomaly, axis=0) / (members - 1))]
    cell_lon = first_col + lax.broadcasted_iota(jnp.int32, (cols, 1), 0)
    lon_part = [scaled_square(lon_distance(cell_lon, lon), radius) for _, lon, radius in obs]
    chunk = 4
    fetch.wait()

    def taper_of(batch, row):
        lat, _, radius = obs[batch]
        room = 1.0 - scaled_square(first_row + row - lat, radius)
        return square(jnp.maximum(room - lon_part[batch], 0.0))

    def spread_chunk(index, carry):
        cells = field[pl.ds(index * chunk, chunk)].reshape(chunk * cols, members)
        covariance = matmul_halves(halves_of(cells), both)
        tapers = [
            jnp.concatenate([taper_of(batch, index * chunk + r) for r in range(chunk)], axis=0)
            for batch in range(BATCHES)
        ]
        first = tapers[0] * covariance[:, :nobs]
        second = tapers[1] * (covariance[:, nobs:] + matmul_halves(halves_of(first), carried))
        at = pl.ds(pl.multiple_of(index * chunk * cols, chunk * cols), chunk * cols)
        for i, part in enumerate(halves_of(jnp.concatenate([first, second], axis=1))):
            spread[i, at] = part
        return carry

    lax.fori_loop(0, rows // chunk, spread_chunk, 0)

    weights.append(weights_of(1, priors[1], anomaly[1]))
    both_weights = halves_of(jnp.concatenate(weights, axis=0))

    def copy_out(index):
        at = pl.ds(index * chunk, chunk)
        return pltpu.make_async_copy(analysis.at[at], out_ref.at[at], out_sem.at[index])

    def update_chunk(index, carry):
        at = pl.ds(pl.multiple_of(index * chunk * cols, chunk * cols), chunk * cols)
        change = matmul_halves((spread[0, at], spread[1, at]), both_weights)
        at = pl.ds(index * chunk, chunk)
        analysis[at] = (field[at] + change.reshape(chunk, cols, members)).astype(jnp.bfloat16)
        copy_out(index).start()
        return carry

    lax.fori_loop(0, rows // chunk, update_chunk, 0)
    for index in range(rows // chunk):
        copy_out(index).wait()


def analyse(priors, field, where, value, variance, noise, lon_count, lat_count):
    rows, cols, members = field.shape
    nobs = where.shape[2]
    vmem, anywhere = pl.BlockSpec(memory_space=pltpu.VMEM), pl.BlockSpec(memory_space=pl.ANY)
    return pl.pallas_call(
        functools.partial(analysis_kernel, (lon_count, lat_count)),
        out_shape=jax.ShapeDtypeStruct((rows, cols, members), jnp.bfloat16),
        in_specs=[vmem, anywhere, vmem, vmem, vmem, vmem],
        out_specs=anywhere,
        scratch_shapes=[
            pltpu.VMEM((rows, cols, members), jnp.float32),
            pltpu.VMEM((2, rows * cols, BATCHES * nobs), jnp.bfloat16),
            pltpu.VMEM((rows, cols, members), jnp.bfloat16),
            pltpu.SemaphoreType.DMA,
            pltpu.SemaphoreType.DMA((rows // 4,)),
        ],
        compiler_params=pltpu.CompilerParams(vmem_limit_bytes=32 * 1024 * 1024),
        name="analyse",
    )(priors, field, where, value, variance, noise)


def body(ensemble_state, courant, obs_where, obs_value, obs_variance, obs_noise):
    counts = lax.axis_size("lon"), lax.axis_size("lat")
    priors, field = gather(ensemble_state, courant, obs_where, *counts)
    return analyse(priors, field, obs_where, obs_value, obs_variance, obs_noise, *counts)


def solution(mesh):
    placed = (P("lat", "lon", None), P(None, "lat", "lon"), P(), P(), P(), P())
    return jax.shard_map(
        body, mesh=mesh, in_specs=placed, out_specs=P("lat", "lon", None), check_vma=False
    )
```

```python
import functools
import jax
import jax.numpy as jnp
from jax import lax
from jax.experimental import pallas as pl
from jax.experimental.pallas import tpu as pltpu
from jax.sharding import PartitionSpec as P

BATCHES = 2
MESH = pl.DeviceIdType.MESH
PAD = 8
LANES = 128
HIGHEST = lax.Precision.HIGHEST
ONE_STEP = ((0, 0), (-1, 0), (1, 0), (0, -1), (0, 1))
TWO_STEPS = tuple(sorted({(a + c, b + d) for a, b in ONE_STEP for c, d in ONE_STEP}))


def split_mesh(lon_count, lat_count):
    plane_lat = 8 if lat_count == 16 else lat_count // 2
    line_lon = 8 if lon_count == 32 else lon_count // 2
    return lon_count // line_lon, line_lon, lat_count // plane_lat, plane_lat


def shifted(field, rows, lanes):
    if rows:
        field = pltpu.roll(field, rows % field.shape[0], 0)
    if lanes:
        field = pltpu.roll(field, lanes % field.shape[1], 1)
    return field


def link_weights(speed_lat, speed_lon, row, total_rows):
    inside = (row >= 0) & (row < total_rows)
    lat_plus = jnp.maximum(speed_lat, 0.0)
    lat_minus = jnp.minimum(speed_lat, 0.0)
    lon_plus = jnp.maximum(speed_lon, 0.0)
    lon_minus = jnp.minimum(speed_lon, 0.0)
    zero = jnp.zeros_like(speed_lat)
    return {
        (0, 0): jnp.where(inside, 1.0 - lat_plus + lat_minus - lon_plus + lon_minus, zero),
        (-1, 0): jnp.where(inside & (row > 0), lat_plus, zero),
        (1, 0): jnp.where(inside & (row < total_rows - 1), -lat_minus, zero),
        (0, -1): jnp.where(inside, lon_plus, zero),
        (0, 1): jnp.where(inside, -lon_minus, zero),
    }


def ring_flips(count):
    flips = [lambda place: place]
    size = 1
    while size < count:
        flips += [lambda place, size=size, f=f: flip_bit(f(place), size) for f in flips]
        size *= 2
    return flips


def flip_bit(place, size):
    return place + size - 2 * size * (place // size % 2)


def gather_kernel(
    sizes, state_hbm, courant_hbm, where_ref,
    priors_ref, field_ref,
    state_ref, courant_ref, near_ns, near_ew, near_corner, reach, wide, stencil, weights, part, pieces, piece, line, priors,
    cells, bands, far_ns, far_ew, far_corner, field,
    in_sem, near_sem, far_sem, part_sem, line_sem, all_sem, send_sem, out_sem,
):
    lon_count, lat_count = sizes
    plane_lon, line_lon, line_lat, plane_lat = split_mesh(lon_count, lat_count)
    plane, lines = plane_lon * plane_lat, line_lat * line_lon
    rows, cols, members = state_ref.shape
    total_rows, total_cols = rows * lat_count, cols * lon_count
    nobs = where_ref.shape[2]
    halves = members // LANES
    band = nobs * halves // plane
    lon, lat = lax.axis_index("lon"), lax.axis_index("lat")
    line_me = (lat // plane_lat) * line_lon + lon % line_lon
    loads = [
        pltpu.make_async_copy(courant_hbm, courant_ref, in_sem.at[0]),
        pltpu.make_async_copy(state_hbm, state_ref, in_sem.at[1]),
    ]
    for load in loads:
        load.start()

    lon_flips, lat_flips = ring_flips(plane_lon), ring_flips(plane_lat)
    plane_x = [flip(lon // line_lon) for flip in lon_flips]
    plane_y = [flip(lat % plane_lat) for flip in lat_flips]
    partners = [(i, j) for i in range(plane_lon) for j in range(plane_lat)][1:]
    hops = {0: 0, 1: 1, 2: 2, 3: 1}
    partners.sort(key=lambda p: -hops[p[0] % 4] - hops[p[1] // 2 % 4])
    distances = sorted(range(1, lines), key=lambda d: -min(d, lines - d))

    def plane_device(partner):
        return {
            "lon": plane_x[partner[0]] * line_lon + lon % line_lon,
            "lat": lat // plane_lat * plane_lat + plane_y[partner[1]],
        }

    def tile_of(partner):
        index = plane_x[partner[0]] * plane_lat + plane_y[partner[1]]
        return (
            pl.ds(pl.multiple_of(index // halves * band, band), band),
            pl.ds(pl.multiple_of(index % halves * LANES, LANES), LANES),
        )

    def line_device(distance):
        index = lax.rem(line_me + distance, lines)
        return {
            "lon": lon // line_lon * line_lon + index % line_lon,
            "lat": index // line_lon * plane_lat + lat % plane_lat,
        }

    def neighbour(lat_step, lon_step):
        return {
            "lon": lax.rem(lon + lon_step + lon_count, lon_count),
            "lat": lax.rem(lat + lat_step + lat_count, lat_count),
        }

    around = [(a, b) for a in (-1, 1) for b in (0, -1, 1)] + [(0, -1), (0, 1)]

    barrier = pltpu.get_barrier_semaphore()
    greeted = [neighbour(*step) for step in around]
    greeted += [line_device(distance) for distance in distances]
    greeted += [plane_device(partner) for partner in partners]
    for target in greeted:
        pl.semaphore_signal(barrier, inc=1, device_id=target, device_id_type=MESH)

    for load in loads:
        load.wait()
    edges, ends = ((0, 2), (rows - 2, rows)), ((0, 2), (cols - 2, cols))
    for side in range(2):
        low, high = edges[side]
        far_ns[side] = state_ref[low:high].astype(jnp.float32)
        low, high = ends[side]
        far_ew[side] = state_ref[:, low:high].astype(jnp.float32)
        for other in range(2):
            row, first = (0, rows - 1)[side], (0, cols - 8)[other]
            far_corner[2 * side + other] = state_ref[row, first : first + 8].astype(jnp.float32)
    cells[...] = jnp.zeros(cells.shape, jnp.bfloat16)
    cells[2 : 2 + rows, :cols] = state_ref[...]
    pl.semaphore_wait(barrier, len(greeted))

    def send(src, dst, sem, step):
        copy = pltpu.make_async_remote_copy(
            src_ref=src, dst_ref=dst, send_sem=sem.at[0], recv_sem=sem.at[1],
            device_id=neighbour(*step), device_id_type=MESH,
        )
        copy.start()
        return copy

    low, high = pl.ds(0, 8), pl.ds(rows - 8, 8)
    near = []
    for index, (a, b) in enumerate(around):
        source = courant_ref.at[:, {-1: low, 1: high}[a], :] if a else courant_ref
        if a and b:
            target = near_corner.at[(0 if a > 0 else 2) + (0 if b > 0 else 1)]
        elif a:
            target = near_ns.at[0 if a > 0 else 1]
        else:
            target = near_ew.at[0 if b > 0 else 1]
        near.append(send(source, target, near_sem.at[index], (a, b)))

    far = []
    for index, (a, b) in enumerate(around):
        up, right = int(a > 0), int(b > 0)
        if a and b:
            source, target = far_corner.at[2 * up + right], far_corner.at[4 + 2 * (1 - up) + (1 - right)]
        elif a:
            source, target = far_ns.at[up], far_ns.at[2 + 1 - up]
        else:
            source, target = far_ew.at[right], far_ew.at[2 + 1 - right]
        far.append(send(source, target, far_sem.at[index], (a, b)))
    for copy in near:
        copy.wait_recv()

    lane = lax.broadcasted_iota(jnp.int32, (8, LANES), 1)

    def assemble(own, west, east):
        blank = jnp.zeros((8, LANES - cols), jnp.float32)
        own = jnp.concatenate([own, blank], axis=1)
        west = jnp.concatenate([blank, west], axis=1)
        east = jnp.concatenate([blank, east], axis=1)
        return jnp.where(lane < cols, own, jnp.where(lane < cols + 2, east, west))

    for c in range(2):
        reach[c, 0:8] = assemble(near_ns[0, c], near_corner[0, c], near_corner[1, c])
        for r in range(0, rows, 8):
            band_rows = pl.ds(r, 8)
            reach[c, r + 8 : r + 16] = assemble(
                courant_ref[c, band_rows], near_ew[0, c, band_rows], near_ew[1, c, band_rows]
            )
        reach[c, rows + 8 : rows + 16] = assemble(near_ns[1, c], near_corner[2, c], near_corner[3, c])

    row = lax.broadcasted_iota(jnp.int32, (rows + 16, LANES), 0) - 8 + lat * rows
    weight = link_weights(reach[0], reach[1], row, total_rows)

    arrived = {step: shifted(weight[step], *step) for step in ONE_STEP}
    sums = {}
    for first in ONE_STEP:
        for second in ONE_STEP:
            total = (first[0] + second[0], first[1] + second[1])
            term = shifted(arrived[first] * weight[second], *second)
            sums[total] = sums[total] + term if total in sums else term
    half = lax.broadcasted_iota(jnp.int32, (rows // 2, LANES), 1) < cols
    for index, total in enumerate(TWO_STEPS):
        wide[index] = sums[total]
        even = wide[index, pl.ds(8, rows // 2, 2), :]
        odd = wide[index, pl.ds(9, rows // 2, 2), :]
        stencil[index] = jnp.where(half, even, pltpu.roll(odd, cols, 1))

    def halves_into(ref, at, columns, value):
        upper = value.astype(jnp.bfloat16)
        count = value.shape[0]
        ref[at : at + count, columns] = upper
        ref[at + count : at + 2 * count, columns] = (value - upper.astype(jnp.float32)).astype(jnp.bfloat16)

    flat_lane = lax.broadcasted_iota(jnp.int32, (nobs, LANES), 1)
    second_row = jnp.where(flat_lane >= cols, 1, 0)
    column = flat_lane - second_row * cols
    flat_state = state_ref[...].reshape(rows * cols, members)
    for batch in range(BATCHES):
        where = jnp.concatenate([where_ref[i, batch : batch + 1] for i in range(3)], axis=0)
        where = jnp.concatenate([where, jnp.zeros((8 - 3, nobs), jnp.int32)], axis=0)
        where = jnp.transpose(where.astype(jnp.float32)).astype(jnp.int32)
        obs_row = where[:, 0:1] - lat * rows
        obs_col = where[:, 1:2] - lon * cols + 2
        obs_col = jnp.where(obs_col < 0, obs_col + total_cols, obs_col) - 2
        obs_col = jnp.where(obs_col >= total_cols - 2, obs_col - total_cols, obs_col)
        lon_step = column - obs_col
        lat_base = second_row - obs_row

        def one_pair(pair, carry):
            lat_step = lat_base + 2 * pair
            total = jnp.zeros((nobs, LANES), jnp.float32)
            for index, (a, b) in enumerate(TWO_STEPS):
                total = jnp.where((lat_step == a) & (lon_step == b), stencil[index, pl.ds(pair, 1), :], total)
            halves_into(weights, 0, pl.ds(pl.multiple_of(pair * LANES, LANES), LANES), total)
            return carry

        lax.fori_loop(0, rows // 2, one_pair, 0)
        share = jnp.dot(weights[...], flat_state, preferred_element_type=jnp.float32)
        part[batch] = share[:nobs] + share[nobs:]
        for index, partner in enumerate(partners):
            pltpu.make_async_remote_copy(
                src_ref=part.at[batch, *tile_of(partner)], dst_ref=pieces.at[batch, index],
                send_sem=send_sem.at[batch, 0], recv_sem=part_sem.at[batch],
                device_id=plane_device(partner), device_id_type=MESH,
            ).start()

    mine = tile_of((0, 0))
    for batch in range(BATCHES):
        pltpu.make_async_copy(pieces.at[batch], pieces.at[batch], part_sem.at[batch]).wait()
        piece[batch] = part[batch, *mine] + jnp.sum(pieces[batch], axis=0)
        for index, distance in enumerate(distances):
            pltpu.make_async_remote_copy(
                src_ref=piece.at[batch], dst_ref=line.at[batch, index],
                send_sem=send_sem.at[batch, 1], recv_sem=line_sem.at[batch],
                device_id=line_device(distance), device_id_type=MESH,
            ).start()

    for copy in far:
        copy.wait_recv()
    gap = jnp.zeros((14, members), jnp.float32)

    def beside(at, west, east):
        cells[at, cols : cols + 16] = jnp.concatenate([east, gap], axis=0).astype(jnp.bfloat16)
        cells[at, LANES - 16 :] = jnp.concatenate([gap, west], axis=0).astype(jnp.bfloat16)

    def beside_row(r, carry):
        beside(r + 2, far_ew[2, r], far_ew[3, r])
        return carry

    lax.fori_loop(0, rows, beside_row, 0)
    for side, at in ((0, 1), (1, rows + 2)):
        cells[(0, rows + 2)[side] : (2, rows + 4)[side], :cols] = far_ns[2 + side].astype(jnp.bfloat16)
        beside(at, far_corner[4 + 2 * side, 6:8], far_corner[4 + 2 * side + 1, 0:2])
    step_lane = lax.broadcasted_iota(jnp.int32, (cols, LANES), 1) - lax.broadcasted_iota(jnp.int32, (cols, LANES), 0)
    step_lane = jnp.where(step_lane > LANES // 2 + 2, step_lane - LANES, step_lane)

    def one_pair_of_rows(pair, carry):
        first = 2 * pair
        for around_row in range(6):
            for r in range(2):
                a = around_row - 2 - r
                total = jnp.zeros((cols, LANES), jnp.float32)
                if -2 <= a <= 2:
                    for index, (lat_step, b) in enumerate(TWO_STEPS):
                        if lat_step == a:
                            total = jnp.where(step_lane == b, wide[index, pl.ds(first + around_row + 6, 1), :], total)
                halves_into(bands, 2 * r * cols, pl.ds(around_row * LANES, LANES), total)
        near_cells = cells[pl.ds(first, 6)].reshape(6 * LANES, members)
        result = jnp.dot(bands[...], near_cells, preferred_element_type=jnp.float32)
        for r in range(2):
            field[first + r] = result[2 * r * cols : (2 * r + 1) * cols] + result[(2 * r + 1) * cols : (2 * r + 2) * cols]
        return carry

    lax.fori_loop(0, rows // 2, one_pair_of_rows, 0)
    out = pltpu.make_async_copy(field, field_ref, out_sem)
    out.start()

    for batch in range(BATCHES):
        pltpu.make_async_copy(line.at[batch], line.at[batch], line_sem.at[batch]).wait()
        priors[batch, *mine] = piece[batch] + jnp.sum(line[batch], axis=0)
        for partner in partners:
            pltpu.make_async_remote_copy(
                src_ref=priors.at[batch, *mine], dst_ref=priors.at[batch, *mine],
                send_sem=send_sem.at[batch, 2], recv_sem=all_sem.at[batch],
                device_id=plane_device(partner), device_id_type=MESH,
            ).start()
    for batch in range(BATCHES):
        pltpu.make_async_copy(pieces.at[batch], pieces.at[batch], all_sem.at[batch]).wait()
        priors_ref[batch] = priors[batch]

    for copy in near + far:
        copy.wait_send()
    for batch in range(BATCHES):
        for sem, sent in enumerate((pieces, line, pieces)):
            pltpu.make_async_copy(sent.at[batch], sent.at[batch], send_sem.at[batch, sem]).wait()
    out.wait()


def gather(state, courant, where, lon_count, lat_count):
    rows, cols, members = state.shape
    nobs = where.shape[2]
    plane_lon, line_lon, line_lat, plane_lat = split_mesh(lon_count, lat_count)
    plane, lines = plane_lon * plane_lat, line_lat * line_lon
    band = nobs * (members // LANES) // plane
    f32, bf16 = jnp.float32, jnp.bfloat16
    vmem, hbm = pl.BlockSpec(memory_space=pltpu.VMEM), pl.BlockSpec(memory_space=pltpu.HBM)
    dma = pltpu.SemaphoreType.DMA
    return pl.pallas_call(
        functools.partial(gather_kernel, (lon_count, lat_count)),
        out_shape=(
            jax.ShapeDtypeStruct((BATCHES, nobs, members), f32),
            jax.ShapeDtypeStruct((rows, cols, members), f32),
        ),
        in_specs=[hbm, hbm, vmem],
        out_specs=(vmem, pl.BlockSpec(memory_space=pl.ANY)),
        scratch_shapes=[
            pltpu.VMEM((rows, cols, members), bf16),
            pltpu.VMEM((2, rows, cols), f32),
            pltpu.VMEM((2, 2, 8, cols), f32),
            pltpu.VMEM((2, 2, rows, cols), f32),
            pltpu.VMEM((4, 2, 8, cols), f32),
            pltpu.VMEM((2, rows + 16, LANES), f32),
            pltpu.VMEM((len(TWO_STEPS), rows + 16, LANES), f32),
            pltpu.VMEM((len(TWO_STEPS), rows // 2, LANES), f32),
            pltpu.VMEM((2 * nobs, rows * cols), bf16),
            pltpu.VMEM((BATCHES, nobs, members), f32),
            pltpu.VMEM((BATCHES, plane - 1, band, LANES), f32),
            pltpu.VMEM((BATCHES, band, LANES), f32),
            pltpu.VMEM((BATCHES, lines - 1, band, LANES), f32),
            pltpu.VMEM((BATCHES, nobs, members), f32),
            pltpu.VMEM((rows + 4, LANES, members), bf16),
            pltpu.VMEM((4 * cols, 6 * LANES), bf16),
            pltpu.VMEM((4, 2, cols, members), f32),
            pltpu.VMEM((4, rows, 2, members), f32),
            pltpu.VMEM((8, 8, members), f32),
            pltpu.VMEM((rows, cols, members), f32),
            dma((2,)),
            dma((8, 2)),
            dma((8, 2)),
            dma((BATCHES,)),
            dma((BATCHES,)),
            dma((BATCHES,)),
            dma((BATCHES, 3)),
            dma,
        ],
        compiler_params=pltpu.CompilerParams(
            collective_id=0, has_side_effects=True, vmem_limit_bytes=40 * 1024 * 1024
        ),
        name="advance_and_gather",
    )(state, courant, where)


def matmul_exact(left, right, contract=(1, 0)):
    return lax.dot_general(
        left, right, (((contract[0],), (contract[1],)), ((), ())),
        precision=HIGHEST, preferred_element_type=jnp.float32,
    )


def halves_of(value):
    upper = value.astype(jnp.bfloat16)
    return upper, (value - upper.astype(jnp.float32)).astype(jnp.bfloat16)


def matmul_halves(left, right):
    total = jnp.dot(left[0], right[1], preferred_element_type=jnp.float32)
    total += jnp.dot(left[1], right[0], preferred_element_type=jnp.float32)
    return total + jnp.dot(left[0], right[0], preferred_element_type=jnp.float32)


def solve_pivot(pivot, rows):
    count = len(rows)
    pivot, rows, factor, inverse = dict(pivot), list(rows), {}, {}
    for j in range(0, count, 2):
        a, b, c = pivot[j, j], pivot[j + 1, j], pivot[j + 1, j + 1]
        scale = 1.0 / (a * c - b * b)
        inverse[j] = first, cross, last = c * scale, -b * scale, a * scale
        for i in range(j + 2, count):
            factor[i, j] = pivot[i, j] * first + pivot[i, j + 1] * cross
            factor[i, j + 1] = pivot[i, j] * cross + pivot[i, j + 1] * last
        for i in range(j + 2, count):
            for k in range(j + 2, i + 1):
                pivot[i, k] -= factor[i, j] * pivot[k, j] + factor[i, j + 1] * pivot[k, j + 1]
    for j in range(0, count, 2):
        for i in range(j + 2, count):
            rows[i] -= factor[i, j] * rows[j] + factor[i, j + 1] * rows[j + 1]
    for j in range(0, count, 2):
        first, cross, last = inverse[j]
        rows[j], rows[j + 1] = first * rows[j] + cross * rows[j + 1], cross * rows[j] + last * rows[j + 1]
    for i in reversed(range(0, count, 2)):
        for j in range(i):
            rows[j] -= factor[i, j] * rows[i] + factor[i + 1, j] * rows[i + 1]
    return rows


def tree_sum(terms):
    while len(terms) > 1:
        terms = [a + b for a, b in zip(terms[::2], terms[1::2])] + terms[len(terms) // 2 * 2 :]
    return terms[0]


def inverse_of(system, panel=32):
    size = system.shape[0]
    spread = (8, size)
    lane = lax.broadcasted_iota(jnp.int32, spread, 1)
    sub = lax.broadcasted_iota(jnp.int32, spread, 0)
    panel_lane = lax.broadcasted_iota(jnp.int32, (panel, size), 1)
    panel_sub = lax.broadcasted_iota(jnp.int32, (panel, size), 0)
    whole_lane = lax.broadcasted_iota(jnp.int32, (size, size), 1)
    for start in range(0, size, panel):
        old = system[start : start + panel]
        bands = [old[i : i + 8] for i in range(0, panel, 8)]
        for here in range(panel // 8):
            first = start + 8 * here
            inside = (lane >= first) & (lane < first + 8)
            columns = [
                [jnp.broadcast_to(band[:, first + j : first + j + 1], spread) for j in range(8)] for band in bands
            ]
            pivot = {
                (i, j): jnp.broadcast_to(columns[here][j][i : i + 1], spread) for i in range(8) for j in range(i + 1)
            }
            rows = [
                jnp.where(inside, jnp.where(lane == first + j, -1.0, 0.0), jnp.broadcast_to(bands[here][j : j + 1], spread))
                for j in range(8)
            ]
            rows = solve_pivot(pivot, rows)
            for i, band in enumerate(bands):
                if i != here:
                    terms = [columns[i][j] * rows[j] for j in range(8)]
                    bands[i] = jnp.where(inside, 0.0, band) - tree_sum(terms)
            swept = rows[7]
            for j in range(7):
                swept = jnp.where(sub == j, rows[j], swept)
            bands[here] = swept
        swept = jnp.concatenate(bands, axis=0)
        inside = (panel_lane >= start) & (panel_lane < start + panel)
        old = jnp.where(inside, jnp.where(panel_lane == panel_sub + start, -1.0, 0.0), old)
        inside = (whole_lane >= start) & (whole_lane < start + panel)
        system = jnp.where(inside, 0.0, system) - matmul_exact(old, swept, (0, 0))
        parts = [system[:start], swept, system[start + panel :]]
        system = jnp.concatenate([part for part in parts if part.shape[0]], axis=0)
    return -system


def square(value):
    return value * value


def analysis_kernel(
    sizes, priors_ref, field_ref, where_ref, value_ref, variance_ref, noise_ref, out_ref,
    field, spread, analysis, field_sem, out_sem,
):
    lon_count, lat_count = sizes
    rows, cols, members = field_ref.shape
    nobs = where_ref.shape[2]
    total_cols = cols * lon_count
    first_row, first_col = lax.axis_index("lat") * rows, lax.axis_index("lon") * cols
    fetch = pltpu.make_async_copy(field_ref, field, field_sem)
    fetch.start()

    blank = jnp.zeros((8 - 2 * BATCHES, nobs), jnp.float32)
    upright = jnp.transpose(jnp.concatenate([value_ref[...], variance_ref[...], blank], axis=0))
    eye = lax.broadcasted_iota(jnp.int32, (nobs, nobs), 0) == lax.broadcasted_iota(jnp.int32, (nobs, nobs), 1)

    def lon_distance(cell, obs):
        gap = jnp.abs(cell - obs)
        return jnp.minimum(gap, total_cols - gap)

    def scaled_square(gap, radius):
        return square(gap).astype(jnp.float32) / square(radius).astype(jnp.float32)

    def weights_of(batch, priors, anomaly):
        variance = upright[:, BATCHES + batch : BATCHES + batch + 1]
        system = matmul_exact(anomaly, anomaly, (1, 1)) / (members - 1)
        system += jnp.where(eye, variance, 0.0)
        misfit = upright[:, batch : batch + 1] + jnp.sqrt(variance) * noise_ref[batch] - priors
        return matmul_exact(inverse_of(system), misfit)

    def centred(priors):
        return priors - jnp.mean(priors, axis=1, keepdims=True)

    obs = [[where_ref[i, batch : batch + 1, :] for i in range(3)] for batch in range(BATCHES)]
    priors = [priors_ref[batch] for batch in range(BATCHES)]
    anomaly, weights = [centred(priors[0])], []
    weights.append(weights_of(0, priors[0], anomaly[0]))

    where = jnp.concatenate(obs[1] + [jnp.zeros((8 - 3, nobs), jnp.int32)], axis=0)
    where = jnp.transpose(where.astype(jnp.float32)).astype(jnp.int32)
    lat_gap = where[:, 0:1] - obs[0][0]
    lon_gap = lon_distance(where[:, 1:2], obs[0][1])
    distance = (square(lat_gap) + square(lon_gap)).astype(jnp.float32)
    taper = square(jnp.maximum(1.0 - distance / square(obs[0][2]).astype(jnp.float32), 0.0))
    covariance = matmul_exact(centred(priors[1]), anomaly[0], (1, 1)) / (members - 1)
    priors[1] += matmul_exact(taper * covariance, weights[0])
    anomaly.append(centred(priors[1]))
    carried = halves_of(matmul_exact(centred(weights[0]), anomaly[1], (1, 1)) / (members - 1))

    both = [jnp.transpose(part) for part in halves_of(jnp.concatenate(anomaly, axis=0) / (members - 1))]
    cell_lon = first_col + lax.broadcasted_iota(jnp.int32, (cols, 1), 0)
    lon_part = [scaled_square(lon_distance(cell_lon, lon), radius) for _, lon, radius in obs]
    chunk = 4
    fetch.wait()

    def taper_of(batch, row):
        lat, _, radius = obs[batch]
        room = 1.0 - scaled_square(first_row + row - lat, radius)
        return square(jnp.maximum(room - lon_part[batch], 0.0))

    def spread_chunk(index, carry):
        cells = field[pl.ds(index * chunk, chunk)].reshape(chunk * cols, members)
        covariance = matmul_halves(halves_of(cells), both)
        tapers = [
            jnp.concatenate([taper_of(batch, index * chunk + r) for r in range(chunk)], axis=0)
            for batch in range(BATCHES)
        ]
        first = tapers[0] * covariance[:, :nobs]
        second = tapers[1] * (covariance[:, nobs:] + matmul_halves(halves_of(first), carried))
        at = pl.ds(pl.multiple_of(index * chunk * cols, chunk * cols), chunk * cols)
        for i, part in enumerate(halves_of(jnp.concatenate([first, second], axis=1))):
            spread[i, at] = part
        return carry

    lax.fori_loop(0, rows // chunk, spread_chunk, 0)

    weights.append(weights_of(1, priors[1], anomaly[1]))
    both_weights = halves_of(jnp.concatenate(weights, axis=0))

    def copy_out(index):
        at = pl.ds(index * chunk, chunk)
        return pltpu.make_async_copy(analysis.at[at], out_ref.at[at], out_sem.at[index])

    def update_chunk(index, carry):
        at = pl.ds(pl.multiple_of(index * chunk * cols, chunk * cols), chunk * cols)
        change = matmul_halves((spread[0, at], spread[1, at]), both_weights)
        at = pl.ds(index * chunk, chunk)
        analysis[at] = (field[at] + change.reshape(chunk, cols, members)).astype(jnp.bfloat16)
        copy_out(index).start()
        return carry

    lax.fori_loop(0, rows // chunk, update_chunk, 0)
    for index in range(rows // chunk):
        copy_out(index).wait()


def analyse(priors, field, where, value, variance, noise, lon_count, lat_count):
    rows, cols, members = field.shape
    nobs = where.shape[2]
    vmem, anywhere = pl.BlockSpec(memory_space=pltpu.VMEM), pl.BlockSpec(memory_space=pl.ANY)
    return pl.pallas_call(
        functools.partial(analysis_kernel, (lon_count, lat_count)),
        out_shape=jax.ShapeDtypeStruct((rows, cols, members), jnp.bfloat16),
        in_specs=[vmem, anywhere, vmem, vmem, vmem, vmem],
        out_specs=anywhere,
        scratch_shapes=[
            pltpu.VMEM((rows, cols, members), jnp.float32),
            pltpu.VMEM((2, rows * cols, BATCHES * nobs), jnp.bfloat16),
            pltpu.VMEM((rows, cols, members), jnp.bfloat16),
            pltpu.SemaphoreType.DMA,
            pltpu.SemaphoreType.DMA((rows // 4,)),
        ],
        compiler_params=pltpu.CompilerParams(vmem_limit_bytes=32 * 1024 * 1024),
        name="analyse",
    )(priors, field, where, value, variance, noise)


def body(ensemble_state, courant, obs_where, obs_value, obs_variance, obs_noise):
    counts = lax.axis_size("lon"), lax.axis_size("lat")
    where = jnp.transpose(obs_where, (1, 0, 2))
    priors, field = gather(ensemble_state, courant, where, *counts)
    return analyse(priors, field, where, obs_value, obs_variance, obs_noise, *counts)


def solution(mesh):
    placed = (P("lat", "lon", None), P(None, "lat", "lon"), P(), P(), P(), P())
    return jax.shard_map(
        body, mesh=mesh, in_specs=placed, out_specs=P("lat", "lon", None), check_vma=False
    )
```

```python
import functools
import jax
import jax.numpy as jnp
from jax import lax
from jax.experimental import pallas as pl
from jax.experimental.pallas import tpu as pltpu
from jax.sharding import PartitionSpec as P

BATCHES = 2
MESH = pl.DeviceIdType.MESH
VMEM_BYTES = 63 * 1024 * 1024
LANES = 128
HIGHEST = lax.Precision.HIGHEST
ONE_STEP = ((0, 0), (-1, 0), (1, 0), (0, -1), (0, 1))
TWO_STEPS = tuple(sorted({(a + c, b + d) for a, b in ONE_STEP for c, d in ONE_STEP}))


def split_mesh(lon_count, lat_count):
    plane_lat = 8 if lat_count == 16 else lat_count // 2
    line_lon = 8 if lon_count == 32 else lon_count // 2
    return lon_count // line_lon, line_lon, lat_count // plane_lat, plane_lat


def shifted(field, rows, lanes):
    if rows:
        field = pltpu.roll(field, rows % field.shape[0], 0)
    if lanes:
        field = pltpu.roll(field, lanes % field.shape[1], 1)
    return field


def link_weights(speed_lat, speed_lon, row, total_rows):
    inside = (row >= 0) & (row < total_rows)
    lat_plus = jnp.maximum(speed_lat, 0.0)
    lat_minus = jnp.minimum(speed_lat, 0.0)
    lon_plus = jnp.maximum(speed_lon, 0.0)
    lon_minus = jnp.minimum(speed_lon, 0.0)
    zero = jnp.zeros_like(speed_lat)
    return {
        (0, 0): jnp.where(inside, 1.0 - lat_plus + lat_minus - lon_plus + lon_minus, zero),
        (-1, 0): jnp.where(inside & (row > 0), lat_plus, zero),
        (1, 0): jnp.where(inside & (row < total_rows - 1), -lat_minus, zero),
        (0, -1): jnp.where(inside, lon_plus, zero),
        (0, 1): jnp.where(inside, -lon_minus, zero),
    }


def ring_flips(count):
    flips = [lambda place: place]
    size = 1
    while size < count:
        flips += [lambda place, size=size, f=f: flip_bit(f(place), size) for f in flips]
        size *= 2
    return flips


def flip_bit(place, size):
    return place + size - 2 * size * (place // size % 2)


def window_kernel(
    sizes, state_hbm, courant_hbm, where_hbm, value_hbm, variance_hbm, noise_hbm, out_ref,
    state_ref, courant_ref, where_ref, value_ref, variance_ref, noise_ref,
    near_ns, near_ew, near_corner, reach, wide, stencil, weights, part, pieces, piece, line, priors,
    cells, bands, far_ns, far_ew, far_corner, field, spread, analysis,
    in_sem, near_sem, far_sem, part_sem, line_sem, all_sem, send_sem, out_sem,
):
    lon_count, lat_count = sizes
    plane_lon, line_lon, line_lat, plane_lat = split_mesh(lon_count, lat_count)
    plane, lines = plane_lon * plane_lat, line_lat * line_lon
    rows, cols, members = state_ref.shape
    total_rows, total_cols = rows * lat_count, cols * lon_count
    nobs = where_ref.shape[2]
    halves = members // LANES
    band = nobs * halves // plane
    lon, lat = lax.axis_index("lon"), lax.axis_index("lat")
    line_me = (lat // plane_lat) * line_lon + lon % line_lon
    arguments = (
        (courant_hbm, courant_ref), (state_hbm, state_ref), (where_hbm, where_ref),
        (value_hbm, value_ref), (variance_hbm, variance_ref), (noise_hbm, noise_ref),
    )
    loads = [pltpu.make_async_copy(*pair, in_sem.at[index]) for index, pair in enumerate(arguments)]
    for load in loads:
        load.start()

    lon_flips, lat_flips = ring_flips(plane_lon), ring_flips(plane_lat)
    plane_x = [flip(lon // line_lon) for flip in lon_flips]
    plane_y = [flip(lat % plane_lat) for flip in lat_flips]
    partners = [(i, j) for i in range(plane_lon) for j in range(plane_lat)][1:]
    hops = {0: 0, 1: 1, 2: 2, 3: 1}
    partners.sort(key=lambda p: -hops[p[0] % 4] - hops[p[1] // 2 % 4])
    distances = sorted(range(1, lines), key=lambda d: -min(d, lines - d))

    def plane_device(partner):
        return {
            "lon": plane_x[partner[0]] * line_lon + lon % line_lon,
            "lat": lat // plane_lat * plane_lat + plane_y[partner[1]],
        }

    def tile_of(partner):
        index = plane_x[partner[0]] * plane_lat + plane_y[partner[1]]
        return (
            pl.ds(pl.multiple_of(index // halves * band, band), band),
            pl.ds(pl.multiple_of(index % halves * LANES, LANES), LANES),
        )

    def line_device(distance):
        index = lax.rem(line_me + distance, lines)
        return {
            "lon": lon // line_lon * line_lon + index % line_lon,
            "lat": index // line_lon * plane_lat + lat % plane_lat,
        }

    def neighbour(lat_step, lon_step):
        return {
            "lon": lax.rem(lon + lon_step + lon_count, lon_count),
            "lat": lax.rem(lat + lat_step + lat_count, lat_count),
        }

    around = [(a, b) for a in (-1, 1) for b in (0, -1, 1)] + [(0, -1), (0, 1)]

    barrier = pltpu.get_barrier_semaphore()
    greeted = [neighbour(*step) for step in around]
    greeted += [line_device(distance) for distance in distances]
    greeted += [plane_device(partner) for partner in partners]
    for target in greeted:
        pl.semaphore_signal(barrier, inc=1, device_id=target, device_id_type=MESH)

    for load in loads:
        load.wait()
    edges, ends = ((0, 2), (rows - 2, rows)), ((0, 2), (cols - 2, cols))
    for side in range(2):
        low, high = edges[side]
        far_ns[side] = state_ref[low:high].astype(jnp.float32)
        low, high = ends[side]
        far_ew[side] = state_ref[:, low:high].astype(jnp.float32)
        for other in range(2):
            row, first = (0, rows - 1)[side], (0, cols - 8)[other]
            far_corner[2 * side + other] = state_ref[row, first : first + 8].astype(jnp.float32)
    cells[...] = jnp.zeros(cells.shape, jnp.bfloat16)
    cells[2 : 2 + rows, :cols] = state_ref[...]
    pl.semaphore_wait(barrier, len(greeted))

    def send(src, dst, sem, step):
        copy = pltpu.make_async_remote_copy(
            src_ref=src, dst_ref=dst, send_sem=sem.at[0], recv_sem=sem.at[1],
            device_id=neighbour(*step), device_id_type=MESH,
        )
        copy.start()
        return copy

    low, high = pl.ds(0, 8), pl.ds(rows - 8, 8)
    near = []
    for index, (a, b) in enumerate(around):
        source = courant_ref.at[:, {-1: low, 1: high}[a], :] if a else courant_ref
        if a and b:
            target = near_corner.at[(0 if a > 0 else 2) + (0 if b > 0 else 1)]
        elif a:
            target = near_ns.at[0 if a > 0 else 1]
        else:
            target = near_ew.at[0 if b > 0 else 1]
        near.append(send(source, target, near_sem.at[index], (a, b)))

    far = []
    for index, (a, b) in enumerate(around):
        up, right = int(a > 0), int(b > 0)
        if a and b:
            source, target = far_corner.at[2 * up + right], far_corner.at[4 + 2 * (1 - up) + (1 - right)]
        elif a:
            source, target = far_ns.at[up], far_ns.at[2 + 1 - up]
        else:
            source, target = far_ew.at[right], far_ew.at[2 + 1 - right]
        far.append(send(source, target, far_sem.at[index], (a, b)))
    for copy in near:
        copy.wait_recv()

    lane = lax.broadcasted_iota(jnp.int32, (8, LANES), 1)

    def assemble(own, west, east):
        blank = jnp.zeros((8, LANES - cols), jnp.float32)
        own = jnp.concatenate([own, blank], axis=1)
        west = jnp.concatenate([blank, west], axis=1)
        east = jnp.concatenate([blank, east], axis=1)
        return jnp.where(lane < cols, own, jnp.where(lane < cols + 2, east, west))

    for c in range(2):
        reach[c, 0:8] = assemble(near_ns[0, c], near_corner[0, c], near_corner[1, c])
        for r in range(0, rows, 8):
            band_rows = pl.ds(r, 8)
            reach[c, r + 8 : r + 16] = assemble(
                courant_ref[c, band_rows], near_ew[0, c, band_rows], near_ew[1, c, band_rows]
            )
        reach[c, rows + 8 : rows + 16] = assemble(near_ns[1, c], near_corner[2, c], near_corner[3, c])

    row = lax.broadcasted_iota(jnp.int32, (rows + 16, LANES), 0) - 8 + lat * rows
    weight = link_weights(reach[0], reach[1], row, total_rows)

    arrived = {step: shifted(weight[step], *step) for step in ONE_STEP}
    sums = {}
    for first in ONE_STEP:
        for second in ONE_STEP:
            total = (first[0] + second[0], first[1] + second[1])
            term = shifted(arrived[first] * weight[second], *second)
            sums[total] = sums[total] + term if total in sums else term
    half = lax.broadcasted_iota(jnp.int32, (rows // 2, LANES), 1) < cols
    for index, total in enumerate(TWO_STEPS):
        wide[index] = sums[total]
        even = wide[index, pl.ds(8, rows // 2, 2), :]
        odd = wide[index, pl.ds(9, rows // 2, 2), :]
        stencil[index] = jnp.where(half, even, pltpu.roll(odd, cols, 1))

    def halves_into(ref, at, columns, value):
        upper = value.astype(jnp.bfloat16)
        count = value.shape[0]
        ref[at : at + count, columns] = upper
        ref[at + count : at + 2 * count, columns] = (value - upper.astype(jnp.float32)).astype(jnp.bfloat16)

    flat_lane = lax.broadcasted_iota(jnp.int32, (nobs, LANES), 1)
    second_row = jnp.where(flat_lane >= cols, 1, 0)
    column = flat_lane - second_row * cols
    flat_state = state_ref[...].reshape(rows * cols, members)
    for batch in range(BATCHES):
        where = jnp.concatenate([where_ref[i, batch : batch + 1] for i in range(3)], axis=0)
        where = jnp.concatenate([where, jnp.zeros((8 - 3, nobs), jnp.int32)], axis=0)
        where = jnp.transpose(where.astype(jnp.float32)).astype(jnp.int32)
        obs_row = where[:, 0:1] - lat * rows
        obs_col = where[:, 1:2] - lon * cols + 2
        obs_col = jnp.where(obs_col < 0, obs_col + total_cols, obs_col) - 2
        obs_col = jnp.where(obs_col >= total_cols - 2, obs_col - total_cols, obs_col)
        lon_step = column - obs_col
        lat_base = second_row - obs_row

        def one_pair(pair, carry):
            lat_step = lat_base + 2 * pair
            total = jnp.zeros((nobs, LANES), jnp.float32)
            for index, (a, b) in enumerate(TWO_STEPS):
                total = jnp.where((lat_step == a) & (lon_step == b), stencil[index, pl.ds(pair, 1), :], total)
            halves_into(weights, 0, pl.ds(pl.multiple_of(pair * LANES, LANES), LANES), total)
            return carry

        lax.fori_loop(0, rows // 2, one_pair, 0)
        share = jnp.dot(weights[...], flat_state, preferred_element_type=jnp.float32)
        part[batch] = share[:nobs] + share[nobs:]
        for index, partner in enumerate(partners):
            pltpu.make_async_remote_copy(
                src_ref=part.at[batch, *tile_of(partner)], dst_ref=pieces.at[batch, index],
                send_sem=send_sem.at[batch, 0], recv_sem=part_sem.at[batch],
                device_id=plane_device(partner), device_id_type=MESH,
            ).start()

    mine = tile_of((0, 0))
    for batch in range(BATCHES):
        pltpu.make_async_copy(pieces.at[batch], pieces.at[batch], part_sem.at[batch]).wait()
        piece[batch] = part[batch, *mine] + jnp.sum(pieces[batch], axis=0)
        for index, distance in enumerate(distances):
            pltpu.make_async_remote_copy(
                src_ref=piece.at[batch], dst_ref=line.at[batch, index],
                send_sem=send_sem.at[batch, 1], recv_sem=line_sem.at[batch],
                device_id=line_device(distance), device_id_type=MESH,
            ).start()

    for copy in far:
        copy.wait_recv()
    gap = jnp.zeros((14, members), jnp.float32)

    def beside(at, west, east):
        cells[at, cols : cols + 16] = jnp.concatenate([east, gap], axis=0).astype(jnp.bfloat16)
        cells[at, LANES - 16 :] = jnp.concatenate([gap, west], axis=0).astype(jnp.bfloat16)

    def beside_row(r, carry):
        beside(r + 2, far_ew[2, r], far_ew[3, r])
        return carry

    lax.fori_loop(0, rows, beside_row, 0)
    for side, at in ((0, 1), (1, rows + 2)):
        cells[(0, rows + 2)[side] : (2, rows + 4)[side], :cols] = far_ns[2 + side].astype(jnp.bfloat16)
        beside(at, far_corner[4 + 2 * side, 6:8], far_corner[4 + 2 * side + 1, 0:2])
    step_lane = lax.broadcasted_iota(jnp.int32, (cols, LANES), 1) - lax.broadcasted_iota(jnp.int32, (cols, LANES), 0)
    step_lane = jnp.where(step_lane > LANES // 2 + 2, step_lane - LANES, step_lane)

    def one_pair_of_rows(pair, carry):
        first = 2 * pair
        for around_row in range(6):
            for r in range(2):
                a = around_row - 2 - r
                total = jnp.zeros((cols, LANES), jnp.float32)
                if -2 <= a <= 2:
                    for index, (lat_step, b) in enumerate(TWO_STEPS):
                        if lat_step == a:
                            total = jnp.where(step_lane == b, wide[index, pl.ds(first + around_row + 6, 1), :], total)
                halves_into(bands, 2 * r * cols, pl.ds(around_row * LANES, LANES), total)
        near_cells = cells[pl.ds(first, 6)].reshape(6 * LANES, members)
        result = jnp.dot(bands[...], near_cells, preferred_element_type=jnp.float32)
        for r in range(2):
            field[first + r] = result[2 * r * cols : (2 * r + 1) * cols] + result[(2 * r + 1) * cols : (2 * r + 2) * cols]
        return carry

    lax.fori_loop(0, rows // 2, one_pair_of_rows, 0)

    for batch in range(BATCHES):
        pltpu.make_async_copy(line.at[batch], line.at[batch], line_sem.at[batch]).wait()
        priors[batch, *mine] = piece[batch] + jnp.sum(line[batch], axis=0)
        for partner in partners:
            pltpu.make_async_remote_copy(
                src_ref=priors.at[batch, *mine], dst_ref=priors.at[batch, *mine],
                send_sem=send_sem.at[batch, 2], recv_sem=all_sem.at[batch],
                device_id=plane_device(partner), device_id_type=MESH,
            ).start()
    def arrival(batch):
        pltpu.make_async_copy(pieces.at[batch], pieces.at[batch], all_sem.at[batch]).wait()
        return priors[batch]

    analyse(
        sizes, arrival, where_ref, value_ref, variance_ref, noise_ref, out_ref, field, spread, analysis, out_sem
    )

    for copy in near + far:
        copy.wait_send()
    for batch in range(BATCHES):
        for sem, sent in enumerate((pieces, line, pieces)):
            pltpu.make_async_copy(sent.at[batch], sent.at[batch], send_sem.at[batch, sem]).wait()


def matmul_exact(left, right, contract=(1, 0)):
    return lax.dot_general(
        left, right, (((contract[0],), (contract[1],)), ((), ())),
        precision=HIGHEST, preferred_element_type=jnp.float32,
    )


def halves_of(value):
    upper = value.astype(jnp.bfloat16)
    return upper, (value - upper.astype(jnp.float32)).astype(jnp.bfloat16)


def matmul_halves(left, right):
    total = jnp.dot(left[0], right[1], preferred_element_type=jnp.float32)
    total += jnp.dot(left[1], right[0], preferred_element_type=jnp.float32)
    return total + jnp.dot(left[0], right[0], preferred_element_type=jnp.float32)


def solve_pivot(pivot, rows):
    count = len(rows)
    pivot, rows, factor, inverse = dict(pivot), list(rows), {}, {}
    for j in range(0, count, 2):
        a, b, c = pivot[j, j], pivot[j + 1, j], pivot[j + 1, j + 1]
        scale = 1.0 / (a * c - b * b)
        inverse[j] = first, cross, last = c * scale, -b * scale, a * scale
        for i in range(j + 2, count):
            factor[i, j] = pivot[i, j] * first + pivot[i, j + 1] * cross
            factor[i, j + 1] = pivot[i, j] * cross + pivot[i, j + 1] * last
        for i in range(j + 2, count):
            for k in range(j + 2, i + 1):
                pivot[i, k] -= factor[i, j] * pivot[k, j] + factor[i, j + 1] * pivot[k, j + 1]
    for j in range(0, count, 2):
        for i in range(j + 2, count):
            rows[i] -= factor[i, j] * rows[j] + factor[i, j + 1] * rows[j + 1]
    for j in range(0, count, 2):
        first, cross, last = inverse[j]
        rows[j], rows[j + 1] = first * rows[j] + cross * rows[j + 1], cross * rows[j] + last * rows[j + 1]
    for i in reversed(range(0, count, 2)):
        for j in range(i):
            rows[j] -= factor[i, j] * rows[i] + factor[i + 1, j] * rows[i + 1]
    return rows


def tree_sum(terms):
    while len(terms) > 1:
        terms = [a + b for a, b in zip(terms[::2], terms[1::2])] + terms[len(terms) // 2 * 2 :]
    return terms[0]


def inverse_of(system, panel=32):
    size = system.shape[0]
    spread = (8, size)
    lane = lax.broadcasted_iota(jnp.int32, spread, 1)
    sub = lax.broadcasted_iota(jnp.int32, spread, 0)
    panel_lane = lax.broadcasted_iota(jnp.int32, (panel, size), 1)
    panel_sub = lax.broadcasted_iota(jnp.int32, (panel, size), 0)
    whole_lane = lax.broadcasted_iota(jnp.int32, (size, size), 1)
    for start in range(0, size, panel):
        old = system[start : start + panel]
        bands = [old[i : i + 8] for i in range(0, panel, 8)]
        for here in range(panel // 8):
            first = start + 8 * here
            inside = (lane >= first) & (lane < first + 8)
            columns = [
                [jnp.broadcast_to(band[:, first + j : first + j + 1], spread) for j in range(8)] for band in bands
            ]
            pivot = {
                (i, j): jnp.broadcast_to(columns[here][j][i : i + 1], spread) for i in range(8) for j in range(i + 1)
            }
            rows = [
                jnp.where(inside, jnp.where(lane == first + j, -1.0, 0.0), jnp.broadcast_to(bands[here][j : j + 1], spread))
                for j in range(8)
            ]
            rows = solve_pivot(pivot, rows)
            for i, band in enumerate(bands):
                if i != here:
                    terms = [columns[i][j] * rows[j] for j in range(8)]
                    bands[i] = jnp.where(inside, 0.0, band) - tree_sum(terms)
            swept = rows[7]
            for j in range(7):
                swept = jnp.where(sub == j, rows[j], swept)
            bands[here] = swept
        swept = jnp.concatenate(bands, axis=0)
        inside = (panel_lane >= start) & (panel_lane < start + panel)
        old = jnp.where(inside, jnp.where(panel_lane == panel_sub + start, -1.0, 0.0), old)
        inside = (whole_lane >= start) & (whole_lane < start + panel)
        system = jnp.where(inside, 0.0, system) - matmul_exact(old, swept, (0, 0))
        parts = [system[:start], swept, system[start + panel :]]
        system = jnp.concatenate([part for part in parts if part.shape[0]], axis=0)
    return -system


def square(value):
    return value * value


def analyse(
    sizes, arrival, where_ref, value_ref, variance_ref, noise_ref, out_ref, field, spread, analysis, out_sem
):
    lon_count, lat_count = sizes
    rows, cols, members = field.shape
    nobs = where_ref.shape[2]
    total_cols = cols * lon_count
    first_row, first_col = lax.axis_index("lat") * rows, lax.axis_index("lon") * cols

    blank = jnp.zeros((8 - 2 * BATCHES, nobs), jnp.float32)
    upright = jnp.transpose(jnp.concatenate([value_ref[...], variance_ref[...], blank], axis=0))
    eye = lax.broadcasted_iota(jnp.int32, (nobs, nobs), 0) == lax.broadcasted_iota(jnp.int32, (nobs, nobs), 1)

    def lon_distance(cell, obs):
        gap = jnp.abs(cell - obs)
        return jnp.minimum(gap, total_cols - gap)

    def scaled_square(gap, radius):
        return square(gap).astype(jnp.float32) / square(radius).astype(jnp.float32)

    def weights_of(batch, priors, anomaly):
        variance = upright[:, BATCHES + batch : BATCHES + batch + 1]
        system = matmul_exact(anomaly, anomaly, (1, 1)) / (members - 1)
        system += jnp.where(eye, variance, 0.0)
        misfit = upright[:, batch : batch + 1] + jnp.sqrt(variance) * noise_ref[batch] - priors
        return matmul_exact(inverse_of(system), misfit)

    def centred(priors):
        return priors - jnp.mean(priors, axis=1, keepdims=True)

    obs = [[where_ref[i, batch : batch + 1, :] for i in range(3)] for batch in range(BATCHES)]
    priors = [arrival(0)]
    anomaly, weights = [centred(priors[0])], []
    weights.append(weights_of(0, priors[0], anomaly[0]))

    where = jnp.concatenate(obs[1] + [jnp.zeros((8 - 3, nobs), jnp.int32)], axis=0)
    where = jnp.transpose(where.astype(jnp.float32)).astype(jnp.int32)
    lat_gap = where[:, 0:1] - obs[0][0]
    lon_gap = lon_distance(where[:, 1:2], obs[0][1])
    distance = (square(lat_gap) + square(lon_gap)).astype(jnp.float32)
    taper = square(jnp.maximum(1.0 - distance / square(obs[0][2]).astype(jnp.float32), 0.0))
    before = arrival(1)
    covariance = matmul_exact(centred(before), anomaly[0], (1, 1)) / (members - 1)
    priors.append(before + matmul_exact(taper * covariance, weights[0]))
    anomaly.append(centred(priors[1]))
    carried = halves_of(matmul_exact(centred(weights[0]), anomaly[1], (1, 1)) / (members - 1))

    both = [jnp.transpose(part) for part in halves_of(jnp.concatenate(anomaly, axis=0) / (members - 1))]
    cell_lon = first_col + lax.broadcasted_iota(jnp.int32, (cols, 1), 0)
    lon_part = [scaled_square(lon_distance(cell_lon, lon), radius) for _, lon, radius in obs]
    chunk = 4

    def taper_of(batch, row):
        lat, _, radius = obs[batch]
        room = 1.0 - scaled_square(first_row + row - lat, radius)
        return square(jnp.maximum(room - lon_part[batch], 0.0))

    def spread_chunk(index, carry):
        cells = field[pl.ds(index * chunk, chunk)].reshape(chunk * cols, members)
        covariance = matmul_halves(halves_of(cells), both)
        tapers = [
            jnp.concatenate([taper_of(batch, index * chunk + r) for r in range(chunk)], axis=0)
            for batch in range(BATCHES)
        ]
        first = tapers[0] * covariance[:, :nobs]
        second = tapers[1] * (covariance[:, nobs:] + matmul_halves(halves_of(first), carried))
        at = pl.ds(pl.multiple_of(index * chunk * cols, chunk * cols), chunk * cols)
        for i, part in enumerate(halves_of(jnp.concatenate([first, second], axis=1))):
            spread[i, at] = part
        return carry

    lax.fori_loop(0, rows // chunk, spread_chunk, 0)

    weights.append(weights_of(1, priors[1], anomaly[1]))
    both_weights = halves_of(jnp.concatenate(weights, axis=0))

    def copy_out(index):
        at = pl.ds(index * chunk, chunk)
        return pltpu.make_async_copy(analysis.at[at], out_ref.at[at], out_sem.at[index])

    def update_chunk(index, carry):
        at = pl.ds(pl.multiple_of(index * chunk * cols, chunk * cols), chunk * cols)
        change = matmul_halves((spread[0, at], spread[1, at]), both_weights)
        at = pl.ds(index * chunk, chunk)
        analysis[at] = (field[at] + change.reshape(chunk, cols, members)).astype(jnp.bfloat16)
        copy_out(index).start()
        return carry

    lax.fori_loop(0, rows // chunk, update_chunk, 0)
    for index in range(rows // chunk):
        copy_out(index).wait()


def window(state, courant, where, value, variance, noise, lon_count, lat_count):
    rows, cols, members = state.shape
    nobs = where.shape[2]
    plane_lon, line_lon, line_lat, plane_lat = split_mesh(lon_count, lat_count)
    plane, lines = plane_lon * plane_lat, line_lat * line_lon
    band = nobs * (members // LANES) // plane
    f32, bf16 = jnp.float32, jnp.bfloat16
    anywhere = pl.BlockSpec(memory_space=pl.ANY)
    dma = pltpu.SemaphoreType.DMA
    arguments = (state, courant, where, value, variance, noise)
    return pl.pallas_call(
        functools.partial(window_kernel, (lon_count, lat_count)),
        out_shape=jax.ShapeDtypeStruct((rows, cols, members), bf16),
        in_specs=[anywhere] * len(arguments),
        out_specs=anywhere,
        scratch_shapes=[pltpu.VMEM(argument.shape, argument.dtype) for argument in arguments]
        + [
            pltpu.VMEM((2, 2, 8, cols), f32),
            pltpu.VMEM((2, 2, rows, cols), f32),
            pltpu.VMEM((4, 2, 8, cols), f32),
            pltpu.VMEM((2, rows + 16, LANES), f32),
            pltpu.VMEM((len(TWO_STEPS), rows + 16, LANES), f32),
            pltpu.VMEM((len(TWO_STEPS), rows // 2, LANES), f32),
            pltpu.VMEM((2 * nobs, rows * cols), bf16),
            pltpu.VMEM((BATCHES, nobs, members), f32),
            pltpu.VMEM((BATCHES, plane - 1, band, LANES), f32),
            pltpu.VMEM((BATCHES, band, LANES), f32),
            pltpu.VMEM((BATCHES, lines - 1, band, LANES), f32),
            pltpu.VMEM((BATCHES, nobs, members), f32),
            pltpu.VMEM((rows + 4, LANES, members), bf16),
            pltpu.VMEM((4 * cols, 6 * LANES), bf16),
            pltpu.VMEM((4, 2, cols, members), f32),
            pltpu.VMEM((4, rows, 2, members), f32),
            pltpu.VMEM((8, 8, members), f32),
            pltpu.VMEM((rows, cols, members), f32),
            pltpu.VMEM((2, rows * cols, BATCHES * nobs), bf16),
            pltpu.VMEM((rows, cols, members), bf16),
            dma((len(arguments),)),
            dma((8, 2)),
            dma((8, 2)),
            dma((BATCHES,)),
            dma((BATCHES,)),
            dma((BATCHES,)),
            dma((BATCHES, 3)),
            dma((rows // 4,)),
        ],
        compiler_params=pltpu.CompilerParams(
            collective_id=0, has_side_effects=True, vmem_limit_bytes=VMEM_BYTES
        ),
        name="window",
    )(*arguments)


def body(ensemble_state, courant, obs_where, obs_value, obs_variance, obs_noise):
    counts = lax.axis_size("lon"), lax.axis_size("lat")
    where = jnp.transpose(obs_where, (1, 0, 2))
    return window(ensemble_state, courant, where, obs_value, obs_variance, obs_noise, *counts)


def solution(mesh):
    placed = (P("lat", "lon", None), P(None, "lat", "lon"), P(), P(), P(), P())
    return jax.shard_map(
        body, mesh=mesh, in_specs=placed, out_specs=P("lat", "lon", None), check_vma=False
    )
```

```python
import functools
import jax
import jax.numpy as jnp
from jax import lax
from jax.experimental import pallas as pl
from jax.experimental.pallas import tpu as pltpu
from jax.sharding import PartitionSpec as P

BATCHES = 2
MESH = pl.DeviceIdType.MESH
UNITS = 16
BLOCK = 8
VMEM_BYTES = 63 * 1024 * 1024
LANES = 128
HIGHEST = lax.Precision.HIGHEST
ONE_STEP = ((0, 0), (-1, 0), (1, 0), (0, -1), (0, 1))
TWO_STEPS = tuple(sorted({(a + c, b + d) for a, b in ONE_STEP for c, d in ONE_STEP}))


def split_mesh(lon_count, lat_count):
    plane_lat = 8 if lat_count == 16 else lat_count // 2
    line_lon = 8 if lon_count == 32 else lon_count // 2
    return lon_count // line_lon, line_lon, lat_count // plane_lat, plane_lat


def shifted(field, rows, lanes):
    if rows:
        field = pltpu.roll(field, rows % field.shape[0], 0)
    if lanes:
        field = pltpu.roll(field, lanes % field.shape[1], 1)
    return field


def link_weights(speed_lat, speed_lon, row, total_rows):
    inside = (row >= 0) & (row < total_rows)
    lat_plus = jnp.maximum(speed_lat, 0.0)
    lat_minus = jnp.minimum(speed_lat, 0.0)
    lon_plus = jnp.maximum(speed_lon, 0.0)
    lon_minus = jnp.minimum(speed_lon, 0.0)
    zero = jnp.zeros_like(speed_lat)
    return {
        (0, 0): jnp.where(inside, 1.0 - lat_plus + lat_minus - lon_plus + lon_minus, zero),
        (-1, 0): jnp.where(inside & (row > 0), lat_plus, zero),
        (1, 0): jnp.where(inside & (row < total_rows - 1), -lat_minus, zero),
        (0, -1): jnp.where(inside, lon_plus, zero),
        (0, 1): jnp.where(inside, -lon_minus, zero),
    }


def ring_flips(count):
    flips = [lambda place: place]
    size = 1
    while size < count:
        flips += [lambda place, size=size, f=f: flip_bit(f(place), size) for f in flips]
        size *= 2
    return flips


def flip_bit(place, size):
    return place + size - 2 * size * (place // size % 2)


def window_kernel(
    sizes, state_hbm, courant_hbm, where_hbm, value_hbm, variance_hbm, noise_hbm,
    field_out, spread_out, change_ref,
    state_ref, courant_ref, where_ref, value_ref, variance_ref, noise_ref,
    near_ns, near_ew, near_corner, reach, wide, stencil, weights, part, pieces, piece, line, priors,
    cells, bands, far_ns, far_ew, far_corner, field, split, spread,
    in_sem, near_sem, far_sem, part_sem, line_sem, all_sem, send_sem, out_sem,
):
    lon_count, lat_count = sizes
    plane_lon, line_lon, line_lat, plane_lat = split_mesh(lon_count, lat_count)
    plane, lines = plane_lon * plane_lat, line_lat * line_lon
    rows, cols, members = state_ref.shape
    total_rows, total_cols = rows * lat_count, cols * lon_count
    nobs = where_ref.shape[2]
    halves = members // LANES
    band = nobs * halves // plane
    lon, lat = lax.axis_index("lon"), lax.axis_index("lat")
    line_me = (lat // plane_lat) * line_lon + lon % line_lon
    arguments = (
        (courant_hbm, courant_ref), (state_hbm, state_ref), (where_hbm, where_ref),
        (value_hbm, value_ref), (variance_hbm, variance_ref), (noise_hbm, noise_ref),
    )
    loads = [pltpu.make_async_copy(*pair, in_sem.at[index]) for index, pair in enumerate(arguments)]
    for load in loads:
        load.start()

    lon_flips, lat_flips = ring_flips(plane_lon), ring_flips(plane_lat)
    plane_x = [flip(lon // line_lon) for flip in lon_flips]
    plane_y = [flip(lat % plane_lat) for flip in lat_flips]
    partners = [(i, j) for i in range(plane_lon) for j in range(plane_lat)][1:]
    hops = {0: 0, 1: 1, 2: 2, 3: 1}
    partners.sort(key=lambda p: -hops[p[0] % 4] - hops[p[1] // 2 % 4])
    distances = sorted(range(1, lines), key=lambda d: -min(d, lines - d))

    def plane_device(partner):
        return {
            "lon": plane_x[partner[0]] * line_lon + lon % line_lon,
            "lat": lat // plane_lat * plane_lat + plane_y[partner[1]],
        }

    def tile_of(partner):
        index = plane_x[partner[0]] * plane_lat + plane_y[partner[1]]
        return (
            pl.ds(pl.multiple_of(index // halves * band, band), band),
            pl.ds(pl.multiple_of(index % halves * LANES, LANES), LANES),
        )

    def line_device(distance):
        index = lax.rem(line_me + distance, lines)
        return {
            "lon": lon // line_lon * line_lon + index % line_lon,
            "lat": index // line_lon * plane_lat + lat % plane_lat,
        }

    def neighbour(lat_step, lon_step):
        return {
            "lon": lax.rem(lon + lon_step + lon_count, lon_count),
            "lat": lax.rem(lat + lat_step + lat_count, lat_count),
        }

    around = [(a, b) for a in (-1, 1) for b in (0, -1, 1)] + [(0, -1), (0, 1)]

    barrier = pltpu.get_barrier_semaphore()
    greeted = [neighbour(*step) for step in around]
    greeted += [line_device(distance) for distance in distances]
    greeted += [plane_device(partner) for partner in partners]
    for target in greeted:
        pl.semaphore_signal(barrier, inc=1, device_id=target, device_id_type=MESH)

    for load in loads:
        load.wait()
    edges, ends = ((0, 2), (rows - 2, rows)), ((0, 2), (cols - 2, cols))
    for side in range(2):
        low, high = edges[side]
        far_ns[side] = state_ref[low:high].astype(jnp.float32)
        low, high = ends[side]
        far_ew[side] = state_ref[:, low:high].astype(jnp.float32)
        for other in range(2):
            row, first = (0, rows - 1)[side], (0, cols - 8)[other]
            far_corner[2 * side + other] = state_ref[row, first : first + 8].astype(jnp.float32)
    cells[...] = jnp.zeros(cells.shape, jnp.bfloat16)
    cells[2 : 2 + rows, :cols] = state_ref[...]
    pl.semaphore_wait(barrier, len(greeted))

    def send(src, dst, sem, step):
        copy = pltpu.make_async_remote_copy(
            src_ref=src, dst_ref=dst, send_sem=sem.at[0], recv_sem=sem.at[1],
            device_id=neighbour(*step), device_id_type=MESH,
        )
        copy.start()
        return copy

    low, high = pl.ds(0, 8), pl.ds(rows - 8, 8)
    near = []
    for index, (a, b) in enumerate(around):
        source = courant_ref.at[:, {-1: low, 1: high}[a], :] if a else courant_ref
        if a and b:
            target = near_corner.at[(0 if a > 0 else 2) + (0 if b > 0 else 1)]
        elif a:
            target = near_ns.at[0 if a > 0 else 1]
        else:
            target = near_ew.at[0 if b > 0 else 1]
        near.append(send(source, target, near_sem.at[index], (a, b)))

    far = []
    for index, (a, b) in enumerate(around):
        up, right = int(a > 0), int(b > 0)
        if a and b:
            source, target = far_corner.at[2 * up + right], far_corner.at[4 + 2 * (1 - up) + (1 - right)]
        elif a:
            source, target = far_ns.at[up], far_ns.at[2 + 1 - up]
        else:
            source, target = far_ew.at[right], far_ew.at[2 + 1 - right]
        far.append(send(source, target, far_sem.at[index], (a, b)))
    for copy in near:
        copy.wait_recv()

    lane = lax.broadcasted_iota(jnp.int32, (8, LANES), 1)

    def assemble(own, west, east):
        blank = jnp.zeros((8, LANES - cols), jnp.float32)
        own = jnp.concatenate([own, blank], axis=1)
        west = jnp.concatenate([blank, west], axis=1)
        east = jnp.concatenate([blank, east], axis=1)
        return jnp.where(lane < cols, own, jnp.where(lane < cols + 2, east, west))

    for c in range(2):
        reach[c, 0:8] = assemble(near_ns[0, c], near_corner[0, c], near_corner[1, c])
        for r in range(0, rows, 8):
            band_rows = pl.ds(r, 8)
            reach[c, r + 8 : r + 16] = assemble(
                courant_ref[c, band_rows], near_ew[0, c, band_rows], near_ew[1, c, band_rows]
            )
        reach[c, rows + 8 : rows + 16] = assemble(near_ns[1, c], near_corner[2, c], near_corner[3, c])

    row = lax.broadcasted_iota(jnp.int32, (rows + 16, LANES), 0) - 8 + lat * rows
    weight = link_weights(reach[0], reach[1], row, total_rows)

    arrived = {step: shifted(weight[step], *step) for step in ONE_STEP}
    sums = {}
    for first in ONE_STEP:
        for second in ONE_STEP:
            total = (first[0] + second[0], first[1] + second[1])
            term = shifted(arrived[first] * weight[second], *second)
            sums[total] = sums[total] + term if total in sums else term
    half = lax.broadcasted_iota(jnp.int32, (rows // 2, LANES), 1) < cols
    for index, total in enumerate(TWO_STEPS):
        wide[index] = sums[total]
        even = wide[index, pl.ds(8, rows // 2, 2), :]
        odd = wide[index, pl.ds(9, rows // 2, 2), :]
        stencil[index] = jnp.where(half, even, pltpu.roll(odd, cols, 1))

    def halves_into(ref, at, columns, value):
        upper = value.astype(jnp.bfloat16)
        count = value.shape[0]
        ref[at : at + count, columns] = upper
        ref[at + count : at + 2 * count, columns] = (value - upper.astype(jnp.float32)).astype(jnp.bfloat16)

    flat_lane = lax.broadcasted_iota(jnp.int32, (nobs, LANES), 1)
    second_row = jnp.where(flat_lane >= cols, 1, 0)
    column = flat_lane - second_row * cols
    flat_state = state_ref[...].reshape(rows * cols, members)
    for batch in range(BATCHES):
        where = jnp.concatenate([where_ref[i, batch : batch + 1] for i in range(3)], axis=0)
        where = jnp.concatenate([where, jnp.zeros((8 - 3, nobs), jnp.int32)], axis=0)
        where = jnp.transpose(where.astype(jnp.float32)).astype(jnp.int32)
        obs_row = where[:, 0:1] - lat * rows
        obs_col = where[:, 1:2] - lon * cols + 2
        obs_col = jnp.where(obs_col < 0, obs_col + total_cols, obs_col) - 2
        obs_col = jnp.where(obs_col >= total_cols - 2, obs_col - total_cols, obs_col)
        lon_step = column - obs_col
        lat_base = second_row - obs_row

        def one_pair(pair, carry):
            lat_step = lat_base + 2 * pair
            total = jnp.zeros((nobs, LANES), jnp.float32)
            for index, (a, b) in enumerate(TWO_STEPS):
                total = jnp.where((lat_step == a) & (lon_step == b), stencil[index, pl.ds(pair, 1), :], total)
            halves_into(weights, 0, pl.ds(pl.multiple_of(pair * LANES, LANES), LANES), total)
            return carry

        lax.fori_loop(0, rows // 2, one_pair, 0)
        share = jnp.dot(weights[...], flat_state, preferred_element_type=jnp.float32)
        part[batch] = share[:nobs] + share[nobs:]
        for index, partner in enumerate(partners):
            pltpu.make_async_remote_copy(
                src_ref=part.at[batch, *tile_of(partner)], dst_ref=pieces.at[batch, index],
                send_sem=send_sem.at[batch, 0], recv_sem=part_sem.at[batch],
                device_id=plane_device(partner), device_id_type=MESH,
            ).start()

    mine = tile_of((0, 0))
    for batch in range(BATCHES):
        pltpu.make_async_copy(pieces.at[batch], pieces.at[batch], part_sem.at[batch]).wait()
        piece[batch] = part[batch, *mine] + jnp.sum(pieces[batch], axis=0)
        for index, distance in enumerate(distances):
            pltpu.make_async_remote_copy(
                src_ref=piece.at[batch], dst_ref=line.at[batch, index],
                send_sem=send_sem.at[batch, 1], recv_sem=line_sem.at[batch],
                device_id=line_device(distance), device_id_type=MESH,
            ).start()

    for copy in far:
        copy.wait_recv()
    gap = jnp.zeros((14, members), jnp.float32)

    def beside(at, west, east):
        cells[at, cols : cols + 16] = jnp.concatenate([east, gap], axis=0).astype(jnp.bfloat16)
        cells[at, LANES - 16 :] = jnp.concatenate([gap, west], axis=0).astype(jnp.bfloat16)

    def beside_row(r, carry):
        beside(r + 2, far_ew[2, r], far_ew[3, r])
        return carry

    lax.fori_loop(0, rows, beside_row, 0)
    for side, at in ((0, 1), (1, rows + 2)):
        cells[(0, rows + 2)[side] : (2, rows + 4)[side], :cols] = far_ns[2 + side].astype(jnp.bfloat16)
        beside(at, far_corner[4 + 2 * side, 6:8], far_corner[4 + 2 * side + 1, 0:2])
    step_lane = lax.broadcasted_iota(jnp.int32, (cols, LANES), 1) - lax.broadcasted_iota(jnp.int32, (cols, LANES), 0)
    step_lane = jnp.where(step_lane > LANES // 2 + 2, step_lane - LANES, step_lane)

    def one_pair_of_rows(pair, carry):
        first = 2 * pair
        for around_row in range(6):
            for r in range(2):
                a = around_row - 2 - r
                total = jnp.zeros((cols, LANES), jnp.float32)
                if -2 <= a <= 2:
                    for index, (lat_step, b) in enumerate(TWO_STEPS):
                        if lat_step == a:
                            total = jnp.where(step_lane == b, wide[index, pl.ds(first + around_row + 6, 1), :], total)
                halves_into(bands, 2 * r * cols, pl.ds(around_row * LANES, LANES), total)
        near_cells = cells[pl.ds(first, 6)].reshape(6 * LANES, members)
        result = jnp.dot(bands[...], near_cells, preferred_element_type=jnp.float32)
        for r in range(2):
            value = result[2 * r * cols : (2 * r + 1) * cols] + result[(2 * r + 1) * cols : (2 * r + 2) * cols]
            field[first + r] = value
            at = pl.ds(pl.multiple_of((first + r) * cols, cols), cols)
            split[at] = jnp.concatenate(halves_of(value), axis=1)
        return carry

    lax.fori_loop(0, rows // 2, one_pair_of_rows, 0)

    for batch in range(BATCHES):
        pltpu.make_async_copy(line.at[batch], line.at[batch], line_sem.at[batch]).wait()
        priors[batch, *mine] = piece[batch] + jnp.sum(line[batch], axis=0)
        for partner in partners:
            pltpu.make_async_remote_copy(
                src_ref=priors.at[batch, *mine], dst_ref=priors.at[batch, *mine],
                send_sem=send_sem.at[batch, 2], recv_sem=all_sem.at[batch],
                device_id=plane_device(partner), device_id_type=MESH,
            ).start()
    def arrival(batch):
        pltpu.make_async_copy(pieces.at[batch], pieces.at[batch], all_sem.at[batch]).wait()
        return priors[batch]

    analyse(
        sizes, arrival, where_ref, value_ref, variance_ref, noise_ref, field_out, spread_out, change_ref, field, split, spread, out_sem
    )

    for copy in near + far:
        copy.wait_send()
    for batch in range(BATCHES):
        for sem, sent in enumerate((pieces, line, pieces)):
            pltpu.make_async_copy(sent.at[batch], sent.at[batch], send_sem.at[batch, sem]).wait()


def matmul_exact(left, right, contract=(1, 0)):
    return lax.dot_general(
        left, right, (((contract[0],), (contract[1],)), ((), ())),
        precision=HIGHEST, preferred_element_type=jnp.float32,
    )


def halves_of(value):
    upper = value.astype(jnp.bfloat16)
    return upper, (value - upper.astype(jnp.float32)).astype(jnp.bfloat16)


def product(left, right):
    return jnp.dot(left, right, preferred_element_type=jnp.float32)


def twice(right):
    upper, lower = halves_of(right)
    return jnp.concatenate(
        [jnp.concatenate([upper, lower], axis=1), jnp.concatenate([upper, jnp.zeros_like(lower)], axis=1)], axis=0
    )


def thrice(right):
    upper, lower = halves_of(right)
    return jnp.concatenate([upper, upper, lower], axis=0)


def solve_pivot(pivot, rows):
    count = len(rows)
    pivot, rows, factor, inverse = dict(pivot), list(rows), {}, {}
    for j in range(0, count, 2):
        a, b, c = pivot[j, j], pivot[j + 1, j], pivot[j + 1, j + 1]
        scale = 1.0 / (a * c - b * b)
        inverse[j] = first, cross, last = c * scale, -b * scale, a * scale
        for i in range(j + 2, count):
            factor[i, j] = pivot[i, j] * first + pivot[i, j + 1] * cross
            factor[i, j + 1] = pivot[i, j] * cross + pivot[i, j + 1] * last
        for i in range(j + 2, count):
            for k in range(j + 2, i + 1):
                pivot[i, k] -= factor[i, j] * pivot[k, j] + factor[i, j + 1] * pivot[k, j + 1]
    for j in range(0, count, 2):
        for i in range(j + 2, count):
            rows[i] -= factor[i, j] * rows[j] + factor[i, j + 1] * rows[j + 1]
    for j in range(0, count, 2):
        first, cross, last = inverse[j]
        rows[j], rows[j + 1] = first * rows[j] + cross * rows[j + 1], cross * rows[j] + last * rows[j + 1]
    for i in reversed(range(0, count, 2)):
        for j in range(i):
            rows[j] -= factor[i, j] * rows[i] + factor[i + 1, j] * rows[i + 1]
    return rows


def tree_sum(terms):
    while len(terms) > 1:
        terms = [a + b for a, b in zip(terms[::2], terms[1::2])] + terms[len(terms) // 2 * 2 :]
    return terms[0]


def inverse_of(system, beside, panel=32, block=8):
    size = system.shape[0]
    spread = (8, size)
    lane = lax.broadcasted_iota(jnp.int32, spread, 1)
    sub = lax.broadcasted_iota(jnp.int32, spread, 0)
    panel_lane = lax.broadcasted_iota(jnp.int32, (panel, size), 1)
    panel_sub = lax.broadcasted_iota(jnp.int32, (panel, size), 0)
    whole_lane = lax.broadcasted_iota(jnp.int32, (size, size), 1)
    for start in range(0, size, panel):
        old = system[start : start + panel]
        bands = [old[i : i + 8] for i in range(0, panel, 8)]
        for here in range(0, panel // 8, block // 8):
            first = start + 8 * here
            inside = (lane >= first) & (lane < first + block)
            columns = [
                [jnp.broadcast_to(band[:, first + j : first + j + 1], spread) for j in range(block)] for band in bands
            ]
            pivot = {
                (i, j): jnp.broadcast_to(columns[here + i // 8][j][i % 8 : i % 8 + 1], spread)
                for i in range(block)
                for j in range(i + 1)
            }
            rows = [
                jnp.where(
                    inside,
                    jnp.where(lane == first + j, -1.0, 0.0),
                    jnp.broadcast_to(bands[here + j // 8][j % 8 : j % 8 + 1], spread),
                )
                for j in range(block)
            ]
            rows = solve_pivot(pivot, rows)
            for i, band in enumerate(bands):
                if here <= i < here + block // 8:
                    bands[i] = rows[8 * (i - here) + 7]
                    for j in range(7):
                        bands[i] = jnp.where(sub == j, rows[8 * (i - here) + j], bands[i])
                else:
                    terms = [columns[i][j] * rows[j] for j in range(block)]
                    bands[i] = jnp.where(inside, 0.0, band) - tree_sum(terms)
            for _ in range(block // 8):
                beside()
        swept = jnp.concatenate(bands, axis=0)
        inside = (panel_lane >= start) & (panel_lane < start + panel)
        old = jnp.where(inside, jnp.where(panel_lane == panel_sub + start, -1.0, 0.0), old)
        inside = (whole_lane >= start) & (whole_lane < start + panel)
        system = jnp.where(inside, 0.0, system) - matmul_exact(old, swept, (0, 0))
        parts = [system[:start], swept, system[start + panel :]]
        system = jnp.concatenate([part for part in parts if part.shape[0]], axis=0)
    return -system


def square(value):
    return value * value


def analyse(
    sizes, arrival, where_ref, value_ref, variance_ref, noise_ref, field_out, spread_out, change_ref, field, split, spread, out_sem
):
    lon_count, lat_count = sizes
    rows, cols, members = field.shape
    nobs = where_ref.shape[2]
    total_cols = cols * lon_count
    first_row, first_col = lax.axis_index("lat") * rows, lax.axis_index("lon") * cols

    blank = jnp.zeros((8 - 2 * BATCHES, nobs), jnp.float32)
    upright = jnp.transpose(jnp.concatenate([value_ref[...], variance_ref[...], blank], axis=0))
    eye = lax.broadcasted_iota(jnp.int32, (nobs, nobs), 0) == lax.broadcasted_iota(jnp.int32, (nobs, nobs), 1)

    def lon_distance(cell, obs):
        gap = jnp.abs(cell - obs)
        return jnp.minimum(gap, total_cols - gap)

    def scaled_square(gap, radius):
        return square(gap).astype(jnp.float32) / square(radius).astype(jnp.float32)

    def weights_of(batch, priors, anomaly, unit):
        variance = upright[:, BATCHES + batch : BATCHES + batch + 1]
        system = matmul_exact(anomaly, anomaly, (1, 1)) / (members - 1)
        system += jnp.where(eye, variance, 0.0)
        misfit = upright[:, batch : batch + 1] + jnp.sqrt(variance) * noise_ref[batch] - priors
        units = iter(range(UNITS))
        inverse = inverse_of(system, lambda: unit(next(units)), 32, BLOCK)
        return matmul_exact(inverse, misfit)

    def centred(priors):
        return priors - jnp.mean(priors, axis=1, keepdims=True)

    obs = [[where_ref[i, batch : batch + 1, :] for i in range(3)] for batch in range(BATCHES)]
    priors = [arrival(0)]
    anomaly, weights = [centred(priors[0])], []
    cell_lon = first_col + lax.broadcasted_iota(jnp.int32, (cols, 1), 0)
    lon_part = [scaled_square(lon_distance(cell_lon, lon), radius) for _, lon, radius in obs]
    count = rows // UNITS

    def taper_of(batch, row):
        lat, _, radius = obs[batch]
        room = 1.0 - scaled_square(first_row + row - lat, radius)
        return square(jnp.maximum(room - lon_part[batch], 0.0))

    def spread_unit(batch, index, covariance):
        covariance = covariance[:, :nobs] + covariance[:, nobs:]
        taper = jnp.concatenate([taper_of(batch, index * count + r) for r in range(count)], axis=0)
        upper, lower = halves_of(taper * covariance)
        spread[batch, cells_of(index)] = jnp.concatenate([upper, lower, upper], axis=1)

    def cells_of(index):
        return pl.ds(index * count * cols, count * cols)

    right = [twice(jnp.transpose(anomaly[0] / (members - 1)))]

    def first_unit(index):
        spread_unit(0, index, product(split[cells_of(index)], right[0]))

    weights.append(weights_of(0, priors[0], anomaly[0], first_unit))

    where = jnp.concatenate(obs[1] + [jnp.zeros((8 - 3, nobs), jnp.int32)], axis=0)
    where = jnp.transpose(where.astype(jnp.float32)).astype(jnp.int32)
    lat_gap = where[:, 0:1] - obs[0][0]
    lon_gap = lon_distance(where[:, 1:2], obs[0][1])
    distance = (square(lat_gap) + square(lon_gap)).astype(jnp.float32)
    taper = square(jnp.maximum(1.0 - distance / square(obs[0][2]).astype(jnp.float32), 0.0))
    before = arrival(1)
    covariance = matmul_exact(centred(before), anomaly[0], (1, 1)) / (members - 1)
    priors.append(before + matmul_exact(taper * covariance, weights[0]))
    anomaly.append(centred(priors[1]))
    carried = twice(matmul_exact(centred(weights[0]), anomaly[1], (1, 1)) / (members - 1))
    right.append(twice(jnp.transpose(anomaly[1] / (members - 1))))
    change = [thrice(weights[0])]

    def second_unit(index):
        at, at_rows = cells_of(index), pl.ds(index * count, count)
        covariance = product(split[at], right[1]) + product(spread[0, at, : 2 * nobs], carried)
        spread_unit(1, index, covariance)
        field[at_rows] += product(spread[0, at], change[0]).reshape(count, cols, members)
        for copy in copies_of(index):
            copy.start()

    def copies_of(index):
        at, at_rows = cells_of(index), pl.ds(index * count, count)
        return (
            pltpu.make_async_copy(field.at[at_rows], field_out.at[at_rows], out_sem.at[index, 0]),
            pltpu.make_async_copy(spread.at[1, at], spread_out.at[at], out_sem.at[index, 1]),
        )

    weights.append(weights_of(1, priors[1], anomaly[1], second_unit))
    change.append(thrice(weights[1]))

    change_ref[...] = change[1]
    for index in range(UNITS):
        for copy in copies_of(index):
            copy.wait()


def update_kernel(
    field_hbm, spread_hbm, change_hbm, out_ref, field, spread, change, analysis, change_sem, in_sem, out_sem
):
    rows, cols, members = field.shape
    chunks = out_sem.shape[0]
    count = rows // chunks
    whole = pltpu.make_async_copy(change_hbm, change, change_sem)
    whole.start()
    loads, stores = [], []
    for index in range(chunks):
        at, at_cells = pl.ds(index * count, count), pl.ds(index * count * cols, count * cols)
        loads.append(
            (
                pltpu.make_async_copy(spread_hbm.at[at_cells], spread.at[at_cells], in_sem.at[index, 0]),
                pltpu.make_async_copy(field_hbm.at[at], field.at[at], in_sem.at[index, 1]),
            )
        )
        for load in loads[-1]:
            load.start()
    whole.wait()
    for index in range(chunks):
        at, at_cells = pl.ds(index * count, count), pl.ds(index * count * cols, count * cols)
        for load in loads[index]:
            load.wait()
        step = product(spread[at_cells], change[...])
        analysis[at] = (field[at] + step.reshape(count, cols, members)).astype(jnp.bfloat16)
        stores.append(pltpu.make_async_copy(analysis.at[at], out_ref.at[at], out_sem.at[index]))
        stores[-1].start()
    for store in stores:
        store.wait()


def update(field, spread, change):
    chunks = 8
    anywhere = pl.BlockSpec(memory_space=pl.ANY)
    dma = pltpu.SemaphoreType.DMA
    return pl.pallas_call(
        update_kernel,
        out_shape=jax.ShapeDtypeStruct(field.shape, jnp.bfloat16),
        in_specs=[anywhere] * 3,
        out_specs=anywhere,
        scratch_shapes=[pltpu.VMEM(array.shape, array.dtype) for array in (field, spread, change)]
        + [pltpu.VMEM(field.shape, jnp.bfloat16), dma, dma((chunks, 2)), dma((chunks,))],
        compiler_params=pltpu.CompilerParams(vmem_limit_bytes=VMEM_BYTES),
        name="update",
    )(field, spread, change)


def window(state, courant, where, value, variance, noise, lon_count, lat_count):
    rows, cols, members = state.shape
    nobs = where.shape[2]
    plane_lon, line_lon, line_lat, plane_lat = split_mesh(lon_count, lat_count)
    plane, lines = plane_lon * plane_lat, line_lat * line_lon
    band = nobs * (members // LANES) // plane
    f32, bf16 = jnp.float32, jnp.bfloat16
    anywhere = pl.BlockSpec(memory_space=pl.ANY)
    dma = pltpu.SemaphoreType.DMA
    arguments = (state, courant, where, value, variance, noise)
    return pl.pallas_call(
        functools.partial(window_kernel, (lon_count, lat_count)),
        out_shape=(
            jax.ShapeDtypeStruct((rows, cols, members), f32),
            jax.ShapeDtypeStruct((rows * cols, 3 * nobs), bf16),
            jax.ShapeDtypeStruct((3 * nobs, members), bf16),
        ),
        in_specs=[anywhere] * len(arguments),
        out_specs=(anywhere, anywhere, pl.BlockSpec(memory_space=pltpu.VMEM)),
        scratch_shapes=[pltpu.VMEM(argument.shape, argument.dtype) for argument in arguments]
        + [
            pltpu.VMEM((2, 2, 8, cols), f32),
            pltpu.VMEM((2, 2, rows, cols), f32),
            pltpu.VMEM((4, 2, 8, cols), f32),
            pltpu.VMEM((2, rows + 16, LANES), f32),
            pltpu.VMEM((len(TWO_STEPS), rows + 16, LANES), f32),
            pltpu.VMEM((len(TWO_STEPS), rows // 2, LANES), f32),
            pltpu.VMEM((2 * nobs, rows * cols), bf16),
            pltpu.VMEM((BATCHES, nobs, members), f32),
            pltpu.VMEM((BATCHES, plane - 1, band, LANES), f32),
            pltpu.VMEM((BATCHES, band, LANES), f32),
            pltpu.VMEM((BATCHES, lines - 1, band, LANES), f32),
            pltpu.VMEM((BATCHES, nobs, members), f32),
            pltpu.VMEM((rows + 4, LANES, members), bf16),
            pltpu.VMEM((4 * cols, 6 * LANES), bf16),
            pltpu.VMEM((4, 2, cols, members), f32),
            pltpu.VMEM((4, rows, 2, members), f32),
            pltpu.VMEM((8, 8, members), f32),
            pltpu.VMEM((rows, cols, members), f32),
            pltpu.VMEM((rows * cols, 2 * members), bf16),
            pltpu.VMEM((BATCHES, rows * cols, 3 * nobs), bf16),
            dma((len(arguments),)),
            dma((8, 2)),
            dma((8, 2)),
            dma((BATCHES,)),
            dma((BATCHES,)),
            dma((BATCHES,)),
            dma((BATCHES, 3)),
            dma((UNITS, 2)),
        ],
        compiler_params=pltpu.CompilerParams(
            collective_id=0, has_side_effects=True, vmem_limit_bytes=VMEM_BYTES
        ),
        name="window",
    )(*arguments)


def body(ensemble_state, courant, obs_where, obs_value, obs_variance, obs_noise):
    counts = lax.axis_size("lon"), lax.axis_size("lat")
    where = jnp.transpose(obs_where, (1, 0, 2))
    return update(*window(ensemble_state, courant, where, obs_value, obs_variance, obs_noise, *counts))


def solution(mesh):
    placed = (P("lat", "lon", None), P(None, "lat", "lon"), P(), P(), P(), P())
    return jax.shard_map(
        body, mesh=mesh, in_specs=placed, out_specs=P("lat", "lon", None), check_vma=False
    )
```

```python
import functools
import jax
import jax.numpy as jnp
from jax import lax
from jax.experimental import pallas as pl
from jax.experimental.pallas import tpu as pltpu
from jax.sharding import PartitionSpec as P

BATCHES = 2
MESH = pl.DeviceIdType.MESH
UNITS = 16
KEY = 8192
BLOCK = 8
VMEM_BYTES = 63 * 1024 * 1024
LANES = 128
HIGHEST = lax.Precision.HIGHEST
ONE_STEP = ((0, 0), (-1, 0), (1, 0), (0, -1), (0, 1))
TWO_STEPS = tuple(sorted({(a + c, b + d) for a, b in ONE_STEP for c, d in ONE_STEP}))


def split_mesh(lon_count, lat_count):
    plane_lat = 8 if lat_count == 16 else lat_count // 2
    line_lon = 8 if lon_count == 32 else lon_count // 2
    return lon_count // line_lon, line_lon, lat_count // plane_lat, plane_lat


def shifted(field, rows, lanes):
    if rows:
        field = pltpu.roll(field, rows % field.shape[0], 0)
    if lanes:
        field = pltpu.roll(field, lanes % field.shape[1], 1)
    return field


def link_weights(speed_lat, speed_lon, row, total_rows):
    inside = (row >= 0) & (row < total_rows)
    lat_plus = jnp.maximum(speed_lat, 0.0)
    lat_minus = jnp.minimum(speed_lat, 0.0)
    lon_plus = jnp.maximum(speed_lon, 0.0)
    lon_minus = jnp.minimum(speed_lon, 0.0)
    zero = jnp.zeros_like(speed_lat)
    return {
        (0, 0): jnp.where(inside, 1.0 - lat_plus + lat_minus - lon_plus + lon_minus, zero),
        (-1, 0): jnp.where(inside & (row > 0), lat_plus, zero),
        (1, 0): jnp.where(inside & (row < total_rows - 1), -lat_minus, zero),
        (0, -1): jnp.where(inside, lon_plus, zero),
        (0, 1): jnp.where(inside, -lon_minus, zero),
    }


def ring_flips(count):
    flips = [lambda place: place]
    size = 1
    while size < count:
        flips += [lambda place, size=size, f=f: flip_bit(f(place), size) for f in flips]
        size *= 2
    return flips


def flip_bit(place, size):
    return place + size - 2 * size * (place // size % 2)


def window_kernel(
    sizes, state_hbm, courant_hbm, where_hbm, value_hbm, variance_hbm, noise_hbm,
    field_out, spread_out, change_ref,
    state_ref, courant_ref, where_ref, value_ref, variance_ref, noise_ref,
    near_ns, near_ew, near_corner, keys, reach, wide, stencil, weights, part, pieces, piece, line, priors,
    cells, bands, far_ns, far_ew, far_corner, field, split, spread,
    in_sem, near_sem, far_sem, part_sem, line_sem, all_sem, send_sem, out_sem,
):
    lon_count, lat_count = sizes
    plane_lon, line_lon, line_lat, plane_lat = split_mesh(lon_count, lat_count)
    plane, lines = plane_lon * plane_lat, line_lat * line_lon
    rows, cols, members = state_ref.shape
    total_rows, total_cols = rows * lat_count, cols * lon_count
    nobs = where_ref.shape[2]
    halves = members // LANES
    band = nobs * halves // plane
    lon, lat = lax.axis_index("lon"), lax.axis_index("lat")
    line_me = (lat // plane_lat) * line_lon + lon % line_lon
    arguments = (
        (courant_hbm, courant_ref), (state_hbm, state_ref), (where_hbm, where_ref),
        (value_hbm, value_ref), (variance_hbm, variance_ref), (noise_hbm, noise_ref),
    )
    loads = [pltpu.make_async_copy(*pair, in_sem.at[index]) for index, pair in enumerate(arguments)]
    for load in loads:
        load.start()

    lon_flips, lat_flips = ring_flips(plane_lon), ring_flips(plane_lat)
    plane_x = [flip(lon // line_lon) for flip in lon_flips]
    plane_y = [flip(lat % plane_lat) for flip in lat_flips]
    partners = [(i, j) for i in range(plane_lon) for j in range(plane_lat)][1:]
    hops = {0: 0, 1: 1, 2: 2, 3: 1}
    partners.sort(key=lambda p: -hops[p[0] % 4] - hops[p[1] // 2 % 4])
    distances = sorted(range(1, lines), key=lambda d: -min(d, lines - d))

    def plane_device(partner):
        return {
            "lon": plane_x[partner[0]] * line_lon + lon % line_lon,
            "lat": lat // plane_lat * plane_lat + plane_y[partner[1]],
        }

    def tile_of(partner):
        index = plane_x[partner[0]] * plane_lat + plane_y[partner[1]]
        return (
            pl.ds(pl.multiple_of(index // halves * band, band), band),
            pl.ds(pl.multiple_of(index % halves * LANES, LANES), LANES),
        )

    def line_device(distance):
        index = lax.rem(line_me + distance, lines)
        return {
            "lon": lon // line_lon * line_lon + index % line_lon,
            "lat": index // line_lon * plane_lat + lat % plane_lat,
        }

    def neighbour(lat_step, lon_step):
        return {
            "lon": lax.rem(lon + lon_step + lon_count, lon_count),
            "lat": lax.rem(lat + lat_step + lat_count, lat_count),
        }

    around = [(a, b) for a in (-1, 1) for b in (0, -1, 1)] + [(0, -1), (0, 1)]

    barrier = pltpu.get_barrier_semaphore()
    greeted = [neighbour(*step) for step in around]
    greeted += [line_device(distance) for distance in distances]
    greeted += [plane_device(partner) for partner in partners]
    for target in greeted:
        pl.semaphore_signal(barrier, inc=1, device_id=target, device_id_type=MESH)

    for load in loads:
        load.wait()
    edges, ends = ((0, 2), (rows - 2, rows)), ((0, 2), (cols - 2, cols))
    for side in range(2):
        low, high = edges[side]
        far_ns[side] = state_ref[low:high].astype(jnp.float32)
        low, high = ends[side]
        far_ew[side] = state_ref[:, low:high].astype(jnp.float32)
        for other in range(2):
            row, first = (0, rows - 1)[side], (0, cols - 8)[other]
            far_corner[2 * side + other] = state_ref[row, first : first + 8].astype(jnp.float32)
    cells[...] = jnp.zeros(cells.shape, jnp.bfloat16)
    cells[2 : 2 + rows, :cols] = state_ref[...]
    flat_lane = lax.broadcasted_iota(jnp.int32, (nobs, LANES), 1)
    second_row = jnp.where(flat_lane >= cols, 1, 0)
    column = flat_lane - second_row * cols
    for batch in range(BATCHES):
        where = jnp.concatenate([where_ref[i, batch : batch + 1] for i in range(3)], axis=0)
        where = jnp.concatenate([where, jnp.zeros((8 - 3, nobs), jnp.int32)], axis=0)
        where = jnp.transpose(where.astype(jnp.float32)).astype(jnp.int32)
        obs_row = where[:, 0:1] - lat * rows
        obs_col = where[:, 1:2] - lon * cols + 2
        obs_col = jnp.where(obs_col < 0, obs_col + total_cols, obs_col) - 2
        obs_col = jnp.where(obs_col >= total_cols - 2, obs_col - total_cols, obs_col)
        keys[batch] = (second_row - obs_row) * KEY + column - obs_col
    pl.semaphore_wait(barrier, len(greeted))

    def send(src, dst, sem, step):
        copy = pltpu.make_async_remote_copy(
            src_ref=src, dst_ref=dst, send_sem=sem.at[0], recv_sem=sem.at[1],
            device_id=neighbour(*step), device_id_type=MESH,
        )
        copy.start()
        return copy

    low, high = pl.ds(0, 8), pl.ds(rows - 8, 8)
    near = []
    for index, (a, b) in enumerate(around):
        source = courant_ref.at[:, {-1: low, 1: high}[a], :] if a else courant_ref
        if a and b:
            target = near_corner.at[(0 if a > 0 else 2) + (0 if b > 0 else 1)]
        elif a:
            target = near_ns.at[0 if a > 0 else 1]
        else:
            target = near_ew.at[0 if b > 0 else 1]
        near.append(send(source, target, near_sem.at[index], (a, b)))

    far = []
    for index, (a, b) in enumerate(around):
        up, right = int(a > 0), int(b > 0)
        if a and b:
            source, target = far_corner.at[2 * up + right], far_corner.at[4 + 2 * (1 - up) + (1 - right)]
        elif a:
            source, target = far_ns.at[up], far_ns.at[2 + 1 - up]
        else:
            source, target = far_ew.at[right], far_ew.at[2 + 1 - right]
        far.append(send(source, target, far_sem.at[index], (a, b)))
    for copy in near:
        copy.wait_recv()

    lane = lax.broadcasted_iota(jnp.int32, (8, LANES), 1)

    def assemble(own, west, east):
        blank = jnp.zeros((8, LANES - cols), jnp.float32)
        own = jnp.concatenate([own, blank], axis=1)
        west = jnp.concatenate([blank, west], axis=1)
        east = jnp.concatenate([blank, east], axis=1)
        return jnp.where(lane < cols, own, jnp.where(lane < cols + 2, east, west))

    for c in range(2):
        reach[c, 0:8] = assemble(near_ns[0, c], near_corner[0, c], near_corner[1, c])
        for r in range(0, rows, 8):
            band_rows = pl.ds(r, 8)
            reach[c, r + 8 : r + 16] = assemble(
                courant_ref[c, band_rows], near_ew[0, c, band_rows], near_ew[1, c, band_rows]
            )
        reach[c, rows + 8 : rows + 16] = assemble(near_ns[1, c], near_corner[2, c], near_corner[3, c])

    row = lax.broadcasted_iota(jnp.int32, (rows + 16, LANES), 0) - 8 + lat * rows
    weight = link_weights(reach[0], reach[1], row, total_rows)

    arrived = {step: shifted(weight[step], *step) for step in ONE_STEP}
    sums = {}
    for first in ONE_STEP:
        for second in ONE_STEP:
            total = (first[0] + second[0], first[1] + second[1])
            term = shifted(arrived[first] * weight[second], *second)
            sums[total] = sums[total] + term if total in sums else term
    half = lax.broadcasted_iota(jnp.int32, (rows // 2, LANES), 1) < cols
    for index, total in enumerate(TWO_STEPS):
        wide[index] = sums[total]
        even = wide[index, pl.ds(8, rows // 2, 2), :]
        odd = wide[index, pl.ds(9, rows // 2, 2), :]
        stencil[index] = jnp.where(half, even, pltpu.roll(odd, cols, 1))

    def halves_into(ref, at, columns, value):
        upper = value.astype(jnp.bfloat16)
        count = value.shape[0]
        ref[at : at + count, columns] = upper
        ref[at + count : at + 2 * count, columns] = (value - upper.astype(jnp.float32)).astype(jnp.bfloat16)

    flat_state = state_ref[...].reshape(rows * cols, members)

    def make_share(batch):
        def one_pair(pair, carry):
            total = jnp.zeros((nobs, LANES), jnp.float32)
            for index, (a, b) in enumerate(TWO_STEPS):
                met = keys[batch] == a * KEY + b - 2 * KEY * pair
                total = jnp.where(met, stencil[index, pl.ds(pair, 1), :], total)
            halves_into(weights, 0, pl.ds(pl.multiple_of(pair * LANES, LANES), LANES), total)
            return carry

        lax.fori_loop(0, rows // 2, one_pair, 0)
        share = jnp.dot(weights[...], flat_state, preferred_element_type=jnp.float32)
        part[batch] = share[:nobs] + share[nobs:]

    def send_share(batch):
        for index, partner in enumerate(partners):
            pltpu.make_async_remote_copy(
                src_ref=part.at[batch, *tile_of(partner)], dst_ref=pieces.at[batch, index],
                send_sem=send_sem.at[batch, 0], recv_sem=part_sem.at[batch],
                device_id=plane_device(partner), device_id_type=MESH,
            ).start()

    mine = tile_of((0, 0))

    def send_piece(batch):
        pltpu.make_async_copy(pieces.at[batch], pieces.at[batch], part_sem.at[batch]).wait()
        piece[batch] = part[batch, *mine] + jnp.sum(pieces[batch], axis=0)
        for index, distance in enumerate(distances):
            pltpu.make_async_remote_copy(
                src_ref=piece.at[batch], dst_ref=line.at[batch, index],
                send_sem=send_sem.at[batch, 1], recv_sem=line_sem.at[batch],
                device_id=line_device(distance), device_id_type=MESH,
            ).start()

    def send_priors(batch):
        pltpu.make_async_copy(line.at[batch], line.at[batch], line_sem.at[batch]).wait()
        priors[batch, *mine] = piece[batch] + jnp.sum(line[batch], axis=0)
        for partner in partners:
            pltpu.make_async_remote_copy(
                src_ref=priors.at[batch, *mine], dst_ref=priors.at[batch, *mine],
                send_sem=send_sem.at[batch, 2], recv_sem=all_sem.at[batch],
                device_id=plane_device(partner), device_id_type=MESH,
            ).start()

    make_share(0)
    send_share(0)
    make_share(1)
    send_piece(0)
    send_share(1)

    for copy in far:
        copy.wait_recv()
    gap = jnp.zeros((14, members), jnp.float32)

    def beside(at, west, east):
        cells[at, cols : cols + 16] = jnp.concatenate([east, gap], axis=0).astype(jnp.bfloat16)
        cells[at, LANES - 16 :] = jnp.concatenate([gap, west], axis=0).astype(jnp.bfloat16)

    def beside_row(r, carry):
        beside(r + 2, far_ew[2, r], far_ew[3, r])
        return carry

    lax.fori_loop(0, rows, beside_row, 0)
    for side, at in ((0, 1), (1, rows + 2)):
        cells[(0, rows + 2)[side] : (2, rows + 4)[side], :cols] = far_ns[2 + side].astype(jnp.bfloat16)
        beside(at, far_corner[4 + 2 * side, 6:8], far_corner[4 + 2 * side + 1, 0:2])
    step_lane = lax.broadcasted_iota(jnp.int32, (cols, LANES), 1) - lax.broadcasted_iota(jnp.int32, (cols, LANES), 0)
    step_lane = jnp.where(step_lane > LANES // 2 + 2, step_lane - LANES, step_lane)

    def one_pair_of_rows(pair, carry):
        first = 2 * pair
        for around_row in range(6):
            for r in range(2):
                a = around_row - 2 - r
                total = jnp.zeros((cols, LANES), jnp.float32)
                if -2 <= a <= 2:
                    for index, (lat_step, b) in enumerate(TWO_STEPS):
                        if lat_step == a:
                            total = jnp.where(step_lane == b, wide[index, pl.ds(first + around_row + 6, 1), :], total)
                halves_into(bands, 2 * r * cols, pl.ds(around_row * LANES, LANES), total)
        near_cells = cells[pl.ds(first, 6)].reshape(6 * LANES, members)
        result = jnp.dot(bands[...], near_cells, preferred_element_type=jnp.float32)
        for r in range(2):
            value = result[2 * r * cols : (2 * r + 1) * cols] + result[(2 * r + 1) * cols : (2 * r + 2) * cols]
            field[first + r] = value
            at = pl.ds(pl.multiple_of((first + r) * cols, cols), cols)
            split[at] = jnp.concatenate(halves_of(value), axis=1)
        return carry

    lax.fori_loop(0, rows // 4, one_pair_of_rows, 0)
    send_piece(1)
    send_priors(0)
    lax.fori_loop(rows // 4, rows // 2, one_pair_of_rows, 0)
    send_priors(1)

    def arrival(batch):
        pltpu.make_async_copy(pieces.at[batch], pieces.at[batch], all_sem.at[batch]).wait()
        return priors[batch]

    analyse(
        sizes, arrival, where_ref, value_ref, variance_ref, noise_ref, field_out, spread_out, change_ref, field, split, spread, out_sem
    )

    for copy in near + far:
        copy.wait_send()
    for batch in range(BATCHES):
        for sem, sent in enumerate((pieces, line, pieces)):
            pltpu.make_async_copy(sent.at[batch], sent.at[batch], send_sem.at[batch, sem]).wait()


def matmul_exact(left, right, contract=(1, 0)):
    return lax.dot_general(
        left, right, (((contract[0],), (contract[1],)), ((), ())),
        precision=HIGHEST, preferred_element_type=jnp.float32,
    )


def thirds_of(value):
    upper = value.astype(jnp.bfloat16)
    rest = value - upper.astype(jnp.float32)
    middle = rest.astype(jnp.bfloat16)
    return upper, middle, (rest - middle.astype(jnp.float32)).astype(jnp.bfloat16)


def matmul_stacked(left, right, contract=(1, 0)):
    a, b, c = thirds_of(left)
    x, y, z = thirds_of(right)
    return lax.dot_general(
        jnp.concatenate([a, b, c, a, b, a], axis=contract[0]),
        jnp.concatenate([z, y, x, y, x, x], axis=contract[1]),
        (((contract[0],), (contract[1],)), ((), ())),
        preferred_element_type=jnp.float32,
    )


def halves_of(value):
    upper = value.astype(jnp.bfloat16)
    return upper, (value - upper.astype(jnp.float32)).astype(jnp.bfloat16)


def product(left, right):
    return jnp.dot(left, right, preferred_element_type=jnp.float32)


def twice(right):
    upper, lower = halves_of(right)
    return jnp.concatenate(
        [jnp.concatenate([upper, lower], axis=1), jnp.concatenate([upper, jnp.zeros_like(lower)], axis=1)], axis=0
    )


def thrice(right):
    upper, lower = halves_of(right)
    return jnp.concatenate([upper, upper, lower], axis=0)


def solve_pivot(pivot, rows):
    count = len(rows)
    pivot, rows, factor, inverse = dict(pivot), list(rows), {}, {}
    for j in range(0, count, 2):
        a, b, c = pivot[j, j], pivot[j + 1, j], pivot[j + 1, j + 1]
        scale = 1.0 / (a * c - b * b)
        inverse[j] = first, cross, last = c * scale, -b * scale, a * scale
        for i in range(j + 2, count):
            factor[i, j] = pivot[i, j] * first + pivot[i, j + 1] * cross
            factor[i, j + 1] = pivot[i, j] * cross + pivot[i, j + 1] * last
        for i in range(j + 2, count):
            for k in range(j + 2, i + 1):
                pivot[i, k] -= factor[i, j] * pivot[k, j] + factor[i, j + 1] * pivot[k, j + 1]
    for j in range(0, count, 2):
        for i in range(j + 2, count):
            rows[i] -= factor[i, j] * rows[j] + factor[i, j + 1] * rows[j + 1]
    for j in range(0, count, 2):
        first, cross, last = inverse[j]
        rows[j], rows[j + 1] = first * rows[j] + cross * rows[j + 1], cross * rows[j] + last * rows[j + 1]
    for i in reversed(range(0, count, 2)):
        for j in range(i):
            rows[j] -= factor[i, j] * rows[i] + factor[i + 1, j] * rows[i + 1]
    return rows


def tree_sum(terms):
    while len(terms) > 1:
        terms = [a + b for a, b in zip(terms[::2], terms[1::2])] + terms[len(terms) // 2 * 2 :]
    return terms[0]


def inverse_of(system, beside, panel=32, block=8):
    size = system.shape[0]
    spread = (8, size)
    lane = lax.broadcasted_iota(jnp.int32, spread, 1)
    sub = lax.broadcasted_iota(jnp.int32, spread, 0)
    panel_lane = lax.broadcasted_iota(jnp.int32, (panel, size), 1)
    panel_sub = lax.broadcasted_iota(jnp.int32, (panel, size), 0)
    whole_lane = lax.broadcasted_iota(jnp.int32, (size, size), 1)
    for start in range(0, size, panel):
        old = system[start : start + panel]
        bands = [old[i : i + 8] for i in range(0, panel, 8)]
        for here in range(0, panel // 8, block // 8):
            first = start + 8 * here
            inside = (lane >= first) & (lane < first + block)
            columns = [
                [jnp.broadcast_to(band[:, first + j : first + j + 1], spread) for j in range(block)] for band in bands
            ]
            pivot = {
                (i, j): jnp.broadcast_to(columns[here + i // 8][j][i % 8 : i % 8 + 1], spread)
                for i in range(block)
                for j in range(i + 1)
            }
            rows = [
                jnp.where(
                    inside,
                    jnp.where(lane == first + j, -1.0, 0.0),
                    jnp.broadcast_to(bands[here + j // 8][j % 8 : j % 8 + 1], spread),
                )
                for j in range(block)
            ]
            rows = solve_pivot(pivot, rows)
            for i, band in enumerate(bands):
                if here <= i < here + block // 8:
                    bands[i] = rows[8 * (i - here) + 7]
                    for j in range(7):
                        bands[i] = jnp.where(sub == j, rows[8 * (i - here) + j], bands[i])
                else:
                    terms = [columns[i][j] * rows[j] for j in range(block)]
                    bands[i] = jnp.where(inside, 0.0, band) - tree_sum(terms)
            for _ in range(block // 8):
                beside()
        swept = jnp.concatenate(bands, axis=0)
        inside = (panel_lane >= start) & (panel_lane < start + panel)
        old = jnp.where(inside, jnp.where(panel_lane == panel_sub + start, -1.0, 0.0), old)
        inside = (whole_lane >= start) & (whole_lane < start + panel)
        system = jnp.where(inside, 0.0, system) - matmul_stacked(old, swept, (0, 0))
        parts = [system[:start], swept, system[start + panel :]]
        system = jnp.concatenate([part for part in parts if part.shape[0]], axis=0)
    return -system


def square(value):
    return value * value


def analyse(
    sizes, arrival, where_ref, value_ref, variance_ref, noise_ref, field_out, spread_out, change_ref, field, split, spread, out_sem
):
    lon_count, lat_count = sizes
    rows, cols, members = field.shape
    nobs = where_ref.shape[2]
    total_cols = cols * lon_count
    first_row, first_col = lax.axis_index("lat") * rows, lax.axis_index("lon") * cols

    blank = jnp.zeros((8 - 2 * BATCHES, nobs), jnp.float32)
    upright = jnp.transpose(jnp.concatenate([value_ref[...], variance_ref[...], blank], axis=0))
    eye = lax.broadcasted_iota(jnp.int32, (nobs, nobs), 0) == lax.broadcasted_iota(jnp.int32, (nobs, nobs), 1)

    def lon_distance(cell, obs):
        gap = jnp.abs(cell - obs)
        return jnp.minimum(gap, total_cols - gap)

    def scaled_square(gap, radius):
        return square(gap).astype(jnp.float32) / square(radius).astype(jnp.float32)

    def weights_of(batch, priors, anomaly, unit):
        variance = upright[:, BATCHES + batch : BATCHES + batch + 1]
        system = matmul_exact(anomaly, anomaly, (1, 1)) / (members - 1)
        system += jnp.where(eye, variance, 0.0)
        misfit = upright[:, batch : batch + 1] + jnp.sqrt(variance) * noise_ref[batch] - priors
        units = iter(range(UNITS))
        inverse = inverse_of(system, lambda: unit(next(units)), 32, BLOCK)
        return matmul_stacked(inverse, misfit)

    def centred(priors):
        return priors - jnp.mean(priors, axis=1, keepdims=True)

    obs = [[where_ref[i, batch : batch + 1, :] for i in range(3)] for batch in range(BATCHES)]
    priors = [arrival(0)]
    anomaly, weights = [centred(priors[0])], []
    cell_lon = first_col + lax.broadcasted_iota(jnp.int32, (cols, 1), 0)
    lon_part = [scaled_square(lon_distance(cell_lon, lon), radius) for _, lon, radius in obs]
    count = rows // UNITS

    def taper_of(batch, row):
        lat, _, radius = obs[batch]
        room = 1.0 - scaled_square(first_row + row - lat, radius)
        return square(jnp.maximum(room - lon_part[batch], 0.0))

    def spread_unit(batch, index, covariance):
        covariance = covariance[:, :nobs] + covariance[:, nobs:]
        taper = jnp.concatenate([taper_of(batch, index * count + r) for r in range(count)], axis=0)
        upper, lower = halves_of(taper * covariance)
        spread[batch, cells_of(index)] = jnp.concatenate([upper, lower, upper], axis=1)

    def cells_of(index):
        return pl.ds(index * count * cols, count * cols)

    right = [twice(jnp.transpose(anomaly[0] / (members - 1)))]

    def first_unit(index):
        spread_unit(0, index, product(split[cells_of(index)], right[0]))

    weights.append(weights_of(0, priors[0], anomaly[0], first_unit))

    where = jnp.concatenate(obs[1] + [jnp.zeros((8 - 3, nobs), jnp.int32)], axis=0)
    where = jnp.transpose(where.astype(jnp.float32)).astype(jnp.int32)
    lat_gap = where[:, 0:1] - obs[0][0]
    lon_gap = lon_distance(where[:, 1:2], obs[0][1])
    distance = (square(lat_gap) + square(lon_gap)).astype(jnp.float32)
    taper = square(jnp.maximum(1.0 - distance / square(obs[0][2]).astype(jnp.float32), 0.0))
    before = arrival(1)
    covariance = matmul_exact(centred(before), anomaly[0], (1, 1)) / (members - 1)
    priors.append(before + matmul_stacked(taper * covariance, weights[0]))
    anomaly.append(centred(priors[1]))
    carried = twice(matmul_exact(centred(weights[0]), anomaly[1], (1, 1)) / (members - 1))
    right.append(twice(jnp.transpose(anomaly[1] / (members - 1))))
    change = [thrice(weights[0])]

    def second_unit(index):
        at, at_rows = cells_of(index), pl.ds(index * count, count)
        covariance = product(split[at], right[1]) + product(spread[0, at, : 2 * nobs], carried)
        spread_unit(1, index, covariance)
        field[at_rows] += product(spread[0, at], change[0]).reshape(count, cols, members)
        for copy in copies_of(index):
            copy.start()

    def copies_of(index):
        at, at_rows = cells_of(index), pl.ds(index * count, count)
        return (
            pltpu.make_async_copy(field.at[at_rows], field_out.at[at_rows], out_sem.at[index, 0]),
            pltpu.make_async_copy(spread.at[1, at], spread_out.at[at], out_sem.at[index, 1]),
        )

    weights.append(weights_of(1, priors[1], anomaly[1], second_unit))
    change.append(thrice(weights[1]))

    change_ref[...] = change[1]
    for index in range(UNITS):
        for copy in copies_of(index):
            copy.wait()


def update_kernel(
    field_hbm, spread_hbm, change_hbm, out_ref, field, spread, change, analysis, change_sem, in_sem, out_sem
):
    rows, cols, members = field.shape
    chunks = out_sem.shape[0]
    count = rows // chunks
    whole = pltpu.make_async_copy(change_hbm, change, change_sem)
    whole.start()
    loads, stores = [], []
    for index in range(chunks):
        at, at_cells = pl.ds(index * count, count), pl.ds(index * count * cols, count * cols)
        loads.append(
            (
                pltpu.make_async_copy(spread_hbm.at[at_cells], spread.at[at_cells], in_sem.at[index, 0]),
                pltpu.make_async_copy(field_hbm.at[at], field.at[at], in_sem.at[index, 1]),
            )
        )
        for load in loads[-1]:
            load.start()
    whole.wait()
    for index in range(chunks):
        at, at_cells = pl.ds(index * count, count), pl.ds(index * count * cols, count * cols)
        for load in loads[index]:
            load.wait()
        step = product(spread[at_cells], change[...])
        analysis[at] = (field[at] + step.reshape(count, cols, members)).astype(jnp.bfloat16)
        stores.append(pltpu.make_async_copy(analysis.at[at], out_ref.at[at], out_sem.at[index]))
        stores[-1].start()
    for store in stores:
        store.wait()


def update(field, spread, change):
    chunks = 2
    anywhere = pl.BlockSpec(memory_space=pl.ANY)
    dma = pltpu.SemaphoreType.DMA
    return pl.pallas_call(
        update_kernel,
        out_shape=jax.ShapeDtypeStruct(field.shape, jnp.bfloat16),
        in_specs=[anywhere] * 3,
        out_specs=anywhere,
        scratch_shapes=[pltpu.VMEM(array.shape, array.dtype) for array in (field, spread, change)]
        + [pltpu.VMEM(field.shape, jnp.bfloat16), dma, dma((chunks, 2)), dma((chunks,))],
        compiler_params=pltpu.CompilerParams(vmem_limit_bytes=VMEM_BYTES),
        name="update",
    )(field, spread, change)


def window(state, courant, where, value, variance, noise, lon_count, lat_count):
    rows, cols, members = state.shape
    nobs = where.shape[2]
    plane_lon, line_lon, line_lat, plane_lat = split_mesh(lon_count, lat_count)
    plane, lines = plane_lon * plane_lat, line_lat * line_lon
    band = nobs * (members // LANES) // plane
    f32, bf16 = jnp.float32, jnp.bfloat16
    anywhere = pl.BlockSpec(memory_space=pl.ANY)
    dma = pltpu.SemaphoreType.DMA
    arguments = (state, courant, where, value, variance, noise)
    return pl.pallas_call(
        functools.partial(window_kernel, (lon_count, lat_count)),
        out_shape=(
            jax.ShapeDtypeStruct((rows, cols, members), f32),
            jax.ShapeDtypeStruct((rows * cols, 3 * nobs), bf16),
            jax.ShapeDtypeStruct((3 * nobs, members), bf16),
        ),
        in_specs=[anywhere] * len(arguments),
        out_specs=(anywhere, anywhere, pl.BlockSpec(memory_space=pltpu.VMEM)),
        scratch_shapes=[pltpu.VMEM(argument.shape, argument.dtype) for argument in arguments]
        + [
            pltpu.VMEM((2, 2, 8, cols), f32),
            pltpu.VMEM((2, 2, rows, cols), f32),
            pltpu.VMEM((4, 2, 8, cols), f32),
            pltpu.VMEM((BATCHES, nobs, LANES), jnp.int32),
            pltpu.VMEM((2, rows + 16, LANES), f32),
            pltpu.VMEM((len(TWO_STEPS), rows + 16, LANES), f32),
            pltpu.VMEM((len(TWO_STEPS), rows // 2, LANES), f32),
            pltpu.VMEM((2 * nobs, rows * cols), bf16),
            pltpu.VMEM((BATCHES, nobs, members), f32),
            pltpu.VMEM((BATCHES, plane - 1, band, LANES), f32),
            pltpu.VMEM((BATCHES, band, LANES), f32),
            pltpu.VMEM((BATCHES, lines - 1, band, LANES), f32),
            pltpu.VMEM((BATCHES, nobs, members), f32),
            pltpu.VMEM((rows + 4, LANES, members), bf16),
            pltpu.VMEM((4 * cols, 6 * LANES), bf16),
            pltpu.VMEM((4, 2, cols, members), f32),
            pltpu.VMEM((4, rows, 2, members), f32),
            pltpu.VMEM((8, 8, members), f32),
            pltpu.VMEM((rows, cols, members), f32),
            pltpu.VMEM((rows * cols, 2 * members), bf16),
            pltpu.VMEM((BATCHES, rows * cols, 3 * nobs), bf16),
            dma((len(arguments),)),
            dma((8, 2)),
            dma((8, 2)),
            dma((BATCHES,)),
            dma((BATCHES,)),
            dma((BATCHES,)),
            dma((BATCHES, 3)),
            dma((UNITS, 2)),
        ],
        compiler_params=pltpu.CompilerParams(
            collective_id=0, has_side_effects=True, vmem_limit_bytes=VMEM_BYTES
        ),
        name="window",
    )(*arguments)


def body(ensemble_state, courant, obs_where, obs_value, obs_variance, obs_noise):
    counts = lax.axis_size("lon"), lax.axis_size("lat")
    where = jnp.transpose(obs_where, (1, 0, 2))
    return update(*window(ensemble_state, courant, where, obs_value, obs_variance, obs_noise, *counts))


def solution(mesh):
    placed = (P("lat", "lon", None), P(None, "lat", "lon"), P(), P(), P(), P())
    return jax.shard_map(
        body, mesh=mesh, in_specs=placed, out_specs=P("lat", "lon", None), check_vma=False
    )
```

```python
import functools
import jax
import jax.numpy as jnp
from jax import lax
from jax.experimental import pallas as pl
from jax.experimental.pallas import tpu as pltpu
from jax.sharding import PartitionSpec as P

BATCHES = 2
MESH = pl.DeviceIdType.MESH
UNITS = 16
KEY = 8192
BLOCK = 8
VMEM_BYTES = 63 * 1024 * 1024
LANES = 128
HIGHEST = lax.Precision.HIGHEST
ONE_STEP = ((0, 0), (-1, 0), (1, 0), (0, -1), (0, 1))
TWO_STEPS = tuple(sorted({(a + c, b + d) for a, b in ONE_STEP for c, d in ONE_STEP}))


def split_mesh(lon_count, lat_count):
    plane_lat = 8 if lat_count == 16 else lat_count // 2
    line_lon = 8 if lon_count == 32 else lon_count // 2
    return lon_count // line_lon, line_lon, lat_count // plane_lat, plane_lat


def shifted(field, rows, lanes):
    if rows:
        field = pltpu.roll(field, rows % field.shape[0], 0)
    if lanes:
        field = pltpu.roll(field, lanes % field.shape[1], 1)
    return field


def link_weights(speed_lat, speed_lon, row, total_rows):
    inside = (row >= 0) & (row < total_rows)
    lat_plus = jnp.maximum(speed_lat, 0.0)
    lat_minus = jnp.minimum(speed_lat, 0.0)
    lon_plus = jnp.maximum(speed_lon, 0.0)
    lon_minus = jnp.minimum(speed_lon, 0.0)
    zero = jnp.zeros_like(speed_lat)
    return {
        (0, 0): jnp.where(inside, 1.0 - lat_plus + lat_minus - lon_plus + lon_minus, zero),
        (-1, 0): jnp.where(inside & (row > 0), lat_plus, zero),
        (1, 0): jnp.where(inside & (row < total_rows - 1), -lat_minus, zero),
        (0, -1): jnp.where(inside, lon_plus, zero),
        (0, 1): jnp.where(inside, -lon_minus, zero),
    }


def ring_flips(count):
    flips = [lambda place: place]
    size = 1
    while size < count:
        flips += [lambda place, size=size, f=f: flip_bit(f(place), size) for f in flips]
        size *= 2
    return flips


def flip_bit(place, size):
    return place + size - 2 * size * (place // size % 2)


def window_kernel(
    sizes, state_hbm, courant_hbm, where_hbm, value_hbm, variance_hbm, noise_hbm,
    out_ref,
    state_ref, courant_ref, where_ref, value_ref, variance_ref, noise_ref,
    near_ns, near_ew, near_corner, keys, reach, wide, stencil, weights, part, pieces, piece, line, priors,
    cells, bands, far_ns, far_ew, far_corner, field, split, spread, analysis,
    in_sem, near_sem, far_sem, part_sem, line_sem, all_sem, send_sem, out_sem,
):
    lon_count, lat_count = sizes
    plane_lon, line_lon, line_lat, plane_lat = split_mesh(lon_count, lat_count)
    plane, lines = plane_lon * plane_lat, line_lat * line_lon
    rows, cols, members = state_ref.shape
    total_rows, total_cols = rows * lat_count, cols * lon_count
    nobs = where_ref.shape[2]
    halves = members // LANES
    band = nobs * halves // plane
    lon, lat = lax.axis_index("lon"), lax.axis_index("lat")
    line_me = (lat // plane_lat) * line_lon + lon % line_lon
    arguments = (
        (courant_hbm, courant_ref), (state_hbm, state_ref), (where_hbm, where_ref),
        (value_hbm, value_ref), (variance_hbm, variance_ref), (noise_hbm, noise_ref),
    )
    loads = [pltpu.make_async_copy(*pair, in_sem.at[index]) for index, pair in enumerate(arguments)]
    for load in loads:
        load.start()

    lon_flips, lat_flips = ring_flips(plane_lon), ring_flips(plane_lat)
    plane_x = [flip(lon // line_lon) for flip in lon_flips]
    plane_y = [flip(lat % plane_lat) for flip in lat_flips]
    partners = [(i, j) for i in range(plane_lon) for j in range(plane_lat)][1:]
    hops = {0: 0, 1: 1, 2: 2, 3: 1}
    partners.sort(key=lambda p: -hops[p[0] % 4] - hops[p[1] // 2 % 4])
    distances = sorted(range(1, lines), key=lambda d: -min(d, lines - d))

    def plane_device(partner):
        return {
            "lon": plane_x[partner[0]] * line_lon + lon % line_lon,
            "lat": lat // plane_lat * plane_lat + plane_y[partner[1]],
        }

    def tile_of(partner):
        index = plane_x[partner[0]] * plane_lat + plane_y[partner[1]]
        return (
            pl.ds(pl.multiple_of(index // halves * band, band), band),
            pl.ds(pl.multiple_of(index % halves * LANES, LANES), LANES),
        )

    def line_device(distance):
        index = lax.rem(line_me + distance, lines)
        return {
            "lon": lon // line_lon * line_lon + index % line_lon,
            "lat": index // line_lon * plane_lat + lat % plane_lat,
        }

    def neighbour(lat_step, lon_step):
        return {
            "lon": lax.rem(lon + lon_step + lon_count, lon_count),
            "lat": lax.rem(lat + lat_step + lat_count, lat_count),
        }

    around = [(a, b) for a in (-1, 1) for b in (0, -1, 1)] + [(0, -1), (0, 1)]

    barrier = pltpu.get_barrier_semaphore()
    greeted = [neighbour(*step) for step in around]
    greeted += [line_device(distance) for distance in distances]
    greeted += [plane_device(partner) for partner in partners]
    for target in greeted:
        pl.semaphore_signal(barrier, inc=1, device_id=target, device_id_type=MESH)

    for load in loads:
        load.wait()
    edges, ends = ((0, 2), (rows - 2, rows)), ((0, 2), (cols - 2, cols))
    for side in range(2):
        low, high = edges[side]
        far_ns[side] = state_ref[low:high].astype(jnp.float32)
        low, high = ends[side]
        far_ew[side] = state_ref[:, low:high].astype(jnp.float32)
        for other in range(2):
            row, first = (0, rows - 1)[side], (0, cols - 8)[other]
            far_corner[2 * side + other] = state_ref[row, first : first + 8].astype(jnp.float32)
    cells[...] = jnp.zeros(cells.shape, jnp.bfloat16)
    cells[2 : 2 + rows, :cols] = state_ref[...]
    flat_lane = lax.broadcasted_iota(jnp.int32, (nobs, LANES), 1)
    second_row = jnp.where(flat_lane >= cols, 1, 0)
    column = flat_lane - second_row * cols
    for batch in range(BATCHES):
        where = jnp.concatenate([where_ref[i, batch : batch + 1] for i in range(3)], axis=0)
        where = jnp.concatenate([where, jnp.zeros((8 - 3, nobs), jnp.int32)], axis=0)
        where = jnp.transpose(where.astype(jnp.float32)).astype(jnp.int32)
        obs_row = where[:, 0:1] - lat * rows
        obs_col = where[:, 1:2] - lon * cols + 2
        obs_col = jnp.where(obs_col < 0, obs_col + total_cols, obs_col) - 2
        obs_col = jnp.where(obs_col >= total_cols - 2, obs_col - total_cols, obs_col)
        keys[batch] = (second_row - obs_row) * KEY + column - obs_col
    pl.semaphore_wait(barrier, len(greeted))

    def has(lat_step):
        return (lat + lat_step >= 0) & (lat + lat_step < lat_count)

    def send(src, dst, sem, step):
        copy = pltpu.make_async_remote_copy(
            src_ref=src, dst_ref=dst, send_sem=sem.at[0], recv_sem=sem.at[1],
            device_id=neighbour(*step), device_id_type=MESH,
        )
        copy.start()
        return copy

    low, high = pl.ds(0, 8), pl.ds(rows - 8, 8)
    near = []
    for index, (a, b) in enumerate(around):
        source = courant_ref.at[:, {-1: low, 1: high}[a], :] if a else courant_ref
        if a and b:
            target = near_corner.at[(0 if a > 0 else 2) + (0 if b > 0 else 1)]
        elif a:
            target = near_ns.at[0 if a > 0 else 1]
        else:
            target = near_ew.at[0 if b > 0 else 1]
        near.append(send(source, target, near_sem.at[index], (a, b)))

    far = []
    for index, (a, b) in enumerate(around):
        up, right = int(a > 0), int(b > 0)
        if a and b:
            source, target = far_corner.at[2 * up + right], far_corner.at[4 + 2 * (1 - up) + (1 - right)]
        elif a:
            source, target = far_ns.at[up], far_ns.at[2 + 1 - up]
        else:
            source, target = far_ew.at[right], far_ew.at[2 + 1 - right]
        far.append(
            (
                pltpu.make_async_remote_copy(
                    src_ref=source, dst_ref=target, send_sem=far_sem.at[index, 0], recv_sem=far_sem.at[index, 1],
                    device_id=neighbour(a, b), device_id_type=MESH,
                ),
                (a, b),
            )
        )
    for copy, (a, _) in far:
        pl.when(has(a))(copy.start)
    for copy in near:
        copy.wait_recv()

    lane = lax.broadcasted_iota(jnp.int32, (8, LANES), 1)

    def assemble(own, west, east):
        blank = jnp.zeros((8, LANES - cols), jnp.float32)
        own = jnp.concatenate([own, blank], axis=1)
        west = jnp.concatenate([blank, west], axis=1)
        east = jnp.concatenate([blank, east], axis=1)
        return jnp.where(lane < cols, own, jnp.where(lane < cols + 2, east, west))

    for c in range(2):
        reach[c, 0:8] = assemble(near_ns[0, c], near_corner[0, c], near_corner[1, c])
        for r in range(0, rows, 8):
            band_rows = pl.ds(r, 8)
            reach[c, r + 8 : r + 16] = assemble(
                courant_ref[c, band_rows], near_ew[0, c, band_rows], near_ew[1, c, band_rows]
            )
        reach[c, rows + 8 : rows + 16] = assemble(near_ns[1, c], near_corner[2, c], near_corner[3, c])

    row = lax.broadcasted_iota(jnp.int32, (rows + 16, LANES), 0) - 8 + lat * rows
    weight = link_weights(reach[0], reach[1], row, total_rows)

    arrived = {step: shifted(weight[step], *step) for step in ONE_STEP}
    sums = {}
    for first in ONE_STEP:
        for second in ONE_STEP:
            total = (first[0] + second[0], first[1] + second[1])
            term = shifted(arrived[first] * weight[second], *second)
            sums[total] = sums[total] + term if total in sums else term
    half = lax.broadcasted_iota(jnp.int32, (rows // 2, LANES), 1) < cols
    for index, total in enumerate(TWO_STEPS):
        wide[index] = sums[total]
        even = wide[index, pl.ds(8, rows // 2, 2), :]
        odd = wide[index, pl.ds(9, rows // 2, 2), :]
        stencil[index] = jnp.where(half, even, pltpu.roll(odd, cols, 1))

    def halves_into(ref, at, columns, value):
        upper = value.astype(jnp.bfloat16)
        count = value.shape[0]
        ref[at : at + count, columns] = upper
        ref[at + count : at + 2 * count, columns] = (value - upper.astype(jnp.float32)).astype(jnp.bfloat16)

    flat_state = state_ref[...].reshape(rows * cols, members)

    def make_share(batch):
        def one_pair(pair, carry):
            total = jnp.zeros((nobs, LANES), jnp.float32)
            for index, (a, b) in enumerate(TWO_STEPS):
                met = keys[batch] == a * KEY + b - 2 * KEY * pair
                total = jnp.where(met, stencil[index, pl.ds(pair, 1), :], total)
            halves_into(weights, 0, pl.ds(pl.multiple_of(pair * LANES, LANES), LANES), total)
            return carry

        lax.fori_loop(0, rows // 2, one_pair, 0)
        share = jnp.dot(weights[...], flat_state, preferred_element_type=jnp.float32)
        part[batch] = share[:nobs] + share[nobs:]

    def send_share(batch):
        for index, partner in enumerate(partners):
            pltpu.make_async_remote_copy(
                src_ref=part.at[batch, *tile_of(partner)], dst_ref=pieces.at[batch, index],
                send_sem=send_sem.at[batch, 0], recv_sem=part_sem.at[batch],
                device_id=plane_device(partner), device_id_type=MESH,
            ).start()

    mine = tile_of((0, 0))

    def send_piece(batch):
        pltpu.make_async_copy(pieces.at[batch], pieces.at[batch], part_sem.at[batch]).wait()
        piece[batch] = part[batch, *mine] + jnp.sum(pieces[batch], axis=0)
        for index, distance in enumerate(distances):
            pltpu.make_async_remote_copy(
                src_ref=piece.at[batch], dst_ref=line.at[batch, index],
                send_sem=send_sem.at[batch, 1], recv_sem=line_sem.at[batch],
                device_id=line_device(distance), device_id_type=MESH,
            ).start()

    def send_priors(batch):
        pltpu.make_async_copy(line.at[batch], line.at[batch], line_sem.at[batch]).wait()
        priors[batch, *mine] = piece[batch] + jnp.sum(line[batch], axis=0)
        for partner in partners:
            pltpu.make_async_remote_copy(
                src_ref=priors.at[batch, *mine], dst_ref=priors.at[batch, *mine],
                send_sem=send_sem.at[batch, 2], recv_sem=all_sem.at[batch],
                device_id=plane_device(partner), device_id_type=MESH,
            ).start()

    make_share(0)
    send_share(0)
    make_share(1)
    send_piece(0)
    send_share(1)

    gap = jnp.zeros((14, members), jnp.float32)

    def beside(at, west, east):
        cells[at, cols : cols + 16] = jnp.concatenate([east, gap], axis=0).astype(jnp.bfloat16)
        cells[at, LANES - 16 :] = jnp.concatenate([gap, west], axis=0).astype(jnp.bfloat16)

    def beside_row(r, carry):
        beside(r + 2, far_ew[2, r], far_ew[3, r])
        return carry

    for copy, (a, _) in far:
        if a == 0:
            copy.wait_recv()
    lax.fori_loop(0, rows, beside_row, 0)
    step_lane = lax.broadcasted_iota(jnp.int32, (cols, LANES), 1) - lax.broadcasted_iota(jnp.int32, (cols, LANES), 0)
    step_lane = jnp.where(step_lane > LANES // 2 + 2, step_lane - LANES, step_lane)

    def one_pair_of_rows(pair, carry):
        first = 2 * pair
        for around_row in range(6):
            for r in range(2):
                a = around_row - 2 - r
                total = jnp.zeros((cols, LANES), jnp.float32)
                if -2 <= a <= 2:
                    for index, (lat_step, b) in enumerate(TWO_STEPS):
                        if lat_step == a:
                            total = jnp.where(step_lane == b, wide[index, pl.ds(first + around_row + 6, 1), :], total)
                halves_into(bands, 2 * r * cols, pl.ds(around_row * LANES, LANES), total)
        near_cells = cells[pl.ds(first, 6)].reshape(6 * LANES, members)
        result = jnp.dot(bands[...], near_cells, preferred_element_type=jnp.float32)
        for r in range(2):
            value = result[2 * r * cols : (2 * r + 1) * cols] + result[(2 * r + 1) * cols : (2 * r + 2) * cols]
            field[first + r] = value
            at = pl.ds(pl.multiple_of((first + r) * cols, cols), cols)
            split[at] = jnp.concatenate(halves_of(value), axis=1)
        return carry

    lax.fori_loop(1, rows // 4, one_pair_of_rows, 0)
    send_piece(1)
    send_priors(0)
    lax.fori_loop(rows // 4, rows // 2 - 1, one_pair_of_rows, 0)
    for copy, (a, _) in far:
        if a:
            pl.when(has(-a))(copy.wait_recv)
    for side, at in ((0, 1), (1, rows + 2)):

        @pl.when(has((-1, 1)[side]))
        def _(side=side, at=at):
            cells[(0, rows + 2)[side] : (2, rows + 4)[side], :cols] = far_ns[2 + side].astype(jnp.bfloat16)
            beside(at, far_corner[4 + 2 * side, 6:8], far_corner[4 + 2 * side + 1, 0:2])

    lax.fori_loop(0, 2, lambda end, carry: one_pair_of_rows(end * (rows // 2 - 1), carry), 0)
    send_priors(1)

    def arrival(batch):
        pltpu.make_async_copy(pieces.at[batch], pieces.at[batch], all_sem.at[batch]).wait()
        return priors[batch]

    analyse(
        sizes, arrival, where_ref, value_ref, variance_ref, noise_ref, out_ref, field, split, spread, analysis, out_sem
    )

    for copy in near:
        copy.wait_send()
    for copy, (a, _) in far:
        pl.when(has(a))(copy.wait_send)
    for batch in range(BATCHES):
        for sem, sent in enumerate((pieces, line, pieces)):
            pltpu.make_async_copy(sent.at[batch], sent.at[batch], send_sem.at[batch, sem]).wait()


def matmul_exact(left, right, contract=(1, 0)):
    return lax.dot_general(
        left, right, (((contract[0],), (contract[1],)), ((), ())),
        precision=HIGHEST, preferred_element_type=jnp.float32,
    )


def thirds_of(value):
    upper = value.astype(jnp.bfloat16)
    rest = value - upper.astype(jnp.float32)
    middle = rest.astype(jnp.bfloat16)
    return upper, middle, (rest - middle.astype(jnp.float32)).astype(jnp.bfloat16)


def matmul_stacked(left, right, contract=(1, 0)):
    a, b, c = thirds_of(left)
    x, y, z = thirds_of(right)
    return lax.dot_general(
        jnp.concatenate([a, b, c, a, b, a], axis=contract[0]),
        jnp.concatenate([z, y, x, y, x, x], axis=contract[1]),
        (((contract[0],), (contract[1],)), ((), ())),
        preferred_element_type=jnp.float32,
    )


def halves_of(value):
    upper = value.astype(jnp.bfloat16)
    return upper, (value - upper.astype(jnp.float32)).astype(jnp.bfloat16)


def product(left, right):
    return jnp.dot(left, right, preferred_element_type=jnp.float32)


def twice(right):
    upper, lower = halves_of(right)
    return jnp.concatenate(
        [jnp.concatenate([upper, lower], axis=1), jnp.concatenate([upper, jnp.zeros_like(lower)], axis=1)], axis=0
    )


def thrice(right):
    upper, lower = halves_of(right)
    return jnp.concatenate([upper, upper, lower], axis=0)


def solve_pivot(pivot, rows):
    count = len(rows)
    pivot, rows, factor, inverse = dict(pivot), list(rows), {}, {}
    for j in range(0, count, 2):
        a, b, c = pivot[j, j], pivot[j + 1, j], pivot[j + 1, j + 1]
        scale = 1.0 / (a * c - b * b)
        inverse[j] = first, cross, last = c * scale, -b * scale, a * scale
        for i in range(j + 2, count):
            factor[i, j] = pivot[i, j] * first + pivot[i, j + 1] * cross
            factor[i, j + 1] = pivot[i, j] * cross + pivot[i, j + 1] * last
        for i in range(j + 2, count):
            for k in range(j + 2, i + 1):
                pivot[i, k] -= factor[i, j] * pivot[k, j] + factor[i, j + 1] * pivot[k, j + 1]
    for j in range(0, count, 2):
        for i in range(j + 2, count):
            rows[i] -= factor[i, j] * rows[j] + factor[i, j + 1] * rows[j + 1]
    for j in range(0, count, 2):
        first, cross, last = inverse[j]
        rows[j], rows[j + 1] = first * rows[j] + cross * rows[j + 1], cross * rows[j] + last * rows[j + 1]
    for i in reversed(range(0, count, 2)):
        for j in range(i):
            rows[j] -= factor[i, j] * rows[i] + factor[i + 1, j] * rows[i + 1]
    return rows


def tree_sum(terms):
    while len(terms) > 1:
        terms = [a + b for a, b in zip(terms[::2], terms[1::2])] + terms[len(terms) // 2 * 2 :]
    return terms[0]


def inverse_of(system, beside, panel=32, block=8):
    size = system.shape[0]
    spread = (8, size)
    lane = lax.broadcasted_iota(jnp.int32, spread, 1)
    sub = lax.broadcasted_iota(jnp.int32, spread, 0)
    panel_lane = lax.broadcasted_iota(jnp.int32, (panel, size), 1)
    panel_sub = lax.broadcasted_iota(jnp.int32, (panel, size), 0)
    whole_lane = lax.broadcasted_iota(jnp.int32, (size, size), 1)
    for start in range(0, size, panel):
        old = system[start : start + panel]
        bands = [old[i : i + 8] for i in range(0, panel, 8)]
        for here in range(0, panel // 8, block // 8):
            first = start + 8 * here
            inside = (lane >= first) & (lane < first + block)
            columns = [
                [jnp.broadcast_to(band[:, first + j : first + j + 1], spread) for j in range(block)] for band in bands
            ]
            pivot = {
                (i, j): jnp.broadcast_to(columns[here + i // 8][j][i % 8 : i % 8 + 1], spread)
                for i in range(block)
                for j in range(i + 1)
            }
            rows = [
                jnp.where(
                    inside,
                    jnp.where(lane == first + j, -1.0, 0.0),
                    jnp.broadcast_to(bands[here + j // 8][j % 8 : j % 8 + 1], spread),
                )
                for j in range(block)
            ]
            rows = solve_pivot(pivot, rows)
            for i, band in enumerate(bands):
                if here <= i < here + block // 8:
                    bands[i] = rows[8 * (i - here) + 7]
                    for j in range(7):
                        bands[i] = jnp.where(sub == j, rows[8 * (i - here) + j], bands[i])
                else:
                    terms = [columns[i][j] * rows[j] for j in range(block)]
                    bands[i] = jnp.where(inside, 0.0, band) - tree_sum(terms)
            for _ in range(block // 8):
                beside()
        swept = jnp.concatenate(bands, axis=0)
        inside = (panel_lane >= start) & (panel_lane < start + panel)
        old = jnp.where(inside, jnp.where(panel_lane == panel_sub + start, -1.0, 0.0), old)
        inside = (whole_lane >= start) & (whole_lane < start + panel)
        system = jnp.where(inside, 0.0, system) - matmul_stacked(old, swept, (0, 0))
        parts = [system[:start], swept, system[start + panel :]]
        system = jnp.concatenate([part for part in parts if part.shape[0]], axis=0)
    return -system


def square(value):
    return value * value


def analyse(
    sizes, arrival, where_ref, value_ref, variance_ref, noise_ref, out_ref, field, split, spread, analysis, out_sem
):
    lon_count, lat_count = sizes
    rows, cols, members = field.shape
    nobs = where_ref.shape[2]
    total_cols = cols * lon_count
    first_row, first_col = lax.axis_index("lat") * rows, lax.axis_index("lon") * cols

    blank = jnp.zeros((8 - 2 * BATCHES, nobs), jnp.float32)
    upright = jnp.transpose(jnp.concatenate([value_ref[...], variance_ref[...], blank], axis=0))
    eye = lax.broadcasted_iota(jnp.int32, (nobs, nobs), 0) == lax.broadcasted_iota(jnp.int32, (nobs, nobs), 1)

    def lon_distance(cell, obs):
        gap = jnp.abs(cell - obs)
        return jnp.minimum(gap, total_cols - gap)

    def scaled_square(gap, radius):
        return square(gap).astype(jnp.float32) / square(radius).astype(jnp.float32)

    def weights_of(batch, priors, anomaly, unit):
        variance = upright[:, BATCHES + batch : BATCHES + batch + 1]
        system = matmul_exact(anomaly, anomaly, (1, 1)) / (members - 1)
        system += jnp.where(eye, variance, 0.0)
        misfit = upright[:, batch : batch + 1] + jnp.sqrt(variance) * noise_ref[batch] - priors
        units = iter(range(UNITS))
        inverse = inverse_of(system, lambda: unit(next(units)), 32, BLOCK)
        return matmul_stacked(inverse, misfit)

    def centred(priors):
        return priors - jnp.mean(priors, axis=1, keepdims=True)

    obs = [[where_ref[i, batch : batch + 1, :] for i in range(3)] for batch in range(BATCHES)]
    priors = [arrival(0)]
    anomaly, weights = [centred(priors[0])], []
    cell_lon = first_col + lax.broadcasted_iota(jnp.int32, (cols, 1), 0)
    lon_part = [scaled_square(lon_distance(cell_lon, lon), radius) for _, lon, radius in obs]
    count = rows // UNITS

    def taper_of(batch, row):
        lat, _, radius = obs[batch]
        room = 1.0 - scaled_square(first_row + row - lat, radius)
        return square(jnp.maximum(room - lon_part[batch], 0.0))

    def spread_unit(batch, index, covariance):
        covariance = covariance[:, :nobs] + covariance[:, nobs:]
        taper = jnp.concatenate([taper_of(batch, index * count + r) for r in range(count)], axis=0)
        upper, lower = halves_of(taper * covariance)
        spread[batch, cells_of(index)] = jnp.concatenate([upper, lower, upper], axis=1)

    def cells_of(index):
        return pl.ds(index * count * cols, count * cols)

    right = [twice(jnp.transpose(anomaly[0] / (members - 1)))]

    def first_unit(index):
        spread_unit(0, index, product(split[cells_of(index)], right[0]))

    weights.append(weights_of(0, priors[0], anomaly[0], first_unit))

    where = jnp.concatenate(obs[1] + [jnp.zeros((8 - 3, nobs), jnp.int32)], axis=0)
    where = jnp.transpose(where.astype(jnp.float32)).astype(jnp.int32)
    lat_gap = where[:, 0:1] - obs[0][0]
    lon_gap = lon_distance(where[:, 1:2], obs[0][1])
    distance = (square(lat_gap) + square(lon_gap)).astype(jnp.float32)
    taper = square(jnp.maximum(1.0 - distance / square(obs[0][2]).astype(jnp.float32), 0.0))
    before = arrival(1)
    covariance = matmul_exact(centred(before), anomaly[0], (1, 1)) / (members - 1)
    priors.append(before + matmul_stacked(taper * covariance, weights[0]))
    anomaly.append(centred(priors[1]))
    carried = twice(matmul_exact(centred(weights[0]), anomaly[1], (1, 1)) / (members - 1))
    right.append(twice(jnp.transpose(anomaly[1] / (members - 1))))
    change = [thrice(weights[0])]

    def second_unit(index):
        at, at_rows = cells_of(index), pl.ds(index * count, count)
        covariance = product(split[at], right[1]) + product(spread[0, at, : 2 * nobs], carried)
        spread_unit(1, index, covariance)
        field[at_rows] += product(spread[0, at], change[0]).reshape(count, cols, members)

    weights.append(weights_of(1, priors[1], anomaly[1], second_unit))
    change.append(thrice(weights[1]))

    stores = []
    chunks = out_sem.shape[0]
    count_out = rows // chunks
    for index in range(chunks):
        at = pl.ds(index * count_out, count_out)
        step = product(spread[1, pl.ds(index * count_out * cols, count_out * cols)], change[1])
        analysis[at] = (field[at] + step.reshape(count_out, cols, members)).astype(jnp.bfloat16)
        stores.append(pltpu.make_async_copy(analysis.at[at], out_ref.at[at], out_sem.at[index]))
        stores[-1].start()
    for store in stores:
        store.wait()


def window(state, courant, where, value, variance, noise, lon_count, lat_count):
    rows, cols, members = state.shape
    nobs = where.shape[2]
    plane_lon, line_lon, line_lat, plane_lat = split_mesh(lon_count, lat_count)
    plane, lines = plane_lon * plane_lat, line_lat * line_lon
    band = nobs * (members // LANES) // plane
    f32, bf16 = jnp.float32, jnp.bfloat16
    anywhere = pl.BlockSpec(memory_space=pl.ANY)
    dma = pltpu.SemaphoreType.DMA
    arguments = (state, courant, where, value, variance, noise)
    return pl.pallas_call(
        functools.partial(window_kernel, (lon_count, lat_count)),
        out_shape=jax.ShapeDtypeStruct((rows, cols, members), bf16),
        in_specs=[anywhere] * len(arguments),
        out_specs=anywhere,
        scratch_shapes=[pltpu.VMEM(argument.shape, argument.dtype) for argument in arguments]
        + [
            pltpu.VMEM((2, 2, 8, cols), f32),
            pltpu.VMEM((2, 2, rows, cols), f32),
            pltpu.VMEM((4, 2, 8, cols), f32),
            pltpu.VMEM((BATCHES, nobs, LANES), jnp.int32),
            pltpu.VMEM((2, rows + 16, LANES), f32),
            pltpu.VMEM((len(TWO_STEPS), rows + 16, LANES), f32),
            pltpu.VMEM((len(TWO_STEPS), rows // 2, LANES), f32),
            pltpu.VMEM((2 * nobs, rows * cols), bf16),
            pltpu.VMEM((BATCHES, nobs, members), f32),
            pltpu.VMEM((BATCHES, plane - 1, band, LANES), f32),
            pltpu.VMEM((BATCHES, band, LANES), f32),
            pltpu.VMEM((BATCHES, lines - 1, band, LANES), f32),
            pltpu.VMEM((BATCHES, nobs, members), f32),
            pltpu.VMEM((rows + 4, LANES, members), bf16),
            pltpu.VMEM((4 * cols, 6 * LANES), bf16),
            pltpu.VMEM((4, 2, cols, members), f32),
            pltpu.VMEM((4, rows, 2, members), f32),
            pltpu.VMEM((8, 8, members), f32),
            pltpu.VMEM((rows, cols, members), f32),
            pltpu.VMEM((rows * cols, 2 * members), bf16),
            pltpu.VMEM((BATCHES, rows * cols, 3 * nobs), bf16),
            pltpu.VMEM((rows, cols, members), bf16),
            dma((len(arguments),)),
            dma((8, 2)),
            dma((8, 2)),
            dma((BATCHES,)),
            dma((BATCHES,)),
            dma((BATCHES,)),
            dma((BATCHES, 3)),
            dma((4,)),
        ],
        compiler_params=pltpu.CompilerParams(
            collective_id=0, has_side_effects=True, vmem_limit_bytes=VMEM_BYTES
        ),
        name="window",
    )(*arguments)


def body(ensemble_state, courant, obs_where, obs_value, obs_variance, obs_noise):
    counts = lax.axis_size("lon"), lax.axis_size("lat")
    where = jnp.transpose(obs_where, (1, 0, 2))
    return window(ensemble_state, courant, where, obs_value, obs_variance, obs_noise, *counts)


def solution(mesh):
    placed = (P("lat", "lon", None), P(None, "lat", "lon"), P(), P(), P(), P())
    return jax.shard_map(
        body, mesh=mesh, in_specs=placed, out_specs=P("lat", "lon", None), check_vma=False
    )
```

```python
import functools
import jax
import jax.numpy as jnp
from jax import lax
from jax.experimental import pallas as pl
from jax.experimental.pallas import tpu as pltpu
from jax.sharding import PartitionSpec as P

BATCHES = 2
MESH = pl.DeviceIdType.MESH
UNITS = 16
KEY = 8192
BLOCK = 8
VMEM_BYTES = 63 * 1024 * 1024
LANES = 128
HIGHEST = lax.Precision.HIGHEST
ONE_STEP = ((0, 0), (-1, 0), (1, 0), (0, -1), (0, 1))
TWO_STEPS = tuple(sorted({(a + c, b + d) for a, b in ONE_STEP for c, d in ONE_STEP}))


def split_mesh(lon_count, lat_count):
    plane_lat = 8 if lat_count == 16 else lat_count // 2
    line_lon = 8 if lon_count == 32 else lon_count // 2
    return lon_count // line_lon, line_lon, lat_count // plane_lat, plane_lat


def shifted(field, rows, lanes):
    if rows:
        field = pltpu.roll(field, rows % field.shape[0], 0)
    if lanes:
        field = pltpu.roll(field, lanes % field.shape[1], 1)
    return field


def link_weights(speed_lat, speed_lon, row, total_rows):
    inside = (row >= 0) & (row < total_rows)
    lat_plus = jnp.maximum(speed_lat, 0.0)
    lat_minus = jnp.minimum(speed_lat, 0.0)
    lon_plus = jnp.maximum(speed_lon, 0.0)
    lon_minus = jnp.minimum(speed_lon, 0.0)
    zero = jnp.zeros_like(speed_lat)
    return {
        (0, 0): jnp.where(inside, 1.0 - lat_plus + lat_minus - lon_plus + lon_minus, zero),
        (-1, 0): jnp.where(inside & (row > 0), lat_plus, zero),
        (1, 0): jnp.where(inside & (row < total_rows - 1), -lat_minus, zero),
        (0, -1): jnp.where(inside, lon_plus, zero),
        (0, 1): jnp.where(inside, -lon_minus, zero),
    }


def ring_flips(count):
    flips = [lambda place: place]
    size = 1
    while size < count:
        flips += [lambda place, size=size, f=f: flip_bit(f(place), size) for f in flips]
        size *= 2
    return flips


def flip_bit(place, size):
    return place + size - 2 * size * (place // size % 2)


def window_kernel(
    sizes, state_hbm, courant_hbm, where_hbm, value_hbm, variance_hbm, noise_hbm,
    out_ref,
    state_ref, courant_ref, where_ref, value_ref, variance_ref, noise_ref,
    near_ns, near_ew, near_corner, keys, reach, wide, stencil, weights, part, pieces, piece, line, priors,
    cells, bands, far_ns, far_ew, far_corner, field, split, spread, analysis,
    in_sem, near_sem, far_sem, part_sem, line_sem, all_sem, send_sem, out_sem,
):
    lon_count, lat_count = sizes
    plane_lon, line_lon, line_lat, plane_lat = split_mesh(lon_count, lat_count)
    plane, lines = plane_lon * plane_lat, line_lat * line_lon
    rows, cols, members = state_ref.shape
    total_rows, total_cols = rows * lat_count, cols * lon_count
    nobs = where_ref.shape[2]
    halves = members // LANES
    band = nobs * halves // plane
    lon, lat = lax.axis_index("lon"), lax.axis_index("lat")
    line_me = (lat // plane_lat) * line_lon + lon % line_lon
    arguments = (
        (courant_hbm, courant_ref), (state_hbm, state_ref), (where_hbm, where_ref),
        (value_hbm, value_ref), (variance_hbm, variance_ref), (noise_hbm, noise_ref),
    )
    loads = [pltpu.make_async_copy(*pair, in_sem.at[index]) for index, pair in enumerate(arguments)]
    for load in loads:
        load.start()

    lon_flips, lat_flips = ring_flips(plane_lon), ring_flips(plane_lat)
    plane_x = [flip(lon // line_lon) for flip in lon_flips]
    plane_y = [flip(lat % plane_lat) for flip in lat_flips]
    partners = [(i, j) for i in range(plane_lon) for j in range(plane_lat)][1:]
    hops = {0: 0, 1: 1, 2: 2, 3: 1}
    partners.sort(key=lambda p: -hops[p[0] % 4] - hops[p[1] // 2 % 4])
    distances = sorted(range(1, lines), key=lambda d: -min(d, lines - d))

    def plane_device(partner):
        return {
            "lon": plane_x[partner[0]] * line_lon + lon % line_lon,
            "lat": lat // plane_lat * plane_lat + plane_y[partner[1]],
        }

    def tile_of(partner):
        index = plane_x[partner[0]] * plane_lat + plane_y[partner[1]]
        return (
            pl.ds(pl.multiple_of(index // halves * band, band), band),
            pl.ds(pl.multiple_of(index % halves * LANES, LANES), LANES),
        )

    def line_device(distance):
        index = lax.rem(line_me + distance, lines)
        return {
            "lon": lon // line_lon * line_lon + index % line_lon,
            "lat": index // line_lon * plane_lat + lat % plane_lat,
        }

    def neighbour(lat_step, lon_step):
        return {
            "lon": lax.rem(lon + lon_step + lon_count, lon_count),
            "lat": lax.rem(lat + lat_step + lat_count, lat_count),
        }

    around = [(a, b) for a in (-1, 1) for b in (0, -1, 1)] + [(0, -1), (0, 1)]

    barrier = pltpu.get_barrier_semaphore()
    greeted = [neighbour(*step) for step in around]
    greeted += [line_device(distance) for distance in distances]
    greeted += [plane_device(partner) for partner in partners]
    for target in greeted:
        pl.semaphore_signal(barrier, inc=1, device_id=target, device_id_type=MESH)

    for load in loads:
        load.wait()
    edges, ends = ((0, 2), (rows - 2, rows)), ((0, 2), (cols - 2, cols))
    for side in range(2):
        low, high = edges[side]
        far_ns[side] = state_ref[low:high].astype(jnp.float32)
        low, high = ends[side]
        far_ew[side] = state_ref[:, low:high].astype(jnp.float32)
        for other in range(2):
            row, first = (0, rows - 1)[side], (0, cols - 8)[other]
            far_corner[2 * side + other] = state_ref[row, first : first + 8].astype(jnp.float32)
    cells[...] = jnp.zeros(cells.shape, jnp.bfloat16)
    cells[2 : 2 + rows, :cols] = state_ref[...]
    flat_lane = lax.broadcasted_iota(jnp.int32, (nobs, LANES), 1)
    second_row = jnp.where(flat_lane >= cols, 1, 0)
    column = flat_lane - second_row * cols
    for batch in range(BATCHES):
        where = jnp.concatenate([where_ref[i, batch : batch + 1] for i in range(3)], axis=0)
        where = jnp.concatenate([where, jnp.zeros((8 - 3, nobs), jnp.int32)], axis=0)
        where = jnp.transpose(where.astype(jnp.float32)).astype(jnp.int32)
        obs_row = where[:, 0:1] - lat * rows
        obs_col = where[:, 1:2] - lon * cols + 2
        obs_col = jnp.where(obs_col < 0, obs_col + total_cols, obs_col) - 2
        obs_col = jnp.where(obs_col >= total_cols - 2, obs_col - total_cols, obs_col)
        keys[batch] = (second_row - obs_row) * KEY + column - obs_col
    pl.semaphore_wait(barrier, len(greeted))

    def has(lat_step):
        return (lat + lat_step >= 0) & (lat + lat_step < lat_count)

    def send(src, dst, sem, step):
        copy = pltpu.make_async_remote_copy(
            src_ref=src, dst_ref=dst, send_sem=sem.at[0], recv_sem=sem.at[1],
            device_id=neighbour(*step), device_id_type=MESH,
        )
        copy.start()
        return copy

    low, high = pl.ds(0, 8), pl.ds(rows - 8, 8)
    near = []
    for index, (a, b) in enumerate(around):
        source = courant_ref.at[:, {-1: low, 1: high}[a], :] if a else courant_ref
        if a and b:
            target = near_corner.at[(0 if a > 0 else 2) + (0 if b > 0 else 1)]
        elif a:
            target = near_ns.at[0 if a > 0 else 1]
        else:
            target = near_ew.at[0 if b > 0 else 1]
        near.append(send(source, target, near_sem.at[index], (a, b)))

    far = []
    for index, (a, b) in enumerate(around):
        up, right = int(a > 0), int(b > 0)
        if a and b:
            source, target = far_corner.at[2 * up + right], far_corner.at[4 + 2 * (1 - up) + (1 - right)]
        elif a:
            source, target = far_ns.at[up], far_ns.at[2 + 1 - up]
        else:
            source, target = far_ew.at[right], far_ew.at[2 + 1 - right]
        far.append(
            (
                pltpu.make_async_remote_copy(
                    src_ref=source, dst_ref=target, send_sem=far_sem.at[index, 0], recv_sem=far_sem.at[index, 1],
                    device_id=neighbour(a, b), device_id_type=MESH,
                ),
                (a, b),
            )
        )
    for copy, (a, _) in far:
        pl.when(has(a))(copy.start)
    for copy in near:
        copy.wait_recv()

    lane = lax.broadcasted_iota(jnp.int32, (8, LANES), 1)

    def assemble(own, west, east):
        blank = jnp.zeros((8, LANES - cols), jnp.float32)
        own = jnp.concatenate([own, blank], axis=1)
        west = jnp.concatenate([blank, west], axis=1)
        east = jnp.concatenate([blank, east], axis=1)
        return jnp.where(lane < cols, own, jnp.where(lane < cols + 2, east, west))

    for c in range(2):
        reach[c, 0:8] = assemble(near_ns[0, c], near_corner[0, c], near_corner[1, c])
        for r in range(0, rows, 8):
            band_rows = pl.ds(r, 8)
            reach[c, r + 8 : r + 16] = assemble(
                courant_ref[c, band_rows], near_ew[0, c, band_rows], near_ew[1, c, band_rows]
            )
        reach[c, rows + 8 : rows + 16] = assemble(near_ns[1, c], near_corner[2, c], near_corner[3, c])

    row = lax.broadcasted_iota(jnp.int32, (rows + 16, LANES), 0) - 8 + lat * rows
    weight = link_weights(reach[0], reach[1], row, total_rows)

    arrived = {step: shifted(weight[step], *step) for step in ONE_STEP}
    sums = {}
    for first in ONE_STEP:
        for second in ONE_STEP:
            total = (first[0] + second[0], first[1] + second[1])
            term = shifted(arrived[first] * weight[second], *second)
            sums[total] = sums[total] + term if total in sums else term
    half = lax.broadcasted_iota(jnp.int32, (rows // 2, LANES), 1) < cols
    for index, total in enumerate(TWO_STEPS):
        wide[index] = sums[total]
        even = wide[index, pl.ds(8, rows // 2, 2), :]
        odd = wide[index, pl.ds(9, rows // 2, 2), :]
        stencil[index] = jnp.where(half, even, pltpu.roll(odd, cols, 1))

    def halves_into(ref, at, columns, value):
        upper = value.astype(jnp.bfloat16)
        count = value.shape[0]
        ref[at : at + count, columns] = upper
        ref[at + count : at + 2 * count, columns] = (value - upper.astype(jnp.float32)).astype(jnp.bfloat16)

    flat_state = state_ref[...].reshape(rows * cols, members)

    def make_share(batch):
        def one_pair(pair, carry):
            total = jnp.zeros((nobs, LANES), jnp.float32)
            for index, (a, b) in enumerate(TWO_STEPS):
                met = keys[batch] == a * KEY + b - 2 * KEY * pair
                total = jnp.where(met, stencil[index, pl.ds(pair, 1), :], total)
            halves_into(weights, 0, pl.ds(pl.multiple_of(pair * LANES, LANES), LANES), total)
            return carry

        lax.fori_loop(0, rows // 2, one_pair, 0)
        share = jnp.dot(weights[...], flat_state, preferred_element_type=jnp.float32)
        part[batch] = share[:nobs] + share[nobs:]

    def send_share(batch):
        for index, partner in enumerate(partners):
            pltpu.make_async_remote_copy(
                src_ref=part.at[batch, *tile_of(partner)], dst_ref=pieces.at[batch, index],
                send_sem=send_sem.at[batch, 0], recv_sem=part_sem.at[batch],
                device_id=plane_device(partner), device_id_type=MESH,
            ).start()

    mine = tile_of((0, 0))

    def send_piece(batch):
        pltpu.make_async_copy(pieces.at[batch], pieces.at[batch], part_sem.at[batch]).wait()
        piece[batch] = part[batch, *mine] + jnp.sum(pieces[batch], axis=0)
        for index, distance in enumerate(distances):
            pltpu.make_async_remote_copy(
                src_ref=piece.at[batch], dst_ref=line.at[batch, index],
                send_sem=send_sem.at[batch, 1], recv_sem=line_sem.at[batch],
                device_id=line_device(distance), device_id_type=MESH,
            ).start()

    def send_priors(batch):
        pltpu.make_async_copy(line.at[batch], line.at[batch], line_sem.at[batch]).wait()
        priors[batch, *mine] = piece[batch] + jnp.sum(line[batch], axis=0)
        for partner in partners:
            pltpu.make_async_remote_copy(
                src_ref=priors.at[batch, *mine], dst_ref=priors.at[batch, *mine],
                send_sem=send_sem.at[batch, 2], recv_sem=all_sem.at[batch],
                device_id=plane_device(partner), device_id_type=MESH,
            ).start()

    make_share(0)
    send_share(0)
    make_share(1)
    send_piece(0)
    send_share(1)

    gap = jnp.zeros((14, members), jnp.float32)

    def beside(at, west, east):
        cells[at, cols : cols + 16] = jnp.concatenate([east, gap], axis=0).astype(jnp.bfloat16)
        cells[at, LANES - 16 :] = jnp.concatenate([gap, west], axis=0).astype(jnp.bfloat16)

    def beside_row(r, carry):
        beside(r + 2, far_ew[2, r], far_ew[3, r])
        return carry

    for copy, (a, _) in far:
        if a == 0:
            copy.wait_recv()
    lax.fori_loop(0, rows, beside_row, 0)
    step_lane = lax.broadcasted_iota(jnp.int32, (cols, LANES), 1) - lax.broadcasted_iota(jnp.int32, (cols, LANES), 0)
    step_lane = jnp.where(step_lane > LANES // 2 + 2, step_lane - LANES, step_lane)

    def one_pair_of_rows(pair, carry):
        first = 2 * pair
        for around_row in range(6):
            for r in range(2):
                a = around_row - 2 - r
                total = jnp.zeros((cols, LANES), jnp.float32)
                if -2 <= a <= 2:
                    for index, (lat_step, b) in enumerate(TWO_STEPS):
                        if lat_step == a:
                            total = jnp.where(step_lane == b, wide[index, pl.ds(first + around_row + 6, 1), :], total)
                halves_into(bands, 2 * r * cols, pl.ds(around_row * LANES, LANES), total)
        near_cells = cells[pl.ds(first, 6)].reshape(6 * LANES, members)
        result = jnp.dot(bands[...], near_cells, preferred_element_type=jnp.float32)
        for r in range(2):
            value = result[2 * r * cols : (2 * r + 1) * cols] + result[(2 * r + 1) * cols : (2 * r + 2) * cols]
            field[first + r] = value
            at = pl.ds(pl.multiple_of((first + r) * cols, cols), cols)
            split[at] = jnp.concatenate(halves_of(value), axis=1)
        return carry

    lax.fori_loop(1, rows // 4, one_pair_of_rows, 0)
    send_piece(1)
    send_priors(0)
    lax.fori_loop(rows // 4, rows // 2 - 1, one_pair_of_rows, 0)
    for copy, (a, _) in far:
        if a:
            pl.when(has(-a))(copy.wait_recv)
    for side, at in ((0, 1), (1, rows + 2)):

        @pl.when(has((-1, 1)[side]))
        def _(side=side, at=at):
            cells[(0, rows + 2)[side] : (2, rows + 4)[side], :cols] = far_ns[2 + side].astype(jnp.bfloat16)
            beside(at, far_corner[4 + 2 * side, 6:8], far_corner[4 + 2 * side + 1, 0:2])

    lax.fori_loop(0, 2, lambda end, carry: one_pair_of_rows(end * (rows // 2 - 1), carry), 0)
    send_priors(1)

    def arrival(batch):
        pltpu.make_async_copy(pieces.at[batch], pieces.at[batch], all_sem.at[batch]).wait()
        return priors[batch]

    analyse(
        sizes, arrival, where_ref, value_ref, variance_ref, noise_ref, out_ref, field, split, spread, analysis, out_sem
    )

    for copy in near:
        copy.wait_send()
    for copy, (a, _) in far:
        pl.when(has(a))(copy.wait_send)
    for batch in range(BATCHES):
        for sem, sent in enumerate((pieces, line, pieces)):
            pltpu.make_async_copy(sent.at[batch], sent.at[batch], send_sem.at[batch, sem]).wait()


def matmul_exact(left, right, contract=(1, 0)):
    return lax.dot_general(
        left, right, (((contract[0],), (contract[1],)), ((), ())),
        precision=HIGHEST, preferred_element_type=jnp.float32,
    )


def thirds_of(value):
    upper = value.astype(jnp.bfloat16)
    rest = value - upper.astype(jnp.float32)
    middle = rest.astype(jnp.bfloat16)
    return upper, middle, (rest - middle.astype(jnp.float32)).astype(jnp.bfloat16)


def matmul_stacked(left, right, contract=(1, 0)):
    a, b, c = thirds_of(left)
    x, y, z = thirds_of(right)
    return lax.dot_general(
        jnp.concatenate([a, b, c, a, b, a], axis=contract[0]),
        jnp.concatenate([z, y, x, y, x, x], axis=contract[1]),
        (((contract[0],), (contract[1],)), ((), ())),
        preferred_element_type=jnp.float32,
    )


def halves_of(value):
    upper = value.astype(jnp.bfloat16)
    return upper, (value - upper.astype(jnp.float32)).astype(jnp.bfloat16)


def product(left, right):
    return jnp.dot(left, right, preferred_element_type=jnp.float32)


def twice(right):
    upper, lower = halves_of(right)
    return jnp.concatenate(
        [jnp.concatenate([upper, lower], axis=1), jnp.concatenate([upper, jnp.zeros_like(lower)], axis=1)], axis=0
    )


def thrice(right):
    upper, lower = halves_of(right)
    return jnp.concatenate([upper, upper, lower], axis=0)


def solve_pivot(pivot, rows):
    count = len(rows)
    pivot, rows, factor, inverse = dict(pivot), list(rows), {}, {}
    for j in range(0, count, 2):
        a, b, c = pivot[j, j], pivot[j + 1, j], pivot[j + 1, j + 1]
        scale = 1.0 / (a * c - b * b)
        inverse[j] = first, cross, last = c * scale, -b * scale, a * scale
        for i in range(j + 2, count):
            factor[i, j] = pivot[i, j] * first + pivot[i, j + 1] * cross
            factor[i, j + 1] = pivot[i, j] * cross + pivot[i, j + 1] * last
        for i in range(j + 2, count):
            for k in range(j + 2, i + 1):
                pivot[i, k] -= factor[i, j] * pivot[k, j] + factor[i, j + 1] * pivot[k, j + 1]
    for j in range(0, count, 2):
        for i in range(j + 2, count):
            rows[i] -= factor[i, j] * rows[j] + factor[i, j + 1] * rows[j + 1]
    for j in range(0, count, 2):
        first, cross, last = inverse[j]
        rows[j], rows[j + 1] = first * rows[j] + cross * rows[j + 1], cross * rows[j] + last * rows[j + 1]
    for i in reversed(range(0, count, 2)):
        for j in range(i):
            rows[j] -= factor[i, j] * rows[i] + factor[i + 1, j] * rows[i + 1]
    return rows


def tree_sum(terms):
    while len(terms) > 1:
        terms = [a + b for a, b in zip(terms[::2], terms[1::2])] + terms[len(terms) // 2 * 2 :]
    return terms[0]


def inverse_of(system, beside, panel=32, block=8):
    size = system.shape[0]
    spread = (8, size)
    lane = lax.broadcasted_iota(jnp.int32, spread, 1)
    sub = lax.broadcasted_iota(jnp.int32, spread, 0)
    panel_lane = lax.broadcasted_iota(jnp.int32, (panel, size), 1)
    panel_sub = lax.broadcasted_iota(jnp.int32, (panel, size), 0)
    whole_lane = lax.broadcasted_iota(jnp.int32, (size, size), 1)
    for start in range(0, size, panel):
        old = system[start : start + panel]
        bands = [old[i : i + 8] for i in range(0, panel, 8)]
        for here in range(0, panel // 8, block // 8):
            first = start + 8 * here
            inside = (lane >= first) & (lane < first + block)
            columns = [
                [jnp.broadcast_to(band[:, first + j : first + j + 1], spread) for j in range(block)] for band in bands
            ]
            pivot = {
                (i, j): jnp.broadcast_to(columns[here + i // 8][j][i % 8 : i % 8 + 1], spread)
                for i in range(block)
                for j in range(i + 1)
            }
            rows = [
                jnp.where(
                    inside,
                    jnp.where(lane == first + j, -1.0, 0.0),
                    jnp.broadcast_to(bands[here + j // 8][j % 8 : j % 8 + 1], spread),
                )
                for j in range(block)
            ]
            rows = solve_pivot(pivot, rows)
            for i, band in enumerate(bands):
                if here <= i < here + block // 8:
                    bands[i] = rows[8 * (i - here) + 7]
                    for j in range(7):
                        bands[i] = jnp.where(sub == j, rows[8 * (i - here) + j], bands[i])
                else:
                    terms = [columns[i][j] * rows[j] for j in range(block)]
                    bands[i] = jnp.where(inside, 0.0, band) - tree_sum(terms)
            for _ in range(block // 8):
                beside()
        swept = jnp.concatenate(bands, axis=0)
        inside = (panel_lane >= start) & (panel_lane < start + panel)
        old = jnp.where(inside, jnp.where(panel_lane == panel_sub + start, -1.0, 0.0), old)
        inside = (whole_lane >= start) & (whole_lane < start + panel)
        system = jnp.where(inside, 0.0, system) - matmul_stacked(old, swept, (0, 0))
        parts = [system[:start], swept, system[start + panel :]]
        system = jnp.concatenate([part for part in parts if part.shape[0]], axis=0)
    return -system


def square(value):
    return value * value


def analyse(
    sizes, arrival, where_ref, value_ref, variance_ref, noise_ref, out_ref, field, split, spread, analysis, out_sem
):
    lon_count, lat_count = sizes
    rows, cols, members = field.shape
    nobs = where_ref.shape[2]
    total_cols = cols * lon_count
    first_row, first_col = lax.axis_index("lat") * rows, lax.axis_index("lon") * cols

    blank = jnp.zeros((8 - 2 * BATCHES, nobs), jnp.float32)
    upright = jnp.transpose(jnp.concatenate([value_ref[...], variance_ref[...], blank], axis=0))
    eye = lax.broadcasted_iota(jnp.int32, (nobs, nobs), 0) == lax.broadcasted_iota(jnp.int32, (nobs, nobs), 1)

    def lon_distance(cell, obs):
        gap = jnp.abs(cell - obs)
        return jnp.minimum(gap, total_cols - gap)

    def scaled_square(gap, radius):
        return square(gap).astype(jnp.float32) / square(radius).astype(jnp.float32)

    def weights_of(batch, priors, anomaly, unit):
        variance = upright[:, BATCHES + batch : BATCHES + batch + 1]
        system = matmul_exact(anomaly, anomaly, (1, 1)) / (members - 1)
        system += jnp.where(eye, variance, 0.0)
        misfit = upright[:, batch : batch + 1] + jnp.sqrt(variance) * noise_ref[batch] - priors
        units = iter(range(UNITS))
        inverse = inverse_of(system, lambda: unit(next(units)), 32, BLOCK)
        both = matmul_stacked(inverse, jnp.concatenate([misfit, centred(misfit)], axis=1))
        return both[:, :members], both[:, members:]

    def centred(priors):
        return priors - jnp.mean(priors, axis=1, keepdims=True)

    obs = [[where_ref[i, batch : batch + 1, :] for i in range(3)] for batch in range(BATCHES)]
    priors = [arrival(0)]
    anomaly, weights = [centred(priors[0])], []
    cell_lon = first_col + lax.broadcasted_iota(jnp.int32, (cols, 1), 0)
    lon_part = [scaled_square(lon_distance(cell_lon, lon), radius) for _, lon, radius in obs]
    count = rows // UNITS

    def taper_of(batch, row):
        lat, _, radius = obs[batch]
        room = 1.0 - scaled_square(first_row + row - lat, radius)
        return square(jnp.maximum(room - lon_part[batch], 0.0))

    def spread_unit(batch, index, covariance):
        covariance = covariance[:, :nobs] + covariance[:, nobs:]
        taper = jnp.concatenate([taper_of(batch, index * count + r) for r in range(count)], axis=0)
        upper, lower = halves_of(taper * covariance)
        spread[batch, cells_of(index)] = jnp.concatenate([upper, lower, upper], axis=1)

    def cells_of(index):
        return pl.ds(index * count * cols, count * cols)

    right = [twice(jnp.transpose(anomaly[0] / (members - 1)))]

    where = jnp.concatenate(obs[1] + [jnp.zeros((8 - 3, nobs), jnp.int32)], axis=0)
    where = jnp.transpose(where.astype(jnp.float32)).astype(jnp.int32)
    lat_gap = where[:, 0:1] - obs[0][0]
    lon_gap = lon_distance(where[:, 1:2], obs[0][1])
    distance = (square(lat_gap) + square(lon_gap)).astype(jnp.float32)
    taper = square(jnp.maximum(1.0 - distance / square(obs[0][2]).astype(jnp.float32), 0.0))
    later = []

    def first_unit(index):
        if index == UNITS - 1:
            before = arrival(1)
            covariance = matmul_exact(centred(before), anomaly[0], (1, 1)) / (members - 1)
            later.extend((before, taper * covariance))
        spread_unit(0, index, product(split[cells_of(index)], right[0]))

    first_weights = weights_of(0, priors[0], anomaly[0], first_unit)
    weights.append(first_weights[0])

    before, tapered = later
    change = matmul_stacked(tapered, jnp.concatenate(first_weights, axis=1))
    priors.append(before + change[:, :members])
    anomaly.append(centred(before) + change[:, members:])
    carried = twice(matmul_exact(first_weights[1], anomaly[1], (1, 1)) / (members - 1))
    right.append(twice(jnp.transpose(anomaly[1] / (members - 1))))
    change = [thrice(weights[0])]

    def second_unit(index):
        at, at_rows = cells_of(index), pl.ds(index * count, count)
        covariance = product(split[at], right[1]) + product(spread[0, at, : 2 * nobs], carried)
        spread_unit(1, index, covariance)
        field[at_rows] += product(spread[0, at], change[0]).reshape(count, cols, members)

    weights.append(weights_of(1, priors[1], anomaly[1], second_unit)[0])
    change.append(thrice(weights[1]))

    stores = []
    chunks = out_sem.shape[0]
    count_out = rows // chunks
    for index in range(chunks):
        at = pl.ds(index * count_out, count_out)
        step = product(spread[1, pl.ds(index * count_out * cols, count_out * cols)], change[1])
        analysis[at] = (field[at] + step.reshape(count_out, cols, members)).astype(jnp.bfloat16)
        stores.append(pltpu.make_async_copy(analysis.at[at], out_ref.at[at], out_sem.at[index]))
        stores[-1].start()
    for store in stores:
        store.wait()


def window(state, courant, where, value, variance, noise, lon_count, lat_count):
    rows, cols, members = state.shape
    nobs = where.shape[2]
    plane_lon, line_lon, line_lat, plane_lat = split_mesh(lon_count, lat_count)
    plane, lines = plane_lon * plane_lat, line_lat * line_lon
    band = nobs * (members // LANES) // plane
    f32, bf16 = jnp.float32, jnp.bfloat16
    anywhere = pl.BlockSpec(memory_space=pl.ANY)
    dma = pltpu.SemaphoreType.DMA
    arguments = (state, courant, where, value, variance, noise)
    return pl.pallas_call(
        functools.partial(window_kernel, (lon_count, lat_count)),
        out_shape=jax.ShapeDtypeStruct((rows, cols, members), bf16),
        in_specs=[anywhere] * len(arguments),
        out_specs=anywhere,
        scratch_shapes=[pltpu.VMEM(argument.shape, argument.dtype) for argument in arguments]
        + [
            pltpu.VMEM((2, 2, 8, cols), f32),
            pltpu.VMEM((2, 2, rows, cols), f32),
            pltpu.VMEM((4, 2, 8, cols), f32),
            pltpu.VMEM((BATCHES, nobs, LANES), jnp.int32),
            pltpu.VMEM((2, rows + 16, LANES), f32),
            pltpu.VMEM((len(TWO_STEPS), rows + 16, LANES), f32),
            pltpu.VMEM((len(TWO_STEPS), rows // 2, LANES), f32),
            pltpu.VMEM((2 * nobs, rows * cols), bf16),
            pltpu.VMEM((BATCHES, nobs, members), f32),
            pltpu.VMEM((BATCHES, plane - 1, band, LANES), f32),
            pltpu.VMEM((BATCHES, band, LANES), f32),
            pltpu.VMEM((BATCHES, lines - 1, band, LANES), f32),
            pltpu.VMEM((BATCHES, nobs, members), f32),
            pltpu.VMEM((rows + 4, LANES, members), bf16),
            pltpu.VMEM((4 * cols, 6 * LANES), bf16),
            pltpu.VMEM((4, 2, cols, members), f32),
            pltpu.VMEM((4, rows, 2, members), f32),
            pltpu.VMEM((8, 8, members), f32),
            pltpu.VMEM((rows, cols, members), f32),
            pltpu.VMEM((rows * cols, 2 * members), bf16),
            pltpu.VMEM((BATCHES, rows * cols, 3 * nobs), bf16),
            pltpu.VMEM((rows, cols, members), bf16),
            dma((len(arguments),)),
            dma((8, 2)),
            dma((8, 2)),
            dma((BATCHES,)),
            dma((BATCHES,)),
            dma((BATCHES,)),
            dma((BATCHES, 3)),
            dma((4,)),
        ],
        compiler_params=pltpu.CompilerParams(
            collective_id=0, has_side_effects=True, vmem_limit_bytes=VMEM_BYTES
        ),
        name="window",
    )(*arguments)


def body(ensemble_state, courant, obs_where, obs_value, obs_variance, obs_noise):
    counts = lax.axis_size("lon"), lax.axis_size("lat")
    where = jnp.transpose(obs_where, (1, 0, 2))
    return window(ensemble_state, courant, where, obs_value, obs_variance, obs_noise, *counts)


def solution(mesh):
    placed = (P("lat", "lon", None), P(None, "lat", "lon"), P(), P(), P(), P())
    return jax.shard_map(
        body, mesh=mesh, in_specs=placed, out_specs=P("lat", "lon", None), check_vma=False
    )
```
